32 devices in a mesh: dp: 8 (over y, x, core), pipe: 4 (over z).
Axes of the slice: x: 2, y: 2, z: 4, core: 2. Of those that a mesh axis runs over, the one named last changes fastest.
Arguments:
- tokens: bfloat16 [16, 2048, 256], P('dp', 'pipe'), may hold values from -6 to 6
- segments: int32 [16, 2048], P('dp'), may hold values from 0 to 7, never falling along the last dimension, each value on 1 to 512 neighbouring positions
- cotangent: bfloat16 [16, 2048, 256], P('dp', 'pipe'), may hold values from -6 to 6
- attention_in: bfloat16 [2, 256, 768], replicated, may hold values from -0.5 to 0.5
- attention_in_bias: float32 [2, 512], replicated, may hold values from -3 to 3
- attention_out: bfloat16 [2, 256, 256], replicated, may hold values from -1.5 to 1.5
- attention_out_bias: float32 [2, 256], replicated, may hold values from -2 to 2
- attention_gain: float32 [2, 256], replicated, may hold values from 0.25 to 1.75
- attention_shift: float32 [2, 256], replicated, may hold values from -2 to 2
- expand_weight: bfloat16 [2, 256, 512], replicated, may hold values from -0.375 to 0.375
- expand_bias: float32 [2, 512], replicated, may hold values from -3 to 3
- contract_weight: bfloat16 [2, 512, 256], replicated, may hold values from -0.375 to 0.375
- contract_bias: float32 [2, 256], replicated, may hold values from -2 to 2
- feed_gain: float32 [2, 256], replicated, may hold values from 0.25 to 1.75
- feed_shift: float32 [2, 256], replicated, may hold values from -2 to 2
Outputs:
- layer_output: bfloat16 [16, 2048, 256], P('dp', 'pipe')
- input_grad: bfloat16 [16, 2048, 256], P('dp', 'pipe')
- gradient_attention_in: float32 [2, 256, 768], replicated
- gradient_attention_in_bias: float32 [2, 512], replicated
- gradient_attention_out: float32 [2, 256, 256], replicated
- gradient_attention_out_bias: float32 [2, 256], replicated
- gradient_attention_gain: float32 [2, 256], replicated
- gradient_attention_shift: float32 [2, 256], replicated
- gradient_expand_weight: float32 [2, 256, 512], replicated
- gradient_expand_bias: float32 [2, 512], replicated
- gradient_contract_weight: float32 [2, 512, 256], replicated
- gradient_contract_bias: float32 [2, 256], replicated
- gradient_feed_gain: float32 [2, 256], replicated
- gradient_feed_shift: float32 [2, 256], replicated
The draws below stay inside these ranges and needn't reach their ends.
Inputs may be any that keep to these rules, and one draw needn't show every extreme that they name: `segments`: along a row the numbers never fall; each of the 8 numbers marks one document of 1 to 512 consecutive positions, and some document has exactly 512.
All inputs are finite; a program needn't handle non-finite values.
Results may differ from the reference program's by a relative error of at most 0.03.
The reference program's roundings to bfloat16 on the way count: a program that leaves them out, or rounds other values in their place, can miss the bound.
Values may be sent and summed in bfloat16 or wider, within the bound.
No kernel may reach another device: no remote copies, remote signals or barrier semaphores. Data moves between devices by JAX's collectives and lax.ppermute only.
A program may use at most 192 MiB of HBM per device.

```python
import math
import jax
import jax.numpy as jnp
import numpy as np
from jax import lax

D = 256
FF = 512
HEADS = 4
HEAD = 64
SEQ = 2048
LAYERS = 2
ROWS = 16


def shard_levels(stream_key, extent, split, smallest, largest):
    def one(dim, shards_of):
        draws = jax.random.uniform(jax.random.fold_in(jax.random.fold_in(stream_key, 6), dim), (shards_of,), jnp.float32, smallest / len(split), largest / len(split))
        return jnp.repeat(jnp.exp(draws), extent[dim] // shards_of).reshape((-1,) + (1,) * (len(extent) - dim - 1))

    gain = one(*split[0])
    for cut in split[1:]:
        gain = gain * one(*cut)
    return gain


def split_up(number_of, total, reach, lean):
    weights = [(1 << 20) // math.isqrt(grade ** lean) + 1 for grade in range(2, number_of + 1)]
    surplus, holding = total - reach - (number_of - 1), [1] * (number_of - 1)
    while surplus > 0:
        free = [i for i in range(number_of - 1) if holding[i] < reach]
        whole, remaining = sum([weights[i] for i in free]), surplus
        for i in free:
            more = min(reach - holding[i], max(1, remaining * weights[i] // whole), surplus)
            holding[i] = holding[i] + more
            surplus = surplus - more
    return np.array([reach] + holding)


def uneven(key, count, total, reach, lean):
    if count == 2:
        one = jax.random.randint(key, (), max(1, total - reach), min(reach, total - 1) + 1)
        return jnp.stack([one, total - one])
    sizes = jnp.asarray(split_up(count, total, reach, lean), jnp.int32)
    pairs = (count - 1) // 2
    source_of, sink = sizes[1:1 + 2 * pairs:2], sizes[2:2 + 2 * pairs:2]
    slack = jnp.minimum(source_of - 1, reach - sink)
    passed = jax.random.randint(jax.random.fold_in(key, 1), (pairs,), 0, 1 << 20) % (slack + 1)
    sizes = sizes.at[1:1 + 2 * pairs:2].set(source_of - passed).at[2:2 + 2 * pairs:2].set(sink + passed)
    return sizes[jax.random.permutation(jax.random.fold_in(key, 2), count)]


def scatter_about(key, shape, width, reach, pieces=(), kind=jnp.bfloat16):
    drawn = jax.random.normal(key, shape, jnp.float32) * width
    if len(pieces) > 0:
        drawn = shard_levels(key, shape, pieces, -0.22, 0.18) * drawn
    return jnp.clip(drawn, min=-reach, max=reach).astype(kind)


def setup_inputs(seed: int = 0) -> dict:
    keys = jax.random.split(jax.random.key(seed), 16)
    return {
        "tokens": scatter_about(keys[0], (ROWS, SEQ, D), 1.0, 6.0, ((0, 8), (1, 4))),
        "segments": jax.vmap(lambda own: jnp.searchsorted(jnp.cumsum(uneven(own, 8, SEQ, SEQ // 4, 0)), jnp.arange(SEQ), side="right"))(jax.random.split(keys[1], ROWS)).reshape((ROWS, SEQ)).astype(jnp.int32),
        "cotangent": scatter_about(keys[2], (ROWS, SEQ, D), 1.0, 6.0, ((0, 8), (1, 4))),
        "attention_in": scatter_about(keys[3], (LAYERS, D, 3 * D), (D // 2) ** -0.5, 0.5),
        "attention_in_bias": scatter_about(keys[4], (LAYERS, 2 * D), 0.5, 3.0, (), jnp.float32),
        "attention_out": scatter_about(keys[5], (LAYERS, D, D), (D // 16) ** -0.5, 1.5),
        "attention_out_bias": scatter_about(keys[6], (LAYERS, D), 0.3, 2.0, (), jnp.float32),
        "attention_gain": jnp.clip(1.0 + 0.15 * jax.random.normal(keys[7], (LAYERS, D), jnp.float32), 0.25, 1.75),
        "attention_shift": scatter_about(keys[8], (LAYERS, D), 0.3, 2.0, (), jnp.float32),
        "expand_weight": scatter_about(keys[9], (LAYERS, D, FF), D ** -0.5, 0.375),
        "expand_bias": scatter_about(keys[10], (LAYERS, FF), 0.5, 3.0, (), jnp.float32),
        "contract_weight": scatter_about(keys[11], (LAYERS, FF, D), (FF // 2) ** -0.5, 0.375),
        "contract_bias": scatter_about(keys[12], (LAYERS, D), 0.3, 2.0, (), jnp.float32),
        "feed_gain": jnp.clip(1.0 + 0.15 * jax.random.normal(keys[13], (LAYERS, D), jnp.float32), 0.25, 1.75),
        "feed_shift": scatter_about(keys[14], (LAYERS, D), 0.3, 2.0, (), jnp.float32),
    }


@jax.custom_vjp
def low(v):
    return lax.optimization_barrier(v.astype(jnp.bfloat16)).astype(jnp.float32)

@jax.custom_vjp
def low_back(v):
    return v

def low_keep(v):
    return (low(v), None)

def low_pass(kept, grad):
    return (grad,)

def back_keep(v):
    return (v, None)

def back_low(kept, grad):
    return (low(grad),)
low.defvjp(low_keep, low_pass)
low_back.defvjp(back_keep, back_low)
EPSILON = 1e-12
MASKED = -1e+30
HIGHEST_PRECISION = lax.Precision.HIGHEST

def normalize(values, norm_gain, norm_shift):
    average = lax.optimization_barrier(jnp.mean(values, axis=-1, keepdims=True))
    centred = values - average
    spread = lax.optimization_barrier(jnp.mean(centred * centred, axis=-1, keepdims=True))
    return centred * lax.rsqrt(spread + EPSILON) * norm_gain + norm_shift

def attend_row(row_pair):
    joined_qkv, seg_row = row_pair
    query_heads = joined_qkv[:, :D].reshape(SEQ, HEADS, HEAD)
    key_heads = joined_qkv[:, D:2 * D].reshape(SEQ, HEADS, HEAD)
    value_heads = joined_qkv[:, 2 * D:].reshape(SEQ, HEADS, HEAD)
    scores = jnp.einsum('qhd,khd->hqk', query_heads, key_heads, precision=HIGHEST_PRECISION) * HEAD ** (-0.5)
    scores = jnp.where((seg_row[:, None] == seg_row[None, :])[None], scores, MASKED)
    scores = low_back(scores)
    highest = lax.optimization_barrier(jnp.max(scores, axis=-1, keepdims=True))
    raised = jnp.exp(scores - highest)
    probs_full = raised / lax.optimization_barrier(jnp.sum(raised, axis=-1, keepdims=True))
    probs_low = low(probs_full)
    context = jnp.einsum('hqk,khd->qhd', probs_low, value_heads, precision=HIGHEST_PRECISION)
    return context.reshape(SEQ, D)

def attention_section(hidden, segments, weight_in, bias_in, weight_out, bias_out, norm_gain, norm_shift):
    bias_full = jnp.concatenate([bias_in[:D], jnp.zeros((D,), jnp.float32), bias_in[D:]])
    joined_qkv = jnp.einsum('rsd,de->rse', hidden, weight_in, precision=HIGHEST_PRECISION) + bias_full
    joined_qkv = low_back(low(joined_qkv))
    context = lax.map(jax.checkpoint(attend_row), (joined_qkv, segments))
    context = low_back(low(context))
    branch = low_back(jnp.einsum('rsd,de->rse', context, weight_out, precision=HIGHEST_PRECISION) + bias_out)
    return normalize(hidden + branch, norm_gain, norm_shift)

def feed_section(hidden, weight_up, bias_up, weight_down, bias_down, norm_gain, norm_shift):
    pre_up = low_back(jnp.einsum('rsd,df->rsf', hidden, weight_up, precision=HIGHEST_PRECISION) + bias_up)
    active = low(jax.nn.gelu(pre_up, approximate=False))
    branch = low_back(jnp.einsum('rsf,fd->rsd', active, weight_down, precision=HIGHEST_PRECISION) + bias_down)
    return normalize(hidden + branch, norm_gain, norm_shift)

def forward(tokens, segments, attention_in, attention_in_bias, attention_out, attention_out_bias, attention_gain, attention_shift, expand_weight, expand_bias, contract_weight, contract_bias, feed_gain, feed_shift):
    hidden = tokens
    for layer_position in range(LAYERS):
        hidden = attention_section(hidden, segments, attention_in[layer_position], attention_in_bias[layer_position], attention_out[layer_position], attention_out_bias[layer_position], attention_gain[layer_position], attention_shift[layer_position])
        hidden = low_back(low(hidden))
        hidden = feed_section(hidden, expand_weight[layer_position], expand_bias[layer_position], contract_weight[layer_position], contract_bias[layer_position], feed_gain[layer_position], feed_shift[layer_position])
        if layer_position + 1 < LAYERS:
            hidden = low_back(low(hidden))
    return hidden

def reference(tokens, segments, cotangent, attention_in, attention_in_bias, attention_out, attention_out_bias, attention_gain, attention_shift, expand_weight, expand_bias, contract_weight, contract_bias, feed_gain, feed_shift):
    floats = tuple((source.astype(jnp.float32) for source in (tokens, attention_in, attention_in_bias, attention_out, attention_out_bias, attention_gain, attention_shift, expand_weight, expand_bias, contract_weight, contract_bias, feed_gain, feed_shift)))

    def wrapped(*operands):
        return forward(operands[0], segments, *operands[1:])
    output, pullback = jax.vjp(wrapped, *floats)
    gradients = pullback(cotangent.astype(jnp.float32))
    return (output.astype(jnp.bfloat16), gradients[0].astype(jnp.bfloat16), gradients[1], gradients[2], gradients[3], gradients[4], gradients[5], gradients[6], gradients[7], gradients[8], gradients[9], gradients[10], gradients[11], gradients[12])
```

```python
from types import SimpleNamespace

import jax
import jax.numpy as jnp
from jax import lax
from jax.experimental import pallas as pl
from jax.experimental.pallas import tpu as pltpu
from jax.sharding import PartitionSpec as P

HEADS = 4
EPSILON = 1e-12
MASKED = -1e30
DOCS = 8
TB = 256
QB = 128
LANES = 128
VMEM_LIMIT = 60 * 1024 * 1024

BF = jnp.bfloat16
F32 = jnp.float32

KEPT = dict(
    x=(256, BF),
    qkv=(768, BF),
    ctx=(256, BF),
    n1=(256, BF),
    r1=(128, F32),
    mid=(256, BF),
    act=(512, BF),
    slope=(512, BF),
    n2=(256, BF),
    r2=(128, F32),
)
NAMES = tuple(KEPT)


def dot(a, b):
    return jnp.dot(a, b, preferred_element_type=F32)


def dot_nt(a, b):
    return lax.dot_general(a, b, (((1,), (1,)), ((), ())), preferred_element_type=F32)


def dot_tn(a, b):
    return lax.dot_general(a, b, (((0,), (0,)), ((), ())), preferred_element_type=F32)


def fold(v):
    return v.reshape(-1, 8, v.shape[-1]).sum(0)


def rows_at(start, count):
    return pl.ds(pl.multiple_of(start, 16), count)


def block(b):
    return pl.ds(pl.multiple_of(b * TB, TB), TB)


class Plan:
    def __init__(self, given, table, items):
        self.given, self.table, self.items = given, table, items

        def one(d, carry):
            offset, tile = carry
            table[d] = offset
            table[items + d] = tile
            length = given[items + d]
            count = lax.shift_right_logical(length + (QB - 1), 7)
            return offset + lax.bitwise_and(length + 15, -16), tile + count * count

        total, _ = lax.fori_loop(0, items, one, (jnp.int32(0), jnp.int32(0)))
        self.blocks = lax.shift_right_logical(total + (TB - 1), 8)

    def start(self, d):
        return self.given[d]

    def length(self, d):
        return self.given[self.items + d]

    def offset(self, d):
        return self.table[d]

    def tile(self, d):
        return self.table[self.items + d]

    def over_docs(self, most, visit):
        def one(d, _):
            length = self.length(d)
            for n in range(1, most + 1):

                @pl.when(lax.shift_right_logical(length + (QB - 1), 7) == n)
                def _():
                    visit(d, n, length)

            return 0

        lax.fori_loop(0, self.items, one, 0)

    def over_blocks(self, visit):
        def one(b, _):
            visit(b)
            return 0

        lax.fori_loop(0, self.blocks, one, 0)


def fill_window(win, own, left, right, span):
    half = left.shape[1]
    whole = own.shape[1]
    for r in range(own.shape[0]):
        base = r * span
        win[pl.ds(base, half), :] = left[r]
        win[pl.ds(base + half, whole), :] = own[r]
        win[pl.ds(base + half + whole, half), :] = right[r]
        clear(win, pl.ds(base + 2 * whole, span - 2 * whole))


REACH = QB + 16


def pack(plan, most, win, dst):
    plan.over_blocks(lambda b: clear(dst, block(b)))

    def visit(d, n, length):
        start, offset = plan.start(d), plan.offset(d)
        shift = lax.bitwise_and(start, 15)
        row = lax.broadcasted_iota(jnp.int32, (QB, REACH), 0)
        col = lax.broadcasted_iota(jnp.int32, (QB, REACH), 1)
        for q in range(n):
            rows = win[rows_at(start - shift + q * QB, REACH), :]
            taken = (col == row + shift) & (row < length - q * QB)
            picked = dot(jnp.where(taken, 1.0, 0.0).astype(BF), rows)
            dst[rows_at(offset + q * QB, QB), :] = picked.astype(BF)

    plan.over_docs(most, visit)


def unpack(plan, most, src, win, own, left, right, span):
    win[...] = jnp.zeros(win.shape, BF)
    clear(src, rows_at(plan.blocks * TB, QB))

    def visit(d, n, length):
        start, offset = plan.start(d), plan.offset(d)
        shift = lax.bitwise_and(start, 15)
        row = lax.broadcasted_iota(jnp.int32, (REACH, QB), 0)
        col = lax.broadcasted_iota(jnp.int32, (REACH, QB), 1)
        for q in range(n):
            rows = src[rows_at(offset + q * QB, QB), :]
            taken = (row == col + shift) & (col < length - q * QB)
            placed = dot(jnp.where(taken, 1.0, 0.0).astype(BF), rows)
            at = rows_at(start - shift + q * QB, REACH)
            win[at, :] = (win[at, :].astype(F32) + placed).astype(BF)

    plan.over_docs(most, visit)
    half = left.shape[1]
    whole = own.shape[1]
    for r in range(own.shape[0]):
        base = r * span
        left[r] = win[pl.ds(base, half), :]
        own[r] = win[pl.ds(base + half, whole), :]
        right[r] = win[pl.ds(base + half + whole, half), :]


def clear(ref, rows):
    ref[rows, :] = jnp.zeros((rows.size, ref.shape[1]), ref.dtype)


def head_masks():
    lane = lax.broadcasted_iota(jnp.int32, (1, LANES), 1)
    low = (lane < LANES // 2).astype(F32)
    return low.astype(BF), (1.0 - low).astype(BF)


def two_heads(v, masks):
    return jnp.concatenate([v * masks[0], v * masks[1]], axis=0)


def one_of_two(v):
    lane = lax.broadcasted_iota(jnp.int32, (QB, LANES), 1)
    return jnp.where(lane < LANES // 2, v[:QB], v[QB:])


def project(plan, kept, weight, bias):
    scaling = (weight.shape[0] // HEADS) ** (-0.5)

    def visit(b):
        rows = block(b)
        y = dot(kept.x[rows, :], weight[...])
        queries = (y[:, 0:256] + bias[:, 0:256]).astype(BF)
        kept.qkv[rows, 0:256] = queries * jnp.asarray(scaling, BF)
        kept.qkv[rows, 256:512] = y[:, 256:512].astype(BF)
        kept.qkv[rows, 512:768] = (y[:, 512:768] + bias[:, 256:512]).astype(BF)
        clear(kept.ctx, rows)

    plan.over_blocks(visit)
    clear(kept.qkv, rows_at(plan.blocks * TB, QB))


def attend(plan, most, kept, weights_low):
    masks = head_masks()

    def visit(d, n, length):
        offset, tile = plan.offset(d), plan.tile(d)
        width = n * QB
        keys_at = rows_at(offset, width)

        def one(q, _):
            queries_at = rows_at(offset + q * QB, QB)
            row = lax.broadcasted_iota(jnp.int32, (QB, 1), 0) + q * QB
            row = jnp.concatenate([row, row], axis=0)
            for g in range(2):
                cols = g * LANES
                keys = kept.qkv[keys_at, 256 + cols : 256 + cols + LANES]
                values = kept.qkv[keys_at, 512 + cols : 512 + cols + LANES]
                queries = two_heads(kept.qkv[queries_at, cols : cols + LANES], masks)
                scores = dot_nt(queries, keys)
                last = scores[:, width - QB :]
                col = lax.broadcasted_iota(jnp.int32, last.shape, 1)
                last = jnp.where(col < length - (width - QB), last, MASKED)
                if n > 1:
                    scores = jnp.concatenate([scores[:, : width - QB], last], axis=1)
                else:
                    scores = last
                highest = jnp.max(scores, axis=1, keepdims=True)
                raised = jnp.exp(scores - highest)
                total = jnp.sum(raised, axis=1, keepdims=True)
                share = jnp.where(row < length, 1.0 / total, 0.0)
                probs = (raised * share).astype(BF)
                for k in range(n):
                    weights_low[tile + q * n + k, g] = probs[:, k * QB : (k + 1) * QB]
                context = one_of_two(dot(probs, values))
                kept.ctx[queries_at, cols : cols + LANES] = context.astype(BF)
            return 0

        lax.fori_loop(0, n, one, 0)

    plan.over_docs(most, visit)


def normal(v):
    centred = v - jnp.mean(v, axis=1, keepdims=True)
    spread = jnp.mean(centred * centred, axis=1, keepdims=True)
    rate = lax.rsqrt(spread + EPSILON)
    return centred * rate, rate


def feed(plan, kept, w, out, each=None):
    def visit(b):
        rows = block(b)
        x = kept.x[rows, :].astype(F32)
        attn_sum = x + dot(kept.ctx[rows, :], w.wout[...]) + w.bout[...]
        n1, r1 = normal(attn_sum)
        kept.n1[rows, :] = n1.astype(BF)
        kept.r1[rows, :] = jnp.broadcast_to(r1, (TB, LANES))
        mid_low = (n1 * w.g1[...] + w.s1[...]).astype(BF)
        kept.mid[rows, :] = mid_low
        pre_up = dot(mid_low, w.wup[...]) + w.bup[...]
        share = 0.5 + 0.5 * lax.erf(pre_up * (0.5**0.5))
        density = jnp.exp(pre_up * pre_up * -0.5) * 0.3989422804014327
        active = (pre_up * share).astype(BF)
        kept.act[rows, :] = active
        kept.slope[rows, :] = (share + pre_up * density).astype(BF)
        feed_sum = mid_low.astype(F32) + dot(active, w.wdown[...]) + w.bdown[...]
        n2, r2 = normal(feed_sum)
        kept.n2[rows, :] = n2.astype(BF)
        kept.r2[rows, :] = jnp.broadcast_to(r2, (TB, LANES))
        out[rows, :] = (n2 * w.g2[...] + w.s2[...]).astype(BF)
        if each is not None:
            each(b)

    plan.over_blocks(visit)


AT_OUT, AT_UP, AT_DOWN, AT_ALL = 768, 1024, 1536, 2048
V_IN, V_OUT, V_G1, V_S1, V_UP, V_DOWN, V_G2, V_S2, V_ALL = 0, 2, 3, 4, 5, 7, 8, 9, 16


def norm_back(upstream, n, rate, gain):
    e = upstream * gain
    inner = jnp.mean(e * n, axis=1, keepdims=True)
    return (e - jnp.mean(e, axis=1, keepdims=True) - n * inner) * rate


def feed_back(plan, kept, w, upstream, r):
    total, small, ctx_grad, sum_grad = r.s_total, r.s_small, r.s_ctx_grad, r.s_sum_grad

    def visit(b):
        rows = block(b)
        up = upstream[rows, :].astype(F32)
        n2 = kept.n2[rows, :].astype(F32)
        small[V_G2] += fold(up * n2)
        small[V_S2] += fold(up)
        r2 = kept.r2[rows, :]
        feed_grad = norm_back(up, n2, jnp.concatenate([r2, r2], axis=1), w.g2[...])
        low = feed_grad.astype(BF)
        small[V_DOWN] += fold(low.astype(F32))
        total[AT_DOWN:AT_ALL, :] += dot_tn(kept.act[rows, :], low)
        active_grad = dot_nt(low, w.wdown[...])
        pre_grad = (active_grad * kept.slope[rows, :].astype(F32)).astype(BF)
        sums = fold(pre_grad.astype(F32))
        small[V_UP] += sums[:, :256]
        small[V_UP + 1] += sums[:, 256:]
        up_grad = dot_tn(kept.mid[rows, :], pre_grad)
        total[AT_UP : AT_UP + 256, :] += up_grad[:, :256]
        total[AT_UP + 256 : AT_DOWN, :] += up_grad[:, 256:]
        mid_grad = (dot_nt(pre_grad, w.wup[...]) + feed_grad).astype(BF).astype(F32)
        n1 = kept.n1[rows, :].astype(F32)
        small[V_G1] += fold(mid_grad * n1)
        small[V_S1] += fold(mid_grad)
        r1 = kept.r1[rows, :]
        attn_grad = norm_back(mid_grad, n1, jnp.concatenate([r1, r1], axis=1), w.g1[...])
        sum_grad[rows, :] = attn_grad
        low = attn_grad.astype(BF)
        small[V_OUT] += fold(low.astype(F32))
        total[AT_OUT:AT_UP, :] += dot_tn(kept.ctx[rows, :], low)
        ctx_grad[rows, :] = dot_nt(low, w.wout[...]).astype(BF)

    plan.over_blocks(visit)
    clear(ctx_grad, rows_at(plan.blocks * TB, QB))


def attend_back(plan, most, kept, r):
    weights_low, ctx_grad, qkv_grad = r.s_probs, r.s_ctx_grad, r.s_qkv_grad
    key_sums, value_sums = r.s_key_sums, r.s_value_sums
    masks = head_masks()
    scaling = (256 // HEADS) ** (-0.5)
    plan.over_blocks(lambda b: clear(qkv_grad, block(b)))

    def visit(d, n, length):
        offset, tile = plan.offset(d), plan.tile(d)
        width = n * QB
        keys_at = rows_at(offset, width)
        key_sums[:width, :] = jnp.zeros((width, 256), F32)
        value_sums[:width, :] = jnp.zeros((width, 256), F32)

        def one(q, _):
            queries_at = rows_at(offset + q * QB, QB)
            for g in range(2):
                cols = g * LANES
                here = slice(cols, cols + LANES)
                keys = kept.qkv[keys_at, 256 + cols : 256 + cols + LANES]
                values = kept.qkv[keys_at, 512 + cols : 512 + cols + LANES]
                queries = two_heads(kept.qkv[queries_at, here], masks)
                grads = two_heads(ctx_grad[queries_at, here], masks)
                probs = [weights_low[tile + q * n + k, g] for k in range(n)]
                probs = jnp.concatenate(probs, axis=1) if n > 1 else probs[0]
                full = probs.astype(F32)
                prob_grad = dot_nt(grads, values)
                inner = jnp.sum(full * prob_grad, axis=1, keepdims=True)
                score_grad = (full * (prob_grad - inner)).astype(BF)
                query_grad = one_of_two(dot(score_grad, keys)) * scaling
                qkv_grad[queries_at, here] = query_grad.astype(BF)
                key_sums[:width, here] += dot_tn(score_grad, queries)
                value_sums[:width, here] += dot_tn(probs, grads)
            return 0

        lax.fori_loop(0, n, one, 0)
        qkv_grad[keys_at, 256:512] = key_sums[:width, :].astype(BF)
        qkv_grad[keys_at, 512:768] = value_sums[:width, :].astype(BF)

    plan.over_docs(most, visit)


def project_back(plan, kept, w, r, out):
    qkv_grad, sum_grad, total, small = r.s_qkv_grad, r.s_sum_grad, r.s_total, r.s_small

    def visit(b):
        rows = block(b)
        grad = qkv_grad[rows, :]
        sums = fold(grad.astype(F32))
        small[V_IN] += sums[:, :256]
        small[V_IN + 1] += sums[:, 512:]
        in_grad = dot_tn(kept.x[rows, :], grad)
        for k in range(3):
            total[256 * k : 256 * (k + 1), :] += in_grad[:, 256 * k : 256 * (k + 1)]
        hidden_grad = dot_nt(grad, w.win[...]) + sum_grad[rows, :]
        out[rows, :] = hidden_grad.astype(BF)

    plan.over_blocks(visit)


def first_kernel(layer, most, span, items, r):
    plan = Plan(r.plan, r.s_table, items)
    kept = SimpleNamespace(**{k: getattr(r, "s_" + k) for k in NAMES})
    w = layer_of(r, layer)

    def copy_block(k, b):
        there = getattr(r, "o_" + k).at[block(b)]
        return pltpu.make_async_copy(getattr(kept, k).at[block(b)], there, r.sems.at[NAMES.index(k)])

    def copy_probs(d, n):
        at = pl.ds(plan.tile(d), n * n)
        return pltpu.make_async_copy(r.s_probs.at[at], r.o_probs.at[at], r.sems.at[len(NAMES)])

    fill_window(r.s_window, r.own, r.left, r.right, span)
    pack(plan, most, r.s_window, kept.x)
    project(plan, kept, w.win, w.bin)
    early, late = NAMES[:2], NAMES[2:]
    plan.over_blocks(lambda b: [copy_block(k, b).start() for k in early])
    attend(plan, most, kept, r.s_probs)
    plan.over_docs(most, lambda d, n, length: copy_probs(d, n).start())
    feed(plan, kept, w, r.o_next, lambda b: [copy_block(k, b).start() for k in late])
    plan.over_blocks(lambda b: [copy_block(k, b).wait() for k in NAMES])
    plan.over_docs(most, lambda d, n, length: copy_probs(d, n).wait())


def second_kernel(layer, most, span, items, r):
    plan = Plan(r.plan, r.s_table, items)
    kept = SimpleNamespace(**{k: getattr(r, "s_" + k) for k in NAMES[1:]}, x=r.x)
    w = layer_of(r, layer)
    project(plan, kept, w.win, w.bin)
    attend(plan, most, kept, r.s_probs)
    feed(plan, kept, w, r.s_rows)
    unpack(plan, most, r.s_rows, r.s_window, r.o_own, r.o_left, r.o_right, span)
    fill_window(r.s_window, r.own, r.left, r.right, span)
    pack(plan, most, r.s_window, r.s_rows)
    clear_totals(r)
    feed_back(plan, kept, w, r.s_rows, r)
    attend_back(plan, most, kept, r)
    project_back(plan, kept, w, r, r.o_next)
    send_pieces(r)
    r.o_small[...] = r.s_small[...].sum(1)


def third_kernel(layer, most, span, items, r):
    plan = Plan(r.plan, r.s_table, items)
    kept = SimpleNamespace(**{k: getattr(r, "s_" + k) for k in NAMES})
    w = layer_of(r, layer)

    def copy_block(k, b):
        given = getattr(r, "i_" + k).at[block(b)]
        return pltpu.make_async_copy(given, getattr(kept, k).at[block(b)], r.sems.at[NAMES.index(k)])

    def copy_probs(d, n):
        at = pl.ds(plan.tile(d), n * n)
        return pltpu.make_async_copy(r.i_probs.at[at], r.s_probs.at[at], r.sems.at[len(NAMES)])

    early, late = NAMES[2:], NAMES[:2]
    plan.over_blocks(lambda b: [copy_block(k, b).start() for k in early])
    plan.over_docs(most, lambda d, n, length: copy_probs(d, n).start())
    plan.over_blocks(lambda b: [copy_block(k, b).start() for k in late])
    clear_totals(r)
    plan.over_blocks(lambda b: [copy_block(k, b).wait() for k in early])
    feed_back(plan, kept, w, r.rows, r)
    plan.over_docs(most, lambda d, n, length: copy_probs(d, n).wait())
    plan.over_blocks(lambda b: [copy_block(k, b).wait() for k in late])
    clear(kept.qkv, rows_at(plan.blocks * TB, QB))
    attend_back(plan, most, kept, r)
    project_back(plan, kept, w, r, r.s_rows)
    unpack(plan, most, r.s_rows, r.s_window, r.o_own, r.o_left, r.o_right, span)
    send_pieces(r)
    send_small(r)


def layer_of(r, layer):
    w = SimpleNamespace(win=r.win, wout=r.wout, wup=r.wup, wdown=r.wdown)
    w = SimpleNamespace(**{k: v.at[layer] for k, v in vars(w).items()})
    vectors = dict(bin=r.bin, bout=r.bout, g1=r.g1, s1=r.s1, bup=r.bup, bdown=r.bdown, g2=r.g2, s2=r.s2)
    return SimpleNamespace(**vars(w), **{k: v[layer : layer + 1, :] for k, v in vectors.items()})


def clear_totals(r):
    r.s_total[...] = jnp.zeros(r.s_total.shape, F32)
    r.s_small[...] = jnp.zeros(r.s_small.shape, F32)


def send_pieces(r):
    count = 2 * r.o_keep.shape[0]
    rows = AT_ALL // count
    for p in range(count):
        out = r.o_keep if p < count // 2 else r.o_send
        piece = lax.bitwise_xor(jnp.int32(p), r.self[0])
        at = pl.ds(pl.multiple_of(piece * rows, rows), rows)
        out[p % (count // 2), 0:rows, :] = r.s_total[at, :].astype(BF)


def send_small(r):
    count = 2 * r.o_keep.shape[0]
    rows = AT_ALL // count
    extra = r.o_keep.shape[1] - rows
    share = 2 * V_ALL // count
    r.s_both[0:V_ALL, :] = r.s_small[...].sum(1)
    r.s_both[V_ALL : 2 * V_ALL, :] = r.small[...]
    for j in range(count):
        own = r.s_both[j * share : (j + 1) * share, :]
        r.s_spread[j] = jnp.concatenate([own, jnp.zeros((extra - share, own.shape[1]), F32)], axis=0)
    for p in range(count):
        out = r.o_keep if p < count // 2 else r.o_send
        piece = lax.bitwise_xor(jnp.int32(p), r.self[0])
        out[p % (count // 2), rows : rows + extra, :] = r.s_spread[piece].astype(BF)


def last_kernel(r):
    half = r.keep0.shape[0]
    count = 2 * half
    rows = AT_ALL // count
    share = 2 * V_ALL // count
    for layer, (keep, got) in enumerate(((r.keep0, r.got0), (r.keep1, r.got1))):
        for p in range(count):
            piece = lax.bitwise_xor(jnp.int32(p), r.self[layer])
            source = keep if p < half else got
            r.s_pieces[layer, piece, 0 : keep.shape[1], :] = source[p % half]
    for layer in range(2):
        for j in range(count):
            value = r.s_pieces[layer, j, 0:rows, :].astype(F32)
            at = j * rows
            for low, high, out in (
                (0, AT_OUT, r.o_in),
                (AT_OUT, AT_UP, r.o_out),
                (AT_UP, AT_DOWN, r.o_up),
                (AT_DOWN, AT_ALL, r.o_down),
            ):
                if low <= at < high:
                    tall = out.shape[1]
                    line, col = (at - low) % tall, (at - low) // tall * 256
                    out[layer, line : line + rows, col : col + 256] = value
    for j in range(count):
        tail = r.s_pieces[0, j, rows : rows + 16, :].astype(F32)
        r.s_both[j * share : (j + 1) * share, :] = tail[0:share]
    for layer in range(2):
        at = layer * V_ALL
        here = pl.ds(layer, 1)

        def line(k):
            return r.s_both[at + k : at + k + 1, :]

        r.o_bin[here, :] = jnp.concatenate([line(V_IN), line(V_IN + 1)], axis=1)
        r.o_bout[here, :] = line(V_OUT)
        r.o_g1[here, :] = line(V_G1)
        r.o_s1[here, :] = line(V_S1)
        r.o_bup[here, :] = jnp.concatenate([line(V_UP), line(V_UP + 1)], axis=1)
        r.o_bdown[here, :] = line(V_DOWN)
        r.o_g2[here, :] = line(V_G2)
        r.o_s2[here, :] = line(V_S2)


def call(kernel, consts, inputs, outputs, scratch, flops):
    names = tuple(inputs) + tuple(outputs) + tuple(scratch)

    def run(*refs):
        kernel(*consts, SimpleNamespace(**dict(zip(names, refs))))

    got = pl.pallas_call(
        run,
        out_shape=[jax.ShapeDtypeStruct(s, d) for s, d, _ in outputs.values()],
        in_specs=[spec for _, spec in inputs.values()],
        out_specs=[spec for _, _, spec in outputs.values()],
        scratch_shapes=list(scratch.values()),
        compiler_params=pltpu.CompilerParams(vmem_limit_bytes=VMEM_LIMIT),
        cost_estimate=pl.CostEstimate(flops=flops, bytes_accessed=8 << 20, transcendentals=0),
    )(*[a for a, _ in inputs.values()])
    return SimpleNamespace(**dict(zip(outputs, got)))


def make_plan(segments, place, section_count):
    row_count, length = segments.shape
    whole = length // section_count
    half = whole // 2
    span = 2 * whole + 2 * QB
    ids = jnp.arange(DOCS + 1, dtype=jnp.int32)
    starts = jnp.sum((segments[:, None, :] < ids[None, :, None]).astype(jnp.int32), axis=2)
    targets = jnp.arange(1, section_count, dtype=jnp.int32) * whole
    away = starts[None] - targets[:, None, None]
    far = (jnp.abs(away) > half).astype(jnp.int32) * (1 << 16)
    base = DOCS + 1
    if row_count == 2:
        cost = jnp.abs(away[:, 0, :, None] + away[:, 1, None, :])
        cost = cost + far[:, 0, :, None] + far[:, 1, None, :]
        code = ids[:, None] * base + ids[None, :]
        best = jnp.min(cost * (base * base) + code[None], axis=(1, 2)) % (base * base)
        chosen = jnp.stack([best // base, best % base], axis=1)
    else:
        chosen = jnp.min((jnp.abs(away) + far) * base + ids, axis=2) % base
    first = jnp.zeros((1, row_count), jnp.int32)
    cuts = jnp.concatenate([first, chosen, first + DOCS], axis=0)
    sections = jnp.arange(section_count + 1)[:, None]
    low = jnp.sum(jnp.where(sections == place, cuts, 0), axis=0)[:, None]
    high = jnp.sum(jnp.where(sections == place + 1, cuts, 0), axis=0)[:, None]
    here = (ids[None, :DOCS] >= low) & (ids[None, :DOCS] < high)
    lengths = jnp.where(here, starts[:, 1:] - starts[:, :-1], 0)
    begins = starts[:, :-1] - place * whole + half
    begins = begins + jnp.arange(row_count, dtype=jnp.int32)[:, None] * span
    begins = jnp.where(here, begins, 0)
    return jnp.stack([begins, lengths]).reshape(-1)


def swapped(low_part, high_part, place, odd):
    count = lax.axis_size("pipe")
    pairs = [(i, i + 1) for i in range(odd, count - 1, 2)]
    upper = lax.rem(place + odd, 2) == 1
    sent = jnp.where(upper, low_part, high_part)
    got = lax.ppermute(sent, "pipe", [p for i, j in pairs for p in ((i, j), (j, i))])
    return upper, got


def halo(low_part, high_part, place):
    even_upper, even = swapped(low_part, high_part, place, 0)
    odd_upper, odd = swapped(low_part, high_part, place, 1)
    return jnp.where(even_upper, even, odd), jnp.where(odd_upper, even, odd)


def orders():
    found = []
    for axis in ("dp", "pipe"):
        stride = 1
        while stride < lax.axis_size(axis):
            found.append((axis, stride))
            stride *= 2
    other = list(found)
    if len(found) > 2:
        other[1], other[2] = found[2], found[1]
    return found, other


SPLIT = 4


def self_index(order):
    index = jnp.int32(0)
    for axis, stride in order[:SPLIT]:
        index = 2 * index + lax.rem(lax.div(lax.axis_index(axis), stride), 2)
    return index.astype(jnp.int32)


def exchange(value, axis, stride):
    count = lax.axis_size(axis)
    return lax.ppermute(value, axis, [(i, i ^ stride) for i in range(count)])


def added(a, b):
    return (a.astype(F32) + b.astype(F32)).astype(BF)


def sum_steps(keep, send, order):
    total = None
    for k, (axis, stride) in enumerate(order[:SPLIT]):
        got = exchange(send, axis, stride)
        yield None
        half = keep.shape[0] // 2
        if half:
            send, keep = added(keep[half:], got[half:]), added(keep[:half], got[:half])
        else:
            total = added(keep, got)
    for axis, stride in order[SPLIT:]:
        got = exchange(total, axis, stride)
        yield None
        total = added(total, got)
    for k, (axis, stride) in enumerate(reversed(order[:SPLIT])):
        got = exchange(total, axis, stride)
        yield (total, got)
        total = jnp.concatenate([total, got], axis=0)


def body(
    tokens,
    segments,
    cotangent,
    attention_in,
    attention_in_bias,
    attention_out,
    attention_out_bias,
    attention_gain,
    attention_shift,
    expand_weight,
    expand_bias,
    contract_weight,
    contract_bias,
    feed_gain,
    feed_shift,
):
    section_count = lax.axis_size("pipe")
    place = lax.axis_index("pipe").astype(jnp.int32)
    row_count, whole, features = tokens.shape
    half = whole // 2
    span = 2 * whole + 2 * QB
    items = row_count * DOCS
    most = whole // QB
    cap = row_count * 2 * whole + items * 16 + QB
    cap = (cap + TB - 1) // TB * TB
    tiles = row_count * 42
    vmem = pl.BlockSpec(memory_space=pltpu.VMEM)
    smem = pl.BlockSpec(memory_space=pltpu.SMEM)
    anywhere = pl.BlockSpec(memory_space=pl.ANY)
    weights = dict(
        win=attention_in,
        bin=attention_in_bias,
        wout=attention_out,
        bout=attention_out_bias,
        g1=attention_gain,
        s1=attention_shift,
        wup=expand_weight,
        bup=expand_bias,
        wdown=contract_weight,
        bdown=contract_bias,
        g2=feed_gain,
        s2=feed_shift,
    )
    weights = {k: (v, vmem) for k, v in weights.items()}

    def with_halo(value):
        left, right = halo(value[:, :half], value[:, half:], place)
        return dict(own=(value, vmem), left=(left, vmem), right=(right, vmem))

    def placed(got):
        low, high = halo(got.o_left, got.o_right, place)
        return got.o_own + jnp.concatenate([low, high], axis=1)

    order0, order1 = orders()
    selves = [self_index(order0), self_index(order1)]
    pieces = 1 << SPLIT
    token_rows = with_halo(tokens)
    plan = dict(plan=(make_plan(segments, place, section_count), smem))
    kept_scratch = {"s_" + k: pltpu.VMEM((cap, c), t) for k, (c, t) in KEPT.items()}
    probs_shape = (tiles, 2, 2 * QB, QB)
    kept_scratch.update(
        s_probs=pltpu.VMEM(probs_shape, BF),
        s_window=pltpu.VMEM((row_count * span, features), BF),
        s_table=pltpu.SMEM((2 * items,), jnp.int32),
    )
    sems = dict(sems=pltpu.SemaphoreType.DMA((len(NAMES) + 1,)))
    back_scratch = dict(
        s_rows=pltpu.VMEM((cap, features), BF),
        s_total=pltpu.VMEM((AT_ALL, features), F32),
        s_small=pltpu.VMEM((V_ALL, 8, features), F32),
        s_ctx_grad=pltpu.VMEM((cap, features), BF),
        s_sum_grad=pltpu.VMEM((cap, features), F32),
        s_qkv_grad=pltpu.VMEM((cap, 3 * features), BF),
        s_key_sums=pltpu.VMEM((whole, features), F32),
        s_value_sums=pltpu.VMEM((whole, features), F32),
    )
    window_out = dict(
        o_own=((row_count, whole, features), BF, vmem),
        o_left=((row_count, half, features), BF, vmem),
        o_right=((row_count, half, features), BF, vmem),
    )

    def pieces_out(extra):
        shape = (pieces // 2, AT_ALL // pieces + extra, features)
        return dict(o_keep=(shape, BF, vmem), o_send=(shape, BF, vmem))

    next_out = dict(o_next=((cap, features), BF, vmem))
    kept_out = {"o_" + k: ((cap, c), t, anywhere) for k, (c, t) in KEPT.items()}
    kept_out.update(o_probs=(probs_shape, BF, anywhere))

    first = call(
        first_kernel,
        (0, most, span, items),
        plan | token_rows | weights,
        kept_out | next_out,
        kept_scratch | sems,
        12 << 30,
    )
    cotangent_rows = with_halo(cotangent)
    second = call(
        second_kernel,
        (1, most, span, items),
        plan
        | cotangent_rows
        | dict(x=(first.o_next, vmem), self=(selves[1].reshape(1), smem))
        | weights,
        window_out
        | pieces_out(0)
        | next_out
        | dict(o_small=((V_ALL, features), F32, vmem)),
        {k: v for k, v in kept_scratch.items() if k != "s_x"} | back_scratch,
        36 << 30,
    )
    kept_in = {"i_" + k: (getattr(first, "o_" + k), anywhere) for k in NAMES + ("probs",)}
    third = call(
        third_kernel,
        (0, most, span, items),
        plan
        | kept_in
        | dict(
            rows=(second.o_next, vmem),
            small=(second.o_small, vmem),
            self=(selves[0].reshape(1), smem),
        )
        | weights,
        window_out | pieces_out(16),
        kept_scratch
        | back_scratch
        | sems
        | dict(
            s_both=pltpu.VMEM((2 * V_ALL, features), F32),
            s_spread=pltpu.VMEM((pieces, 16, features), F32),
        ),
        24 << 30,
    )
    layer_output = placed(second)
    input_grad = placed(third)
    sums = [sum_steps(third.o_keep, third.o_send, order0)]
    sums.append(sum_steps(second.o_keep, second.o_send, order1))
    for ends in zip(*sums):
        pass
    layers = attention_in.shape[0]

    def out(*shape):
        return ((layers,) + shape, F32, vmem)

    vector = out(features)
    result = call(
        last_kernel,
        (),
        dict(
            self=(jnp.stack(selves), smem),
            keep0=(ends[0][0], vmem),
            got0=(ends[0][1], vmem),
            keep1=(ends[1][0], vmem),
            got1=(ends[1][1], vmem),
        ),
        dict(
            o_in=out(features, 3 * features),
            o_bin=out(2 * features),
            o_out=out(features, features),
            o_bout=vector,
            o_g1=vector,
            o_s1=vector,
            o_up=out(features, 2 * features),
            o_bup=out(2 * features),
            o_down=out(2 * features, features),
            o_bdown=vector,
            o_g2=vector,
            o_s2=vector,
        ),
        dict(
            s_pieces=pltpu.VMEM((2, pieces, AT_ALL // pieces + 16, features), BF),
            s_both=pltpu.VMEM((2 * V_ALL, features), F32),
        ),
        1 << 30,
    )
    return (layer_output, input_grad) + tuple(vars(result).values())


def solution(mesh):
    rows = P("dp", "pipe", None)
    return jax.shard_map(
        body,
        mesh=mesh,
        in_specs=(rows, P("dp", None), rows) + (P(),) * 12,
        out_specs=(rows, rows) + (P(),) * 12,
        check_vma=False,
    )
```

```python
from types import SimpleNamespace

import jax
import jax.numpy as jnp
from jax import lax
from jax.experimental import pallas as pl
from jax.experimental.pallas import tpu as pltpu
from jax.sharding import PartitionSpec as P

HEADS = 4
EPSILON = 1e-12
MASKED = -1e30
DOCS = 8
TB = 512
QB = 128
TURNS = (1, 2, 3, 4)
LANES = 128
VMEM_LIMIT = 60 * 1024 * 1024

BF = jnp.bfloat16
F32 = jnp.float32

KEPT = dict(
    x=(256, BF),
    qkv=(768, BF),
    ctx=(256, BF),
    n1=(256, BF),
    r1=(128, F32),
    mid=(256, BF),
    act=(512, BF),
    slope=(512, BF),
    n2=(256, BF),
    r2=(128, F32),
)
NAMES = tuple(KEPT)


def dot(a, b):
    return jnp.dot(a, b, preferred_element_type=F32)


def dot_nt(a, b):
    return lax.dot_general(a, b, (((1,), (1,)), ((), ())), preferred_element_type=F32)


def dot_tn(a, b):
    return lax.dot_general(a, b, (((0,), (0,)), ((), ())), preferred_element_type=F32)


def fold(v):
    return v.reshape(-1, 8, v.shape[-1]).sum(0)


def rows_at(start, count):
    return pl.ds(pl.multiple_of(start, 16), count)


def block(b):
    return pl.ds(pl.multiple_of(b * TB, TB), TB)


class Plan:
    def __init__(self, given, table, items):
        self.given, self.table, self.items = given, table, items

        def one(d, carry):
            offset, tile = carry
            table[d] = offset
            table[items + d] = tile
            length = given[items + d]
            count = lax.shift_right_logical(length + (QB - 1), 7)
            return offset + lax.bitwise_and(length + 15, -16), tile + count * count

        total, _ = lax.fori_loop(0, items, one, (jnp.int32(0), jnp.int32(0)))
        self.blocks = lax.shift_right_logical(total + (TB - 1), 9)

    def start(self, d):
        return self.given[d]

    def length(self, d):
        return self.given[self.items + d]

    def offset(self, d):
        return self.table[d]

    def tile(self, d):
        return self.table[self.items + d]

    def over_docs(self, most, visit):
        def one(d, _):
            length = self.length(d)
            for n in range(1, most + 1):

                @pl.when(lax.shift_right_logical(length + (QB - 1), 7) == n)
                def _():
                    visit(d, n, length)

            return 0

        lax.fori_loop(0, self.items, one, 0)

    def over_blocks(self, visit):
        def one(b, _):
            visit(b)
            return 0

        lax.fori_loop(0, self.blocks, one, 0)


def fill_window(win, own, left, right, span):
    half = left.shape[1]
    whole = own.shape[1]
    for r in range(own.shape[0]):
        base = r * span
        win[pl.ds(base, half), :] = left[r]
        win[pl.ds(base + half, whole), :] = own[r]
        win[pl.ds(base + half + whole, half), :] = right[r]
        clear(win, pl.ds(base + 2 * whole, span - 2 * whole))


REACH = QB + 16


def pack(plan, most, win, dst):
    plan.over_blocks(lambda b: clear(dst, block(b)))

    def visit(d, n, length):
        start, offset = plan.start(d), plan.offset(d)
        shift = lax.bitwise_and(start, 15)
        row = lax.broadcasted_iota(jnp.int32, (QB, REACH), 0)
        col = lax.broadcasted_iota(jnp.int32, (QB, REACH), 1)
        for q in range(n):
            rows = win[rows_at(start - shift + q * QB, REACH), :]
            taken = (col == row + shift) & (row < length - q * QB)
            picked = dot(jnp.where(taken, 1.0, 0.0).astype(BF), rows)
            dst[rows_at(offset + q * QB, QB), :] = picked.astype(BF)

    plan.over_docs(most, visit)


def unpack(plan, most, src, win, own, left, right, span):
    win[...] = jnp.zeros(win.shape, BF)
    clear(src, rows_at(plan.blocks * TB, QB))

    def visit(d, n, length):
        start, offset = plan.start(d), plan.offset(d)
        shift = lax.bitwise_and(start, 15)
        row = lax.broadcasted_iota(jnp.int32, (REACH, QB), 0)
        col = lax.broadcasted_iota(jnp.int32, (REACH, QB), 1)
        for q in range(n):
            rows = src[rows_at(offset + q * QB, QB), :]
            taken = (row == col + shift) & (col < length - q * QB)
            placed = dot(jnp.where(taken, 1.0, 0.0).astype(BF), rows)
            at = rows_at(start - shift + q * QB, REACH)
            win[at, :] = (win[at, :].astype(F32) + placed).astype(BF)

    plan.over_docs(most, visit)
    half = left.shape[1]
    whole = own.shape[1]
    for r in range(own.shape[0]):
        base = r * span
        left[r] = win[pl.ds(base, half), :]
        own[r] = win[pl.ds(base + half, whole), :]
        right[r] = win[pl.ds(base + half + whole, half), :]


def clear(ref, rows):
    ref[rows, :] = jnp.zeros((rows.size, ref.shape[1]), ref.dtype)


def head_masks():
    lane = lax.broadcasted_iota(jnp.int32, (1, LANES), 1)
    low = (lane < LANES // 2).astype(F32)
    return low.astype(BF), (1.0 - low).astype(BF)


def two_heads(v, masks):
    return jnp.concatenate([v * masks[0], v * masks[1]], axis=0)


def turned_back(v):
    row = lax.broadcasted_iota(jnp.int32, (LANES, QB), 0)
    return jnp.where(row < LANES // 2, v[:, :QB], v[:, QB:]).T


def turn(src, dst, width):
    for k in range(width // LANES):
        at = slice(k * LANES, (k + 1) * LANES)
        for g in range(2):
            here = slice(g * LANES, (g + 1) * LANES)
            dst[here, at] = src[at, here].T


def project(plan, kept, weight, bias):
    scaling = (weight.shape[0] // HEADS) ** (-0.5)

    def visit(b):
        rows = block(b)
        y = dot(kept.x[rows, :], weight[...])
        queries = (y[:, 0:256] + bias[:, 0:256]).astype(BF)
        kept.qkv[rows, 0:256] = queries * jnp.asarray(scaling, BF)
        kept.qkv[rows, 256:512] = y[:, 256:512].astype(BF)
        kept.qkv[rows, 512:768] = (y[:, 512:768] + bias[:, 256:512]).astype(BF)
        clear(kept.ctx, rows)

    plan.over_blocks(visit)
    clear(kept.qkv, rows_at(plan.blocks * TB, QB))


def in_turns(count, some):
    step = TURNS[count - 1]
    if step == count:
        some(0, count)
        return

    def one(k, _):
        some(k * step, step)
        return 0

    lax.fori_loop(0, count // step, one, 0)


def attend(plan, most, kept, weights_low, values_turned):
    masks = head_masks()

    def visit(d, n, length):
        offset, tile = plan.offset(d), plan.tile(d)
        width = n * QB
        keys_at = rows_at(offset, width)
        turn(kept.qkv[keys_at, 512:768], values_turned, width)

        def some(first, count):
            column = lax.broadcasted_iota(jnp.int32, (1, 2 * QB), 1)
            column = lax.bitwise_and(column, QB - 1)
            row = lax.broadcasted_iota(jnp.int32, (QB, 2 * QB), 0)
            inside = row < length - (width - QB)
            chains = [(first + q, g) for q in range(count) for g in range(2)]
            cols = [slice(g * LANES, (g + 1) * LANES) for g in range(2)]
            keys = [kept.qkv[keys_at, 256 + c.start : 256 + c.stop] for c in cols]
            turned = [values_turned[c, :width] for c in cols]
            queries = [kept.qkv[rows_at(offset + q * QB, QB), cols[g]] for q, g in chains]
            queries = [two_heads(v, masks) for v in queries]
            scores = [dot_nt(keys[g], v) for v, (_, g) in zip(queries, chains)]
            probs = []
            for v, (q, g) in zip(scores, chains):
                last = jnp.where(inside, v[width - QB :, :], MASKED)
                v = jnp.concatenate([v[: width - QB, :], last], axis=0) if n > 1 else last
                raised = jnp.exp(v - jnp.max(v, axis=0, keepdims=True))
                total = jnp.sum(raised, axis=0, keepdims=True)
                share = jnp.where(column + q * QB < length, 1.0 / total, 0.0)
                probs.append((raised * share).astype(BF))
            contexts = [dot(turned[g], v) for v, (_, g) in zip(probs, chains)]
            contexts = [turned_back(v).astype(BF) for v in contexts]
            for v, context, (q, g) in zip(probs, contexts, chains):
                kept.ctx[rows_at(offset + q * QB, QB), cols[g]] = context
                for k in range(n):
                    weights_low[tile + q * n + k, g] = v[k * QB : (k + 1) * QB, :]

        in_turns(n, some)

    plan.over_docs(most, visit)


def normal(v):
    centred = v - jnp.mean(v, axis=1, keepdims=True)
    spread = jnp.mean(centred * centred, axis=1, keepdims=True)
    rate = lax.rsqrt(spread + EPSILON)
    return centred * rate, rate


def parts_of(b, count):
    step = TB // count
    return [rows_at(b * TB + k * step, step) for k in range(count)]


def feed(plan, kept, w, out, each=None):
    def visit(b):
        chains = parts_of(b, 1)
        wout, wup, wdown = w.wout[...], w.wup[...], w.wdown[...]
        x = [kept.x[at, :] for at in chains]
        ctx = [kept.ctx[at, :] for at in chains]
        attn_sum = [u.astype(F32) + dot(v, wout) + w.bout for u, v in zip(x, ctx)]
        first = [normal(v) for v in attn_sum]
        mid_low = [(n * w.g1 + w.s1).astype(BF) for n, _ in first]
        pre_up = [dot(v, wup) + w.bup for v in mid_low]
        share = [0.5 + 0.5 * lax.erf(v * (0.5**0.5)) for v in pre_up]
        active = [(v * p).astype(BF) for v, p in zip(pre_up, share)]
        density = [jnp.exp(v * v * -0.5) * 0.3989422804014327 for v in pre_up]
        slope = [(p + v * q).astype(BF) for v, p, q in zip(pre_up, share, density)]
        feed_sum = [u.astype(F32) + dot(v, wdown) + w.bdown for u, v in zip(mid_low, active)]
        second = [normal(v) for v in feed_sum]
        for k, at in enumerate(chains):
            kept.n1[at, :] = first[k][0].astype(BF)
            kept.r1[at, :] = jnp.broadcast_to(first[k][1], (at.size, LANES))
            kept.mid[at, :] = mid_low[k]
            kept.act[at, :] = active[k]
            kept.slope[at, :] = slope[k]
            kept.n2[at, :] = second[k][0].astype(BF)
            kept.r2[at, :] = jnp.broadcast_to(second[k][1], (at.size, LANES))
            out[at, :] = (second[k][0] * w.g2 + w.s2).astype(BF)
        if each is not None:
            each(b)

    plan.over_blocks(visit)


AT_OUT, AT_UP, AT_DOWN, AT_ALL = 768, 1024, 1536, 2048
V_IN, V_OUT, V_G1, V_S1, V_UP, V_DOWN, V_G2, V_S2, V_ALL = 0, 2, 3, 4, 5, 7, 8, 9, 16


def norm_back(upstream, n, rate, gain):
    e = upstream * gain
    inner = jnp.mean(e * n, axis=1, keepdims=True)
    return (e - jnp.mean(e, axis=1, keepdims=True) - n * inner) * rate


def doubled(v):
    return jnp.concatenate([v, v], axis=1)


def joined(values):
    return jnp.concatenate(values, axis=0) if len(values) > 1 else values[0]


def feed_back(plan, kept, w, upstream, r):
    total, small, ctx_grad, sum_grad = r.s_total, r.s_small, r.s_ctx_grad, r.s_sum_grad

    def visit(b):
        chains = parts_of(b, 2)
        rows = block(b)
        wout, wup, wdown = w.wout[...], w.wup[...], w.wdown[...]
        up = [upstream[at, :].astype(F32) for at in chains]
        n2 = [kept.n2[at, :].astype(F32) for at in chains]
        r2 = [doubled(kept.r2[at, :]) for at in chains]
        slope = [kept.slope[at, :] for at in chains]
        n1 = [kept.n1[at, :].astype(F32) for at in chains]
        r1 = [doubled(kept.r1[at, :]) for at in chains]
        act, mid, ctx = kept.act[rows, :], kept.mid[rows, :], kept.ctx[rows, :]
        feed_grad = [norm_back(u, n, v, w.g2) for u, n, v in zip(up, n2, r2)]
        feed_low = [v.astype(BF) for v in feed_grad]
        active_grad = [dot_nt(v, wdown) for v in feed_low]
        pre_grad = [(v * p.astype(F32)).astype(BF) for v, p in zip(active_grad, slope)]
        mid_grad = [dot_nt(v, wup) + u for v, u in zip(pre_grad, feed_grad)]
        mid_grad = [v.astype(BF).astype(F32) for v in mid_grad]
        attn_grad = [norm_back(u, n, v, w.g1) for u, n, v in zip(mid_grad, n1, r1)]
        attn_low = [v.astype(BF) for v in attn_grad]
        back = [dot_nt(v, wout).astype(BF) for v in attn_low]
        down_total = dot_tn(act, joined(feed_low))
        up_total = dot_tn(mid, joined(pre_grad))
        out_total = dot_tn(ctx, joined(attn_low))
        up_sums = fold(joined(pre_grad).astype(F32))
        sums = [
            (V_G2, fold(joined([u * n for u, n in zip(up, n2)]))),
            (V_S2, fold(joined(up))),
            (V_DOWN, fold(joined(feed_low).astype(F32))),
            (V_UP, up_sums[:, :256]),
            (V_UP + 1, up_sums[:, 256:]),
            (V_G1, fold(joined([u * n for u, n in zip(mid_grad, n1)]))),
            (V_S1, fold(joined(mid_grad))),
            (V_OUT, fold(joined(attn_low).astype(F32))),
        ]
        for k, at in enumerate(chains):
            sum_grad[at, :] = attn_grad[k]
            ctx_grad[at, :] = back[k]
        total[AT_DOWN:AT_ALL, :] += down_total
        total[AT_UP : AT_UP + 256, :] += up_total[:, :256]
        total[AT_UP + 256 : AT_DOWN, :] += up_total[:, 256:]
        total[AT_OUT:AT_UP, :] += out_total
        for line, v in sums:
            small[line] += v

    plan.over_blocks(visit)
    clear(ctx_grad, rows_at(plan.blocks * TB, QB))


def attend_back(plan, most, kept, r):
    weights_low, ctx_grad, qkv_grad = r.s_probs, r.s_ctx_grad, r.s_qkv_grad
    key_sums, value_sums, keys_turned = r.s_key_sums, r.s_value_sums, r.s_turned
    masks = head_masks()
    scaling = (256 // HEADS) ** (-0.5)
    plan.over_blocks(lambda b: clear(qkv_grad, block(b)))

    def visit(d, n, length):
        offset, tile = plan.offset(d), plan.tile(d)
        width = n * QB
        keys_at = rows_at(offset, width)
        turn(kept.qkv[keys_at, 256:512], keys_turned, width)
        key_sums[:width, :] = jnp.zeros((width, 256), F32)
        value_sums[:width, :] = jnp.zeros((width, 256), F32)

        def some(first, count):
            chains = [(first + q, g) for q in range(count) for g in range(2)]
            cols = [slice(g * LANES, (g + 1) * LANES) for g in range(2)]
            values = [kept.qkv[keys_at, 512 + c.start : 512 + c.stop] for c in cols]
            turned = [keys_turned[c, :width] for c in cols]
            queries = [kept.qkv[rows_at(offset + q * QB, QB), cols[g]] for q, g in chains]
            grads = [ctx_grad[rows_at(offset + q * QB, QB), cols[g]] for q, g in chains]
            probs = []
            for q, g in chains:
                parts = [weights_low[tile + q * n + k, g] for k in range(n)]
                probs.append(jnp.concatenate(parts, axis=0) if n > 1 else parts[0])
            queries = [two_heads(v, masks) for v in queries]
            grads = [two_heads(v, masks) for v in grads]
            prob_grads = [dot_nt(values[g], v) for v, (_, g) in zip(grads, chains)]
            score_grads = []
            for low, v in zip(probs, prob_grads):
                full = low.astype(F32)
                inner = jnp.sum(full * v, axis=0, keepdims=True)
                score_grads.append((full * (v - inner)).astype(BF))
            query_grads = [dot(turned[g], v) for v, (_, g) in zip(score_grads, chains)]
            query_grads = [(turned_back(v) * scaling).astype(BF) for v in query_grads]
            for g in range(2):
                mine = [i for i, (_, own) in enumerate(chains) if own == g]
                rows = jnp.concatenate([queries[i] for i in mine], axis=0)
                sides = jnp.concatenate([score_grads[i] for i in mine], axis=1)
                key_sums[:width, cols[g]] += dot(sides, rows)
                rows = jnp.concatenate([grads[i] for i in mine], axis=0)
                sides = jnp.concatenate([probs[i] for i in mine], axis=1)
                value_sums[:width, cols[g]] += dot(sides, rows)
            for v, (q, g) in zip(query_grads, chains):
                qkv_grad[rows_at(offset + q * QB, QB), cols[g]] = v

        in_turns(n, some)
        qkv_grad[keys_at, 256:512] = key_sums[:width, :].astype(BF)
        qkv_grad[keys_at, 512:768] = value_sums[:width, :].astype(BF)

    plan.over_docs(most, visit)


def project_back(plan, kept, w, r, out):
    qkv_grad, sum_grad, total, small = r.s_qkv_grad, r.s_sum_grad, r.s_total, r.s_small

    def visit(b):
        rows = block(b)
        grad = qkv_grad[rows, :]
        sums = fold(grad.astype(F32))
        small[V_IN] += sums[:, :256]
        small[V_IN + 1] += sums[:, 512:]
        in_grad = dot_tn(kept.x[rows, :], grad)
        for k in range(3):
            total[256 * k : 256 * (k + 1), :] += in_grad[:, 256 * k : 256 * (k + 1)]
        hidden_grad = dot_nt(grad, w.win[...]) + sum_grad[rows, :]
        out[rows, :] = hidden_grad.astype(BF)

    plan.over_blocks(visit)


def first_kernel(layer, most, span, items, r):
    plan = Plan(r.plan, r.s_table, items)
    kept = SimpleNamespace(**{k: getattr(r, "s_" + k) for k in NAMES})
    w = layer_of(r, layer)

    def copy_block(k, b):
        there = getattr(r, "o_" + k).at[block(b)]
        return pltpu.make_async_copy(getattr(kept, k).at[block(b)], there, r.sems.at[NAMES.index(k)])

    def copy_probs(d, n):
        at = pl.ds(plan.tile(d), n * n)
        return pltpu.make_async_copy(r.s_probs.at[at], r.o_probs.at[at], r.sems.at[len(NAMES)])

    fill_window(r.s_window, r.own, r.left, r.right, span)
    pack(plan, most, r.s_window, kept.x)
    project(plan, kept, w.win, w.bin)
    early, late = NAMES[:2], NAMES[2:]
    plan.over_blocks(lambda b: [copy_block(k, b).start() for k in early])
    attend(plan, most, kept, r.s_probs, r.s_turned)
    plan.over_docs(most, lambda d, n, length: copy_probs(d, n).start())
    feed(plan, kept, w, r.o_next, lambda b: [copy_block(k, b).start() for k in late])
    plan.over_blocks(lambda b: [copy_block(k, b).wait() for k in NAMES])
    plan.over_docs(most, lambda d, n, length: copy_probs(d, n).wait())


def second_kernel(layer, most, span, items, r):
    plan = Plan(r.plan, r.s_table, items)
    kept = SimpleNamespace(**{k: getattr(r, "s_" + k) for k in NAMES[1:]}, x=r.x)
    w = layer_of(r, layer)
    project(plan, kept, w.win, w.bin)
    attend(plan, most, kept, r.s_probs, r.s_turned)
    feed(plan, kept, w, r.s_rows)
    unpack(plan, most, r.s_rows, r.s_window, r.o_own, r.o_left, r.o_right, span)
    fill_window(r.s_window, r.own, r.left, r.right, span)
    pack(plan, most, r.s_window, r.s_rows)
    clear_totals(r)
    feed_back(plan, kept, w, r.s_rows, r)
    attend_back(plan, most, kept, r)
    project_back(plan, kept, w, r, r.o_next)
    send_pieces(r)
    r.o_small[...] = r.s_small[...].sum(1)


def third_kernel(layer, most, span, items, r):
    plan = Plan(r.plan, r.s_table, items)
    kept = SimpleNamespace(**{k: getattr(r, "s_" + k) for k in NAMES})
    w = layer_of(r, layer)

    def copy_block(k, b):
        given = getattr(r, "i_" + k).at[block(b)]
        return pltpu.make_async_copy(given, getattr(kept, k).at[block(b)], r.sems.at[NAMES.index(k)])

    def copy_probs(d, n):
        at = pl.ds(plan.tile(d), n * n)
        return pltpu.make_async_copy(r.i_probs.at[at], r.s_probs.at[at], r.sems.at[len(NAMES)])

    early, late = NAMES[2:], NAMES[:2]
    plan.over_blocks(lambda b: [copy_block(k, b).start() for k in early])
    plan.over_docs(most, lambda d, n, length: copy_probs(d, n).start())
    plan.over_blocks(lambda b: [copy_block(k, b).start() for k in late])
    clear_totals(r)
    plan.over_blocks(lambda b: [copy_block(k, b).wait() for k in early])
    feed_back(plan, kept, w, r.rows, r)
    plan.over_docs(most, lambda d, n, length: copy_probs(d, n).wait())
    plan.over_blocks(lambda b: [copy_block(k, b).wait() for k in late])
    clear(kept.qkv, rows_at(plan.blocks * TB, QB))
    attend_back(plan, most, kept, r)
    project_back(plan, kept, w, r, r.s_rows)
    unpack(plan, most, r.s_rows, r.s_window, r.o_own, r.o_left, r.o_right, span)
    send_pieces(r)
    send_small(r)


def layer_of(r, layer):
    w = SimpleNamespace(win=r.win, wout=r.wout, wup=r.wup, wdown=r.wdown)
    w = SimpleNamespace(**{k: v.at[layer] for k, v in vars(w).items()})
    vectors = dict(bin=r.bin, bout=r.bout, g1=r.g1, s1=r.s1, bup=r.bup, bdown=r.bdown, g2=r.g2, s2=r.s2)
    return SimpleNamespace(**vars(w), **{k: v[layer : layer + 1, :] for k, v in vectors.items()})


def clear_totals(r):
    r.s_total[...] = jnp.zeros(r.s_total.shape, F32)
    r.s_small[...] = jnp.zeros(r.s_small.shape, F32)


def send_pieces(r):
    count = 2 * r.o_keep.shape[0]
    rows = AT_ALL // count
    for p in range(count):
        out = r.o_keep if p < count // 2 else r.o_send
        piece = lax.bitwise_xor(jnp.int32(p), r.self[0])
        at = pl.ds(pl.multiple_of(piece * rows, rows), rows)
        out[p % (count // 2), 0:rows, :] = r.s_total[at, :].astype(BF)


def send_small(r):
    count = 2 * r.o_keep.shape[0]
    rows = AT_ALL // count
    extra = r.o_keep.shape[1] - rows
    share = 2 * V_ALL // count
    r.s_both[0:V_ALL, :] = r.s_small[...].sum(1)
    r.s_both[V_ALL : 2 * V_ALL, :] = r.small[...]
    for j in range(count):
        own = r.s_both[j * share : (j + 1) * share, :]
        r.s_spread[j] = jnp.concatenate([own, jnp.zeros((extra - share, own.shape[1]), F32)], axis=0)
    for p in range(count):
        out = r.o_keep if p < count // 2 else r.o_send
        piece = lax.bitwise_xor(jnp.int32(p), r.self[0])
        out[p % (count // 2), rows : rows + extra, :] = r.s_spread[piece].astype(BF)


def last_kernel(r):
    half = r.keep0.shape[0]
    count = 2 * half
    rows = AT_ALL // count
    share = 2 * V_ALL // count
    for layer, (keep, got) in enumerate(((r.keep0, r.got0), (r.keep1, r.got1))):
        for p in range(count):
            piece = lax.bitwise_xor(jnp.int32(p), r.self[layer])
            source = keep if p < half else got
            r.s_pieces[layer, piece, 0 : keep.shape[1], :] = source[p % half]
    for layer in range(2):
        for j in range(count):
            value = r.s_pieces[layer, j, 0:rows, :].astype(F32)
            at = j * rows
            for low, high, out in (
                (0, AT_OUT, r.o_in),
                (AT_OUT, AT_UP, r.o_out),
                (AT_UP, AT_DOWN, r.o_up),
                (AT_DOWN, AT_ALL, r.o_down),
            ):
                if low <= at < high:
                    tall = out.shape[1]
                    line, col = (at - low) % tall, (at - low) // tall * 256
                    out[layer, line : line + rows, col : col + 256] = value
    for j in range(count):
        tail = r.s_pieces[0, j, rows : rows + 16, :].astype(F32)
        r.s_both[j * share : (j + 1) * share, :] = tail[0:share]
    for layer in range(2):
        at = layer * V_ALL
        here = pl.ds(layer, 1)

        def line(k):
            return r.s_both[at + k : at + k + 1, :]

        r.o_bin[here, :] = jnp.concatenate([line(V_IN), line(V_IN + 1)], axis=1)
        r.o_bout[here, :] = line(V_OUT)
        r.o_g1[here, :] = line(V_G1)
        r.o_s1[here, :] = line(V_S1)
        r.o_bup[here, :] = jnp.concatenate([line(V_UP), line(V_UP + 1)], axis=1)
        r.o_bdown[here, :] = line(V_DOWN)
        r.o_g2[here, :] = line(V_G2)
        r.o_s2[here, :] = line(V_S2)


def call(kernel, consts, inputs, outputs, scratch, flops):
    names = tuple(inputs) + tuple(outputs) + tuple(scratch)

    def run(*refs):
        kernel(*consts, SimpleNamespace(**dict(zip(names, refs))))

    got = pl.pallas_call(
        run,
        out_shape=[jax.ShapeDtypeStruct(s, d) for s, d, _ in outputs.values()],
        in_specs=[spec for _, spec in inputs.values()],
        out_specs=[spec for _, _, spec in outputs.values()],
        scratch_shapes=list(scratch.values()),
        compiler_params=pltpu.CompilerParams(vmem_limit_bytes=VMEM_LIMIT),
        cost_estimate=pl.CostEstimate(flops=flops, bytes_accessed=8 << 20, transcendentals=0),
    )(*[a for a, _ in inputs.values()])
    return SimpleNamespace(**dict(zip(outputs, got)))


def make_plan(segments, place, section_count):
    row_count, length = segments.shape
    whole = length // section_count
    half = whole // 2
    span = 2 * whole + 2 * QB
    ids = jnp.arange(DOCS + 1, dtype=jnp.int32)
    starts = jnp.sum((segments[:, None, :] < ids[None, :, None]).astype(jnp.int32), axis=2)
    targets = jnp.arange(1, section_count, dtype=jnp.int32) * whole
    away = starts[None] - targets[:, None, None]
    far = (jnp.abs(away) > half).astype(jnp.int32) * (1 << 16)
    base = DOCS + 1
    if row_count == 2:
        cost = jnp.abs(away[:, 0, :, None] + away[:, 1, None, :])
        cost = cost + far[:, 0, :, None] + far[:, 1, None, :]
        code = ids[:, None] * base + ids[None, :]
        best = jnp.min(cost * (base * base) + code[None], axis=(1, 2)) % (base * base)
        chosen = jnp.stack([best // base, best % base], axis=1)
    else:
        chosen = jnp.min((jnp.abs(away) + far) * base + ids, axis=2) % base
    first = jnp.zeros((1, row_count), jnp.int32)
    cuts = jnp.concatenate([first, chosen, first + DOCS], axis=0)
    sections = jnp.arange(section_count + 1)[:, None]
    low = jnp.sum(jnp.where(sections == place, cuts, 0), axis=0)[:, None]
    high = jnp.sum(jnp.where(sections == place + 1, cuts, 0), axis=0)[:, None]
    here = (ids[None, :DOCS] >= low) & (ids[None, :DOCS] < high)
    lengths = jnp.where(here, starts[:, 1:] - starts[:, :-1], 0)
    begins = starts[:, :-1] - place * whole + half
    begins = begins + jnp.arange(row_count, dtype=jnp.int32)[:, None] * span
    begins = jnp.where(here, begins, 0)
    return jnp.stack([begins, lengths]).reshape(-1)


def swapped(low_part, high_part, place, odd):
    count = lax.axis_size("pipe")
    pairs = [(i, i + 1) for i in range(odd, count - 1, 2)]
    upper = lax.rem(place + odd, 2) == 1
    sent = jnp.where(upper, low_part, high_part)
    got = lax.ppermute(sent, "pipe", [p for i, j in pairs for p in ((i, j), (j, i))])
    return upper, got


def halo(low_part, high_part, place):
    even_upper, even = swapped(low_part, high_part, place, 0)
    odd_upper, odd = swapped(low_part, high_part, place, 1)
    return jnp.where(even_upper, even, odd), jnp.where(odd_upper, even, odd)


def orders():
    found = []
    for axis in ("dp", "pipe"):
        stride = 1
        while stride < lax.axis_size(axis):
            found.append((axis, stride))
            stride *= 2
    other = list(found)
    if len(found) > 2:
        other[1], other[2] = found[2], found[1]
    return found, other


SPLIT = 4


def self_index(order):
    index = jnp.int32(0)
    for axis, stride in order[:SPLIT]:
        index = 2 * index + lax.rem(lax.div(lax.axis_index(axis), stride), 2)
    return index.astype(jnp.int32)


def exchange(value, axis, stride):
    count = lax.axis_size(axis)
    return lax.ppermute(value, axis, [(i, i ^ stride) for i in range(count)])


def added(a, b):
    return (a.astype(F32) + b.astype(F32)).astype(BF)


def sum_steps(keep, send, order):
    total = None
    for k, (axis, stride) in enumerate(order[:SPLIT]):
        got = exchange(send, axis, stride)
        yield None
        half = keep.shape[0] // 2
        if half:
            send, keep = added(keep[half:], got[half:]), added(keep[:half], got[:half])
        else:
            total = added(keep, got)
    for axis, stride in order[SPLIT:]:
        got = exchange(total, axis, stride)
        yield None
        total = added(total, got)
    for k, (axis, stride) in enumerate(reversed(order[:SPLIT])):
        got = exchange(total, axis, stride)
        yield (total, got)
        total = jnp.concatenate([total, got], axis=0)


def body(
    tokens,
    segments,
    cotangent,
    attention_in,
    attention_in_bias,
    attention_out,
    attention_out_bias,
    attention_gain,
    attention_shift,
    expand_weight,
    expand_bias,
    contract_weight,
    contract_bias,
    feed_gain,
    feed_shift,
):
    section_count = lax.axis_size("pipe")
    place = lax.axis_index("pipe").astype(jnp.int32)
    row_count, whole, features = tokens.shape
    half = whole // 2
    span = 2 * whole + 2 * QB
    items = row_count * DOCS
    most = whole // QB
    cap = row_count * 2 * whole + items * 16 + QB
    cap = (cap + TB - 1) // TB * TB
    tiles = row_count * 42
    vmem = pl.BlockSpec(memory_space=pltpu.VMEM)
    smem = pl.BlockSpec(memory_space=pltpu.SMEM)
    anywhere = pl.BlockSpec(memory_space=pl.ANY)
    weights = dict(
        win=attention_in,
        bin=attention_in_bias,
        wout=attention_out,
        bout=attention_out_bias,
        g1=attention_gain,
        s1=attention_shift,
        wup=expand_weight,
        bup=expand_bias,
        wdown=contract_weight,
        bdown=contract_bias,
        g2=feed_gain,
        s2=feed_shift,
    )
    weights = {k: (v, vmem) for k, v in weights.items()}

    def with_halo(value):
        left, right = halo(value[:, :half], value[:, half:], place)
        return dict(own=(value, vmem), left=(left, vmem), right=(right, vmem))

    def placed(got):
        low, high = halo(got.o_left, got.o_right, place)
        return got.o_own + jnp.concatenate([low, high], axis=1)

    order0, order1 = orders()
    selves = [self_index(order0), self_index(order1)]
    pieces = 1 << SPLIT
    token_rows = with_halo(tokens)
    plan = dict(plan=(make_plan(segments, place, section_count), smem))
    kept_scratch = {"s_" + k: pltpu.VMEM((cap, c), t) for k, (c, t) in KEPT.items()}
    probs_shape = (tiles, 2, QB, 2 * QB)
    kept_scratch.update(
        s_probs=pltpu.VMEM(probs_shape, BF),
        s_window=pltpu.VMEM((row_count * span, features), BF),
        s_turned=pltpu.VMEM((features, whole), BF),
        s_table=pltpu.SMEM((2 * items,), jnp.int32),
    )
    sems = dict(sems=pltpu.SemaphoreType.DMA((len(NAMES) + 1,)))
    back_scratch = dict(
        s_rows=pltpu.VMEM((cap, features), BF),
        s_total=pltpu.VMEM((AT_ALL, features), F32),
        s_small=pltpu.VMEM((V_ALL, 8, features), F32),
        s_ctx_grad=pltpu.VMEM((cap, features), BF),
        s_sum_grad=pltpu.VMEM((cap, features), F32),
        s_qkv_grad=pltpu.VMEM((cap, 3 * features), BF),
        s_key_sums=pltpu.VMEM((whole, features), F32),
        s_value_sums=pltpu.VMEM((whole, features), F32),
    )
    window_out = dict(
        o_own=((row_count, whole, features), BF, vmem),
        o_left=((row_count, half, features), BF, vmem),
        o_right=((row_count, half, features), BF, vmem),
    )

    def pieces_out(extra):
        shape = (pieces // 2, AT_ALL // pieces + extra, features)
        return dict(o_keep=(shape, BF, vmem), o_send=(shape, BF, vmem))

    next_out = dict(o_next=((cap, features), BF, vmem))
    kept_out = {"o_" + k: ((cap, c), t, anywhere) for k, (c, t) in KEPT.items()}
    kept_out.update(o_probs=(probs_shape, BF, anywhere))

    first = call(
        first_kernel,
        (0, most, span, items),
        plan | token_rows | weights,
        kept_out | next_out,
        kept_scratch | sems,
        12 << 30,
    )
    cotangent_rows = with_halo(cotangent)
    second = call(
        second_kernel,
        (1, most, span, items),
        plan
        | cotangent_rows
        | dict(x=(first.o_next, vmem), self=(selves[1].reshape(1), smem))
        | weights,
        window_out
        | pieces_out(0)
        | next_out
        | dict(o_small=((V_ALL, features), F32, vmem)),
        {k: v for k, v in kept_scratch.items() if k != "s_x"} | back_scratch,
        36 << 30,
    )
    kept_in = {"i_" + k: (getattr(first, "o_" + k), anywhere) for k in NAMES + ("probs",)}
    third = call(
        third_kernel,
        (0, most, span, items),
        plan
        | kept_in
        | dict(
            rows=(second.o_next, vmem),
            small=(second.o_small, vmem),
            self=(selves[0].reshape(1), smem),
        )
        | weights,
        window_out | pieces_out(16),
        kept_scratch
        | back_scratch
        | sems
        | dict(
            s_both=pltpu.VMEM((2 * V_ALL, features), F32),
            s_spread=pltpu.VMEM((pieces, 16, features), F32),
        ),
        24 << 30,
    )
    layer_output = placed(second)
    input_grad = placed(third)
    sums = [sum_steps(third.o_keep, third.o_send, order0)]
    sums.append(sum_steps(second.o_keep, second.o_send, order1))
    for ends in zip(*sums):
        pass
    layers = attention_in.shape[0]

    def out(*shape):
        return ((layers,) + shape, F32, vmem)

    vector = out(features)
    result = call(
        last_kernel,
        (),
        dict(
            self=(jnp.stack(selves), smem),
            keep0=(ends[0][0], vmem),
            got0=(ends[0][1], vmem),
            keep1=(ends[1][0], vmem),
            got1=(ends[1][1], vmem),
        ),
        dict(
            o_in=out(features, 3 * features),
            o_bin=out(2 * features),
            o_out=out(features, features),
            o_bout=vector,
            o_g1=vector,
            o_s1=vector,
            o_up=out(features, 2 * features),
            o_bup=out(2 * features),
            o_down=out(2 * features, features),
            o_bdown=vector,
            o_g2=vector,
            o_s2=vector,
        ),
        dict(
            s_pieces=pltpu.VMEM((2, pieces, AT_ALL // pieces + 16, features), BF),
            s_both=pltpu.VMEM((2 * V_ALL, features), F32),
        ),
        1 << 30,
    )
    return (layer_output, input_grad) + tuple(vars(result).values())


def solution(mesh):
    rows = P("dp", "pipe", None)
    return jax.shard_map(
        body,
        mesh=mesh,
        in_specs=(rows, P("dp", None), rows) + (P(),) * 12,
        out_specs=(rows, rows) + (P(),) * 12,
        check_vma=False,
    )
```

```python
from types import SimpleNamespace

import jax
import jax.numpy as jnp
from jax import lax
from jax.experimental import pallas as pl
from jax.experimental.pallas import tpu as pltpu
from jax.sharding import PartitionSpec as P

HEADS = 4
EPSILON = 1e-12
MASKED = -1e30
DOCS = 8
REACH = 320
TB = 512
MOST_BLOCKS = 8
QB = 128
TURNS = (1, 2, 3, 4)
LANES = 128

BF = jnp.bfloat16
F32 = jnp.float32

KEPT = dict(
    x=(256, BF),
    qkv=(768, BF),
    ctx=(256, BF),
    n1=(256, BF),
    r1=(128, F32),
    mid=(256, BF),
    act=(512, BF),
    slope=(512, BF),
    n2=(256, BF),
    r2=(128, F32),
)
NAMES = tuple(KEPT)


def dot(a, b):
    return jnp.dot(a, b, preferred_element_type=F32)


def dot_nt(a, b):
    return lax.dot_general(a, b, (((1,), (1,)), ((), ())), preferred_element_type=F32)


def dot_tn(a, b):
    return lax.dot_general(a, b, (((0,), (0,)), ((), ())), preferred_element_type=F32)


def fold(v):
    return v.reshape(-1, 8, v.shape[-1]).sum(0)


def rows_at(start, count):
    return pl.ds(pl.multiple_of(start, 16), count)


class Plan:
    def __init__(self, r, items):
        self.begins, self.lengths, self.table, self.items = r.begins, r.lengths, r.s_table, items
        table = r.s_table

        def one(d, carry):
            offset, tile = carry
            table[d] = offset
            table[items + d] = tile
            length = self.length(d)
            count = lax.shift_right_logical(length + (QB - 1), 7)
            return offset + lax.bitwise_and(length + 15, -16), tile + count * count

        total, _ = lax.fori_loop(0, items, one, (jnp.int32(0), jnp.int32(0)))
        halves = lax.shift_right_logical(total + (TB // 2 - 1), 8)
        self.blocks = lax.shift_right_logical(halves, 1)
        self.odd = lax.bitwise_and(halves, 1)
        self.end = halves * (TB // 2)

    def start(self, d):
        return self.begins[lax.shift_right_logical(d, 3), lax.bitwise_and(d, DOCS - 1)]

    def length(self, d):
        return self.lengths[lax.shift_right_logical(d, 3), lax.bitwise_and(d, DOCS - 1)]

    def offset(self, d):
        return self.table[d]

    def tile(self, d):
        return self.table[self.items + d]

    def over_docs(self, most, visit):
        def one(d, _):
            length = self.length(d)

            @pl.when(length > 0)
            def _():
                blocks = lax.shift_right_logical(length + (QB - 1), 7)
                for n in range(1, most + 1):

                    @pl.when(blocks == n)
                    def _():
                        visit(d, n, length)

            return 0

        lax.fori_loop(0, self.items, one, 0)

    def over_blocks(self, visit):
        def one(b, _):
            visit(b, rows_at(b * TB, TB))
            return 0

        lax.fori_loop(0, self.blocks, one, 0)

        @pl.when(self.odd == 1)
        def _():
            visit(self.blocks, rows_at(self.blocks * TB, TB // 2))


def window_copies(win, span, own, low, high, sems, out):
    reach, whole = low.shape[1], own.shape[1]
    found = []
    for k in range(own.shape[0]):
        at = k * span
        for far, count in ((low, reach), (own, whole), (high, reach)):
            ends = (win.at[pl.ds(at, count)], far.at[k])
            found.append(pltpu.make_async_copy(*(ends if out else ends[::-1]), sems.at[len(found)]))
            at += count
    return found


def with_halos(r, win, span, act):
    upper = lax.bitwise_and(r.place[0], 1)
    for side in range(2):

        @pl.when(upper == 1 - side)
        def _():
            low, high = (r.odd, r.even) if side else (r.even, r.odd)
            act(window_copies(win, span, r.own, low, high, r.window_sems, False))


def clear_between(win, span, count):
    used = span - 2 * QB
    for k in range(count):
        clear(win, pl.ds(k * span + used, 2 * QB))


SPREAD = QB + 16


def pack(plan, most, win, dst):
    plan.over_blocks(lambda b, rows: clear(dst, rows))

    def visit(d, n, length):
        start, offset = plan.start(d), plan.offset(d)
        shift = lax.bitwise_and(start, 15)
        row = lax.broadcasted_iota(jnp.int32, (QB, SPREAD), 0)
        col = lax.broadcasted_iota(jnp.int32, (QB, SPREAD), 1)
        taken = col == row + shift
        kept = jnp.where(taken & (row < length - (n - 1) * QB), 1.0, 0.0).astype(BF)
        taken = jnp.where(taken, 1.0, 0.0).astype(BF)
        rows = [win[rows_at(start - shift + q * QB, SPREAD), :] for q in range(n)]
        picked = [dot(taken if q < n - 1 else kept, v).astype(BF) for q, v in enumerate(rows)]
        for q, v in enumerate(picked):
            dst[rows_at(offset + q * QB, QB), :] = v

    plan.over_docs(most, visit)


def unpack(plan, most, src, win, r, span, which):
    win[...] = jnp.zeros(win.shape, BF)
    clear(src, rows_at(plan.end, QB))

    def visit(d, n, length):
        start, offset = plan.start(d), plan.offset(d)
        shift = lax.bitwise_and(start, 15)
        row = lax.broadcasted_iota(jnp.int32, (SPREAD, QB), 0)
        col = lax.broadcasted_iota(jnp.int32, (SPREAD, QB), 1)
        taken = row == col + shift
        kept = jnp.where(taken & (col < length - (n - 1) * QB), 1.0, 0.0).astype(BF)
        taken = jnp.where(taken, 1.0, 0.0).astype(BF)
        rows = [src[rows_at(offset + q * QB, QB), :] for q in range(n)]
        placed = [dot(taken if q < n - 1 else kept, v) for q, v in enumerate(rows)]
        for q, v in enumerate(placed):
            at = rows_at(start - shift + q * QB, SPREAD)
            win[at, :] = (win[at, :].astype(F32) + v).astype(BF)

    plan.over_docs(most, visit)
    ends = [v.at[which] for v in (r.o_own, r.o_left, r.o_right)]
    found = window_copies(win, span, *ends, r.window_sems.at[which], True)
    started(found)
    return found


def clear(ref, rows):
    ref[rows, :] = jnp.zeros((rows.size, ref.shape[1]), ref.dtype)


def head_masks():
    lane = lax.broadcasted_iota(jnp.int32, (1, LANES), 1)
    low = (lane < LANES // 2).astype(F32)
    return low.astype(BF), (1.0 - low).astype(BF)


def two_heads(v, masks):
    return jnp.concatenate([v * masks[0], v * masks[1]], axis=0)


def turned_back(v):
    row = lax.broadcasted_iota(jnp.int32, (LANES, QB), 0)
    return jnp.where(row < LANES // 2, v[:, :QB], v[:, QB:]).T


def turn(src, dst, width):
    for k in range(width // LANES):
        at = slice(k * LANES, (k + 1) * LANES)
        for g in range(2):
            here = slice(g * LANES, (g + 1) * LANES)
            dst[here, at] = src[at, here].T


def project(plan, kept, weight, bias, before=None):
    scaling = (weight.shape[0] // HEADS) ** (-0.5)

    def visit(b, rows):
        if before is not None:
            before(b, rows)
        y = dot(kept.x[rows, :], weight[...])
        queries = (y[:, 0:256] + bias[:, 0:256]).astype(BF)
        kept.qkv[rows, 0:256] = queries * jnp.asarray(scaling, BF)
        kept.qkv[rows, 256:512] = y[:, 256:512].astype(BF)
        kept.qkv[rows, 512:768] = (y[:, 512:768] + bias[:, 256:512]).astype(BF)
        clear(kept.ctx, rows)

    plan.over_blocks(visit)
    clear(kept.qkv, rows_at(plan.end, QB))


def in_turns(count, some):
    step = TURNS[count - 1]
    if step == count:
        some(0, count)
        return

    def one(k, _):
        some(k * step, step)
        return 0

    lax.fori_loop(0, count // step, one, 0)


def attend(plan, most, kept, weights_low, values_turned):
    masks = head_masks()

    def visit(d, n, length):
        offset, tile = plan.offset(d), plan.tile(d)
        width = n * QB
        keys_at = rows_at(offset, width)
        turn(kept.qkv[keys_at, 512:768], values_turned, width)

        def some(first, count):
            column = lax.broadcasted_iota(jnp.int32, (1, 2 * QB), 1)
            column = lax.bitwise_and(column, QB - 1)
            row = lax.broadcasted_iota(jnp.int32, (QB, 2 * QB), 0)
            inside = row < length - (width - QB)
            chains = [(first + q, g) for q in range(count) for g in range(2)]
            cols = [slice(g * LANES, (g + 1) * LANES) for g in range(2)]
            keys = [kept.qkv[keys_at, 256 + c.start : 256 + c.stop] for c in cols]
            turned = [values_turned[c, :width] for c in cols]
            queries = [kept.qkv[rows_at(offset + q * QB, QB), cols[g]] for q, g in chains]
            queries = [two_heads(v, masks) for v in queries]
            scores = [dot_nt(keys[g], v) for v, (_, g) in zip(queries, chains)]
            probs = []
            for v, (q, g) in zip(scores, chains):
                last = jnp.where(inside, v[width - QB :, :], MASKED)
                v = jnp.concatenate([v[: width - QB, :], last], axis=0) if n > 1 else last
                raised = jnp.exp(v - jnp.max(v, axis=0, keepdims=True))
                total = jnp.sum(raised, axis=0, keepdims=True)
                share = jnp.where(column + q * QB < length, 1.0 / total, 0.0)
                probs.append((raised * share).astype(BF))
            contexts = [dot(turned[g], v) for v, (_, g) in zip(probs, chains)]
            contexts = [turned_back(v).astype(BF) for v in contexts]
            for v, context, (q, g) in zip(probs, contexts, chains):
                kept.ctx[rows_at(offset + q * QB, QB), cols[g]] = context
                for k in range(n):
                    weights_low[tile + q * n + k, g] = v[k * QB : (k + 1) * QB, :]

        in_turns(n, some)

    plan.over_docs(most, visit)


def normal(v):
    centred = v - jnp.mean(v, axis=1, keepdims=True)
    spread = jnp.mean(centred * centred, axis=1, keepdims=True)
    rate = lax.rsqrt(spread + EPSILON)
    return centred * rate, rate


def parts_of(rows, count):
    step = rows.size // count
    return [rows_at(rows.start + k * step, step) for k in range(count)]


def feed(plan, kept, w, out, each=None):
    def visit(b, rows):
        chains = parts_of(rows, 1)
        wout, wup, wdown = w.wout[...], w.wup[...], w.wdown[...]
        x = [kept.x[at, :] for at in chains]
        ctx = [kept.ctx[at, :] for at in chains]
        attn_sum = [u.astype(F32) + dot(v, wout) + w.bout for u, v in zip(x, ctx)]
        first = [normal(v) for v in attn_sum]
        mid_low = [(n * w.g1 + w.s1).astype(BF) for n, _ in first]
        pre_up = [dot(v, wup) + w.bup for v in mid_low]
        share = [0.5 + 0.5 * lax.erf(v * (0.5**0.5)) for v in pre_up]
        active = [(v * p).astype(BF) for v, p in zip(pre_up, share)]
        density = [jnp.exp(v * v * -0.5) * 0.3989422804014327 for v in pre_up]
        slope = [(p + v * q).astype(BF) for v, p, q in zip(pre_up, share, density)]
        feed_sum = [u.astype(F32) + dot(v, wdown) + w.bdown for u, v in zip(mid_low, active)]
        second = [normal(v) for v in feed_sum]
        for k, at in enumerate(chains):
            kept.n1[at, :] = first[k][0].astype(BF)
            kept.r1[at, :] = jnp.broadcast_to(first[k][1], (at.size, LANES))
            kept.mid[at, :] = mid_low[k]
            kept.act[at, :] = active[k]
            kept.slope[at, :] = slope[k]
            kept.n2[at, :] = second[k][0].astype(BF)
            kept.r2[at, :] = jnp.broadcast_to(second[k][1], (at.size, LANES))
            out[at, :] = (second[k][0] * w.g2 + w.s2).astype(BF)
        if each is not None:
            each(b, rows)

    plan.over_blocks(visit)


AT_OUT, AT_UP, AT_DOWN, AT_ALL = 768, 1024, 1536, 2048
V_IN, V_OUT, V_G1, V_S1, V_UP, V_DOWN, V_G2, V_S2, V_ALL = 0, 2, 3, 4, 5, 7, 8, 9, 16


def norm_back(upstream, n, rate, gain):
    e = upstream * gain
    inner = jnp.mean(e * n, axis=1, keepdims=True)
    return (e - jnp.mean(e, axis=1, keepdims=True) - n * inner) * rate


def doubled(v):
    return jnp.concatenate([v, v], axis=1)


def joined(values):
    return jnp.concatenate(values, axis=0) if len(values) > 1 else values[0]


def feed_back(plan, kept, w, upstream, r, before=None):
    total, small, ctx_grad, sum_grad = r.s_total, r.s_small, r.s_ctx_grad, r.s_sum_grad

    def visit(b, rows):
        if before is not None:
            before(b, rows)
        chains = parts_of(rows, 2)
        wout, wup, wdown = w.wout[...], w.wup[...], w.wdown[...]
        up = [upstream[at, :].astype(F32) for at in chains]
        n2 = [kept.n2[at, :].astype(F32) for at in chains]
        r2 = [doubled(kept.r2[at, :]) for at in chains]
        slope = [kept.slope[at, :] for at in chains]
        n1 = [kept.n1[at, :].astype(F32) for at in chains]
        r1 = [doubled(kept.r1[at, :]) for at in chains]
        act, mid, ctx = kept.act[rows, :], kept.mid[rows, :], kept.ctx[rows, :]
        feed_grad = [norm_back(u, n, v, w.g2) for u, n, v in zip(up, n2, r2)]
        feed_low = [v.astype(BF) for v in feed_grad]
        active_grad = [dot_nt(v, wdown) for v in feed_low]
        pre_grad = [(v * p.astype(F32)).astype(BF) for v, p in zip(active_grad, slope)]
        mid_grad = [dot_nt(v, wup) + u for v, u in zip(pre_grad, feed_grad)]
        mid_grad = [v.astype(BF).astype(F32) for v in mid_grad]
        attn_grad = [norm_back(u, n, v, w.g1) for u, n, v in zip(mid_grad, n1, r1)]
        attn_low = [v.astype(BF) for v in attn_grad]
        back = [dot_nt(v, wout).astype(BF) for v in attn_low]
        down_total = dot_tn(act, joined(feed_low))
        up_total = dot_tn(mid, joined(pre_grad))
        out_total = dot_tn(ctx, joined(attn_low))
        up_sums = fold(joined(pre_grad).astype(F32))
        sums = [
            (V_G2, fold(joined([u * n for u, n in zip(up, n2)]))),
            (V_S2, fold(joined(up))),
            (V_DOWN, fold(joined(feed_low).astype(F32))),
            (V_UP, up_sums[:, :256]),
            (V_UP + 1, up_sums[:, 256:]),
            (V_G1, fold(joined([u * n for u, n in zip(mid_grad, n1)]))),
            (V_S1, fold(joined(mid_grad))),
            (V_OUT, fold(joined(attn_low).astype(F32))),
        ]
        for k, at in enumerate(chains):
            sum_grad[at, :] = attn_grad[k]
            ctx_grad[at, :] = back[k]
        total[AT_DOWN:AT_ALL, :] += down_total
        total[AT_UP : AT_UP + 256, :] += up_total[:, :256]
        total[AT_UP + 256 : AT_DOWN, :] += up_total[:, 256:]
        total[AT_OUT:AT_UP, :] += out_total
        for line, v in sums:
            small[line] += v

    plan.over_blocks(visit)
    clear(ctx_grad, rows_at(plan.end, QB))


def attend_back(plan, most, kept, r):
    weights_low, ctx_grad, qkv_grad = r.s_probs, r.s_ctx_grad, r.s_qkv_grad
    key_sums, value_sums, keys_turned = r.s_key_sums, r.s_value_sums, r.s_turned
    masks = head_masks()
    scaling = (256 // HEADS) ** (-0.5)
    plan.over_blocks(lambda b, rows: clear(qkv_grad, rows))

    def visit(d, n, length):
        offset, tile = plan.offset(d), plan.tile(d)
        width = n * QB
        keys_at = rows_at(offset, width)
        turn(kept.qkv[keys_at, 256:512], keys_turned, width)
        key_sums[:width, :] = jnp.zeros((width, 256), F32)
        value_sums[:width, :] = jnp.zeros((width, 256), F32)

        def some(first, count):
            chains = [(first + q, g) for q in range(count) for g in range(2)]
            cols = [slice(g * LANES, (g + 1) * LANES) for g in range(2)]
            values = [kept.qkv[keys_at, 512 + c.start : 512 + c.stop] for c in cols]
            turned = [keys_turned[c, :width] for c in cols]
            queries = [kept.qkv[rows_at(offset + q * QB, QB), cols[g]] for q, g in chains]
            grads = [ctx_grad[rows_at(offset + q * QB, QB), cols[g]] for q, g in chains]
            probs = []
            for q, g in chains:
                parts = [weights_low[tile + q * n + k, g] for k in range(n)]
                probs.append(jnp.concatenate(parts, axis=0) if n > 1 else parts[0])
            queries = [two_heads(v, masks) for v in queries]
            grads = [two_heads(v, masks) for v in grads]
            prob_grads = [dot_nt(values[g], v) for v, (_, g) in zip(grads, chains)]
            score_grads = []
            for low, v in zip(probs, prob_grads):
                full = low.astype(F32)
                inner = jnp.sum(full * v, axis=0, keepdims=True)
                score_grads.append((full * (v - inner)).astype(BF))
            query_grads = [dot(turned[g], v) for v, (_, g) in zip(score_grads, chains)]
            query_grads = [(turned_back(v) * scaling).astype(BF) for v in query_grads]
            for g in range(2):
                mine = [i for i, (_, own) in enumerate(chains) if own == g]
                rows = jnp.concatenate([queries[i] for i in mine], axis=0)
                sides = jnp.concatenate([score_grads[i] for i in mine], axis=1)
                key_sums[:width, cols[g]] += dot(sides, rows)
                rows = jnp.concatenate([grads[i] for i in mine], axis=0)
                sides = jnp.concatenate([probs[i] for i in mine], axis=1)
                value_sums[:width, cols[g]] += dot(sides, rows)
            for v, (q, g) in zip(query_grads, chains):
                qkv_grad[rows_at(offset + q * QB, QB), cols[g]] = v

        in_turns(n, some)
        qkv_grad[keys_at, 256:512] = key_sums[:width, :].astype(BF)
        qkv_grad[keys_at, 512:768] = value_sums[:width, :].astype(BF)

    plan.over_docs(most, visit)


def project_back(plan, kept, w, r, out, after=None):
    qkv_grad, sum_grad, total, small = r.s_qkv_grad, r.s_sum_grad, r.s_total, r.s_small

    def visit(b, rows):
        grad = qkv_grad[rows, :]
        sums = fold(grad.astype(F32))
        small[V_IN] += sums[:, :256]
        small[V_IN + 1] += sums[:, 512:]
        in_grad = dot_tn(kept.x[rows, :], grad)
        for k in range(3):
            total[256 * k : 256 * (k + 1), :] += in_grad[:, 256 * k : 256 * (k + 1)]
        hidden_grad = dot_nt(grad, w.win[...]) + sum_grad[rows, :]
        out[rows, :] = hidden_grad.astype(BF)
        if after is not None:
            after(b, rows)

    plan.over_blocks(visit)


def copies(r, kept, plan, out):
    def one(name, rows, sem):
        near = getattr(r if name == "probs" else kept, "s_probs" if name == "probs" else name)
        far = getattr(r, ("o_" if out else "i_") + name)
        ends = (near.at[rows], far.at[rows])
        return pltpu.make_async_copy(*(ends if out else ends[::-1]), sem)

    def of_block(names, b, rows):
        return [one(k, rows, r.sems.at[NAMES.index(k), b]) for k in names]

    def of_doc(d, n):
        return one("probs", pl.ds(plan.tile(d), n * n), r.sems.at[len(NAMES), 0])

    return of_block, of_doc


def by_block(source, target, sems):
    return lambda b, rows: [pltpu.make_async_copy(source.at[rows], target.at[rows], sems.at[b])]


def started(found):
    for c in found:
        c.start()


def waited(found):
    for c in found:
        c.wait()


def first_kernel(most, span, items, r):
    with_halos(r, r.s_window, span, started)
    w = layer_of(r, 0)
    plan = Plan(r, items)
    kept = SimpleNamespace(**{k: getattr(r, "s_" + k) for k in NAMES})
    of_block, of_doc = copies(r, kept, plan, True)
    leaving = by_block(r.s_rows, r.o_next, r.out_sems)
    clear_between(r.s_window, span, r.own.shape[0])
    with_halos(r, r.s_window, span, waited)
    pack(plan, most, r.s_window, kept.x)
    waited(w.coming)
    project(plan, kept, w.win, w.bin)
    early, late = NAMES[:2], NAMES[2:]
    plan.over_blocks(lambda b, rows: started(of_block(early, b, rows)))
    attend(plan, most, kept, r.s_probs, r.s_turned)
    plan.over_docs(most, lambda d, n, length: of_doc(d, n).start())
    feed(plan, kept, w, r.s_rows, lambda b, rows: started(leaving(b, rows) + of_block(late, b, rows)))
    plan.over_blocks(lambda b, rows: waited(leaving(b, rows) + of_block(NAMES, b, rows)))
    plan.over_docs(most, lambda d, n, length: of_doc(d, n).wait())


def second_kernel(most, span, items, r):
    plan = Plan(r, items)
    kept = SimpleNamespace(**{k: getattr(r, "s_" + k) for k in NAMES})
    coming = by_block(r.x, kept.x, r.in_sems)
    plan.over_blocks(lambda b, rows: started(coming(b, rows)))
    w = layer_of(r, 1)
    with_halos(r, r.s_window, span, started)
    below = layer_of(r, 0)
    waited(w.coming)
    project(plan, kept, w.win, w.bin, lambda b, rows: waited(coming(b, rows)))
    attend(plan, most, kept, r.s_probs, r.s_turned)
    leaving = by_block(r.s_sent, r.o_out, r.out_sems)
    feed(plan, kept, w, r.s_sent, lambda b, rows: started(leaving(b, rows)))
    clear_between(r.s_window, span, r.own.shape[0])
    with_halos(r, r.s_window, span, waited)
    pack(plan, most, r.s_window, r.s_rows)
    clear_totals(r)
    feed_back(plan, kept, w, r.s_rows, r)
    of_block, of_doc = copies(r, kept, plan, False)
    fed = NAMES[2:]
    plan.over_blocks(lambda b, rows: started(of_block(fed, b, rows)))
    attend_back(plan, most, kept, r)
    plan.over_docs(most, lambda d, n, length: of_doc(d, n).start())
    plan.over_blocks(lambda b, rows: started(of_block(NAMES[1:2], b, rows)))
    project_back(plan, kept, w, r, r.s_rows)
    plan.over_blocks(lambda b, rows: started(of_block(NAMES[:1], b, rows)))
    send_pieces(r, r.o_keep1, r.o_send1, r.self[1])
    r.s_both[V_ALL : 2 * V_ALL, :] = r.s_small[...].sum(1)
    clear_totals(r)
    plan.over_blocks(lambda b, rows: waited(leaving(b, rows)))
    waited(below.coming)
    feed_back(plan, kept, below, r.s_rows, r, lambda b, rows: waited(of_block(fed, b, rows)))
    plan.over_docs(most, lambda d, n, length: of_doc(d, n).wait())
    plan.over_blocks(lambda b, rows: waited(of_block(NAMES[1:2], b, rows)))
    attend_back(plan, most, kept, r)
    plan.over_blocks(lambda b, rows: waited(of_block(NAMES[:1], b, rows)))
    leaving = by_block(r.s_sent, r.o_grad, r.out_sems)
    project_back(plan, kept, below, r, r.s_sent, lambda b, rows: started(leaving(b, rows)))
    send_pieces(r, r.o_keep0, r.o_send0, r.self[0])
    r.s_both[0:V_ALL, :] = r.s_small[...].sum(1)
    send_small(r, r.o_keep0, r.o_send0, r.self[0])
    plan.over_blocks(lambda b, rows: waited(leaving(b, rows)))


def third_kernel(most, span, items, r):
    plan = Plan(r, items)
    coming = [by_block(r.out, r.s_rows, r.in_sems), by_block(r.grad, r.s_sent, r.out_sems)]
    for one in coming:
        plan.over_blocks(lambda b, rows: started(one(b, rows)))
    found = []
    for k, (one, rows) in enumerate(zip(coming, (r.s_rows, r.s_sent))):
        plan.over_blocks(lambda b, at: waited(one(b, at)))
        found += unpack(plan, most, rows, r.s_window.at[k], r, span, k)
    waited(found)


def layer_of(r, layer):
    given = dict(win=r.win, wout=r.wout, wup=r.wup, wdown=r.wdown)
    near = dict(win=r.s_win, wout=r.s_wout, wup=r.s_wup, wdown=r.s_wdown)
    near = {k: v.at[layer] for k, v in near.items()}
    coming = []
    for k, name in enumerate(given):
        sem = r.weight_sems.at[4 * layer + k]
        coming.append(pltpu.make_async_copy(given[name].at[layer], near[name], sem))
    started(coming)
    vectors = dict(bin=r.bin, bout=r.bout, g1=r.g1, s1=r.s1, bup=r.bup, bdown=r.bdown, g2=r.g2, s2=r.s2)
    vectors = {k: v[layer : layer + 1, :] for k, v in vectors.items()}
    return SimpleNamespace(**near, **vectors, coming=coming)


def clear_totals(r):
    r.s_total[...] = jnp.zeros(r.s_total.shape, F32)
    r.s_small[...] = jnp.zeros(r.s_small.shape, F32)


def send_pieces(r, keep, send, own):
    half = keep.shape[0]
    rows = AT_ALL // (2 * half)
    for p in range(2 * half):
        out = keep if p < half else send
        at = pl.ds(pl.multiple_of(lax.bitwise_xor(jnp.int32(p), own) * rows, rows), rows)
        out[p % half, 0:rows, :] = r.s_total[at, :].astype(BF)


def send_small(r, keep, send, own):
    half = keep.shape[0]
    rows = AT_ALL // (2 * half)
    extra = keep.shape[1] - rows
    share = V_ALL // half
    for j in range(2 * half):
        line = r.s_both[j * share : (j + 1) * share, :]
        r.s_spread[j] = jnp.concatenate([line, jnp.zeros((extra - share, line.shape[1]), F32)], axis=0)
    for p in range(2 * half):
        out = keep if p < half else send
        out[p % half, rows : rows + extra, :] = r.s_spread[lax.bitwise_xor(jnp.int32(p), own)].astype(BF)


def last_kernel(r):
    half = r.keep0.shape[0]
    count = 2 * half
    rows = AT_ALL // count
    share = 2 * V_ALL // count
    big = (
        (0, AT_OUT, r.s_in, r.o_in),
        (AT_OUT, AT_UP, r.s_out, r.o_out),
        (AT_UP, AT_DOWN, r.s_up, r.o_up),
        (AT_DOWN, AT_ALL, r.s_down, r.o_down),
    )
    sent = []
    for layer, (keep, got) in enumerate(((r.keep0, r.got0), (r.keep1, r.got1))):
        for p in range(count):
            piece = lax.bitwise_xor(jnp.int32(p), r.self[layer])
            source = keep if p < half else got
            r.s_pieces[layer, piece, 0 : keep.shape[1], :] = source[p % half]
        for low, high, near, far in big:
            tall = near.shape[1]
            for at in range(low, high, rows):
                line, col = (at - low) % tall, (at - low) // tall * 256
                value = r.s_pieces[layer, at // rows, 0:rows, :].astype(F32)
                near[layer, line : line + rows, col : col + 256] = value
            copy = pltpu.make_async_copy(near.at[layer], far.at[layer], r.sems.at[len(sent)])
            copy.start()
            sent.append(copy)
    for j in range(count):
        tail = r.s_pieces[0, j, rows : rows + 16, :].astype(F32)
        r.s_both[j * share : (j + 1) * share, :] = tail[0:share]
    for layer in range(2):
        at = layer * V_ALL
        here = pl.ds(layer, 1)

        def line(k):
            return r.s_both[at + k : at + k + 1, :]

        r.o_bin[here, :] = jnp.concatenate([line(V_IN), line(V_IN + 1)], axis=1)
        r.o_bout[here, :] = line(V_OUT)
        r.o_g1[here, :] = line(V_G1)
        r.o_s1[here, :] = line(V_S1)
        r.o_bup[here, :] = jnp.concatenate([line(V_UP), line(V_UP + 1)], axis=1)
        r.o_bdown[here, :] = line(V_DOWN)
        r.o_g2[here, :] = line(V_G2)
        r.o_s2[here, :] = line(V_S2)
    waited(sent)


def call(kernel, consts, inputs, outputs, scratch, flops, megabytes):
    names = tuple(inputs) + tuple(outputs) + tuple(scratch)

    def run(*refs):
        kernel(*consts, SimpleNamespace(**dict(zip(names, refs))))

    got = pl.pallas_call(
        run,
        out_shape=[jax.ShapeDtypeStruct(s, d) for s, d, _ in outputs.values()],
        in_specs=[spec for _, spec in inputs.values()],
        out_specs=[spec for _, _, spec in outputs.values()],
        scratch_shapes=list(scratch.values()),
        compiler_params=pltpu.CompilerParams(vmem_limit_bytes=megabytes << 20),
        cost_estimate=pl.CostEstimate(flops=flops, bytes_accessed=8 << 20, transcendentals=0),
    )(*[a for a, _ in inputs.values()])
    return SimpleNamespace(**dict(zip(outputs, got)))


def cheapest_cuts(starts, costs, section_count, whole):
    base = DOCS + 1
    bar = 1 << 15
    index = jnp.arange(base * base, dtype=jnp.int32)
    first, second = index // base, index % base
    before = jnp.arange(base)[:, None] > jnp.arange(DOCS)[None, :]
    sums = jnp.sum(jnp.where(before[None], costs[:, None, :], 0), axis=2)

    def pairs(values):
        return (values[0][:, None] + values[1][None, :]).reshape(-1)

    spent = pairs(sums)
    ordered = (first[:, None] >= first[None, :]) & (second[:, None] >= second[None, :])
    steps = jnp.where(ordered, spent[:, None] - spent[None, :], bar)
    reached, way, bits = spent, jnp.zeros_like(spent), 0
    for section in range(1, section_count):
        if section > 1:
            packed = jnp.maximum(reached[None, :], steps) * (1 << bits) + way[None, :]
            packed = jnp.min(packed, axis=1)
            reached, way = lax.shift_right_logical(packed, bits), lax.bitwise_and(packed, (1 << bits) - 1)
        far = pairs((jnp.abs(starts - section * whole) > REACH).astype(jnp.int32)) * bar
        reached = jnp.minimum(reached + far, 2 * bar - 1)
        if section < section_count - 1:
            way, bits = way * 128 + index, bits + 7
    last = jnp.min(jnp.maximum(reached, jnp.sum(costs) - spent) * 128 + index)
    last = lax.bitwise_and(last, 127)
    way = jnp.sum(jnp.where(index == last, way, 0))
    cuts = [jnp.int32(0)]
    for section in range(1, section_count - 1):
        shift = 7 * (section_count - 2 - section)
        cuts.append(lax.bitwise_and(lax.shift_right_logical(way, shift), 127))
    cuts = jnp.stack(cuts + [last, jnp.int32(base * base - 1)])
    return jnp.stack([cuts // base, cuts % base], axis=1)


def make_plan(segments, place, section_count):
    row_count, length = segments.shape
    whole = length // section_count
    span = whole + 2 * REACH + 2 * QB
    ids = jnp.arange(DOCS + 1, dtype=jnp.int32)
    starts = jnp.sum((segments[:, None, :] < ids[None, :, None]).astype(jnp.int32), axis=2)
    sizes = starts[:, 1:] - starts[:, :-1]
    if row_count == 2:
        costs = sizes + 190
        for k, more in enumerate((140, 170, 330)):
            costs = costs + jnp.where(sizes > (k + 1) * QB, more, 0)
        cuts = cheapest_cuts(starts, costs, section_count, whole)
    else:
        targets = jnp.arange(section_count + 1, dtype=jnp.int32) * whole
        away = jnp.abs(starts[None] - targets[:, None, None])
        cuts = jnp.min(away * (DOCS + 1) + ids, axis=2) % (DOCS + 1)
    sections = jnp.arange(section_count + 1)[:, None]
    low = jnp.sum(jnp.where(sections == place, cuts, 0), axis=0)[:, None]
    high = jnp.sum(jnp.where(sections == place + 1, cuts, 0), axis=0)[:, None]
    here = (ids[None, :DOCS] >= low) & (ids[None, :DOCS] < high)
    lengths = jnp.where(here, sizes, 0)
    begins = starts[:, :-1] - place * whole + REACH
    begins = begins + jnp.arange(row_count, dtype=jnp.int32)[:, None] * span
    return jnp.where(here, begins, 0), lengths


def halo_sent(low_part, high_part, place):
    upper = lax.rem(place, 2) == 1
    return jnp.where(upper, low_part, high_part), jnp.where(upper, high_part, low_part)


def halo(sent):
    count = lax.axis_size("pipe")
    got = []
    for odd, value in enumerate(sent):
        pairs = [(i, i + 1) for i in range(odd, count - 1, 2)]
        got.append(lax.ppermute(value, "pipe", [p for i, j in pairs for p in ((i, j), (j, i))]))
    return got


def orders():
    found = []
    for axis in ("dp", "pipe"):
        stride = 1
        while stride < lax.axis_size(axis):
            found.append((axis, stride))
            stride *= 2
    other = list(found)
    if len(found) > 2:
        other[1], other[2] = found[2], found[1]
    return found, other


SPLIT = 4


def self_index(order):
    index = jnp.int32(0)
    for axis, stride in order[:SPLIT]:
        index = 2 * index + lax.rem(lax.div(lax.axis_index(axis), stride), 2)
    return index.astype(jnp.int32)


def exchange(value, axis, stride):
    count = lax.axis_size(axis)
    return lax.ppermute(value, axis, [(i, i ^ stride) for i in range(count)])


def added(a, b):
    return (a.astype(F32) + b.astype(F32)).astype(BF)


def sum_steps(keep, send, order):
    total = None
    for k, (axis, stride) in enumerate(order[:SPLIT]):
        got = exchange(send, axis, stride)
        yield None
        half = keep.shape[0] // 2
        if half:
            send, keep = added(keep[half:], got[half:]), added(keep[:half], got[:half])
        else:
            total = added(keep, got)
    for axis, stride in order[SPLIT:]:
        got = exchange(total, axis, stride)
        yield None
        total = added(total, got)
    for k, (axis, stride) in enumerate(reversed(order[:SPLIT])):
        got = exchange(total, axis, stride)
        yield (total, got)
        total = jnp.concatenate([total, got], axis=0)


def body(
    tokens,
    segments,
    cotangent,
    attention_in,
    attention_in_bias,
    attention_out,
    attention_out_bias,
    attention_gain,
    attention_shift,
    expand_weight,
    expand_bias,
    contract_weight,
    contract_bias,
    feed_gain,
    feed_shift,
):
    section_count = lax.axis_size("pipe")
    place = lax.axis_index("pipe").astype(jnp.int32)
    row_count, whole, features = tokens.shape
    span = whole + 2 * REACH + 2 * QB
    items = row_count * DOCS
    most = whole // QB
    cap = row_count * (whole + 2 * REACH) + items * 15
    cap = (cap + TB // 2 - 1) // (TB // 2) * (TB // 2) + QB
    tiles = row_count * 46
    vmem = pl.BlockSpec(memory_space=pltpu.VMEM)
    smem = pl.BlockSpec(memory_space=pltpu.SMEM)
    hbm = pl.BlockSpec(memory_space=pltpu.HBM)
    anywhere = pl.BlockSpec(memory_space=pl.ANY)
    weights = dict(
        win=attention_in,
        bin=attention_in_bias,
        wout=attention_out,
        bout=attention_out_bias,
        g1=attention_gain,
        s1=attention_shift,
        wup=expand_weight,
        bup=expand_bias,
        wdown=contract_weight,
        bdown=contract_bias,
        g2=feed_gain,
        s2=feed_shift,
    )
    weights = {k: (v, vmem if v.ndim == 2 else hbm) for k, v in weights.items()}
    weight_scratch = dict(
        s_win=pltpu.VMEM(attention_in.shape, BF),
        s_wout=pltpu.VMEM(attention_out.shape, BF),
        s_wup=pltpu.VMEM(expand_weight.shape, BF),
        s_wdown=pltpu.VMEM(contract_weight.shape, BF),
        weight_sems=pltpu.SemaphoreType.DMA((4 * attention_in.shape[0],)),
    )

    order0, order1 = orders()
    selves = [self_index(order0), self_index(order1)]
    pieces = 1 << SPLIT
    even, odd = halo(halo_sent(tokens[:, :REACH], tokens[:, whole - REACH :], place))
    token_rows = dict(own=(tokens, anywhere), even=(even, anywhere), odd=(odd, anywhere))
    sent = halo_sent(cotangent[:, :REACH], cotangent[:, whole - REACH :], place)
    even, odd = halo(lax.optimization_barrier((*sent, even, odd))[:2])
    cotangent_rows = dict(own=(cotangent, anywhere), even=(even, anywhere), odd=(odd, anywhere))
    begins, lengths = make_plan(segments, place, section_count)
    plan = dict(begins=(begins, smem), lengths=(lengths, smem), place=(place.reshape(1), smem))
    kept_scratch = {"s_" + k: pltpu.VMEM((cap, c), t) for k, (c, t) in KEPT.items()}
    kept_scratch.update(weight_scratch)
    probs_shape = (tiles, 2, QB, 2 * QB)
    kept_scratch.update(
        s_probs=pltpu.VMEM(probs_shape, BF),
        s_window=pltpu.VMEM((row_count * span, features), BF),
        s_turned=pltpu.VMEM((features, whole), BF),
        s_table=pltpu.SMEM((2 * items,), jnp.int32),
    )
    sems = dict(sems=pltpu.SemaphoreType.DMA((len(NAMES) + 1, MOST_BLOCKS)))
    moved = dict(
        s_rows=pltpu.VMEM((cap, features), BF),
        window_sems=pltpu.SemaphoreType.DMA((3 * row_count,)),
        in_sems=pltpu.SemaphoreType.DMA((MOST_BLOCKS,)),
        out_sems=pltpu.SemaphoreType.DMA((MOST_BLOCKS,)),
    )
    back_scratch = dict(
        s_sent=pltpu.VMEM((cap, features), BF),
        s_total=pltpu.VMEM((AT_ALL, features), F32),
        s_small=pltpu.VMEM((V_ALL, 8, features), F32),
        s_ctx_grad=pltpu.VMEM((cap, features), BF),
        s_sum_grad=pltpu.VMEM((cap, features), F32),
        s_qkv_grad=pltpu.VMEM((cap, 3 * features), BF),
        s_key_sums=pltpu.VMEM((whole, features), F32),
        s_value_sums=pltpu.VMEM((whole, features), F32),
    )
    def pieces_out(extra):
        return ((pieces // 2, AT_ALL // pieces + extra, features), BF, vmem)

    rows_out = ((cap, features), BF, hbm)
    kept_out = {"o_" + k: ((cap, c), t, hbm) for k, (c, t) in KEPT.items()}
    kept_out.update(o_probs=(probs_shape, BF, hbm), o_next=rows_out)
    shape = (most, span, items)

    first = call(
        first_kernel,
        shape,
        plan | token_rows | weights,
        kept_out,
        kept_scratch | sems | moved,
        12 << 30,
        60,
    )
    kept_in = {"i_" + k: (getattr(first, "o_" + k), hbm) for k in NAMES + ("probs",)}
    second = call(
        second_kernel,
        shape,
        plan
        | cotangent_rows
        | kept_in
        | dict(x=(first.o_next, hbm), self=(jnp.stack(selves), smem))
        | weights,
        dict(
            o_keep0=pieces_out(16),
            o_send0=pieces_out(16),
            o_keep1=pieces_out(0),
            o_send1=pieces_out(0),
            o_out=rows_out,
            o_grad=rows_out,
        ),
        kept_scratch
        | back_scratch
        | sems
        | moved
        | dict(
            s_both=pltpu.VMEM((2 * V_ALL, features), F32),
            s_spread=pltpu.VMEM((pieces, 16, features), F32),
        ),
        60 << 30,
        60,
    )
    sums = [sum_steps(second.o_keep0, second.o_send0, order0)]
    sums.append(sum_steps(second.o_keep1, second.o_send1, order1))
    third = call(
        third_kernel,
        shape,
        plan | dict(out=(second.o_out, hbm), grad=(second.o_grad, hbm)),
        dict(
            o_own=((2, row_count, whole, features), BF, anywhere),
            o_left=((2, row_count, REACH, features), BF, anywhere),
            o_right=((2, row_count, REACH, features), BF, anywhere),
        ),
        moved
        | dict(
            s_sent=pltpu.VMEM((cap, features), BF),
            s_window=pltpu.VMEM((2, row_count * span, features), BF),
            s_table=pltpu.SMEM((2 * items,), jnp.int32),
            window_sems=pltpu.SemaphoreType.DMA((2, 3 * row_count)),
        ),
        2 << 30,
        20,
    )
    even, odd = halo(halo_sent(third.o_left, third.o_right, place))
    upper = lax.rem(place, 2) == 1
    gap = jnp.zeros((2, row_count, whole - REACH, features), BF)
    low = jnp.concatenate([jnp.where(upper, even, odd), gap], axis=2)
    high = jnp.concatenate([gap, jnp.where(upper, odd, even)], axis=2)
    layer_output, input_grad = [third.o_own[k] + low[k] + high[k] for k in range(2)]
    for ends in zip(*sums):
        pass
    layers = attention_in.shape[0]

    def out(*shape):
        return ((layers,) + shape, F32, hbm)

    def small_out(*shape):
        return ((layers,) + shape, F32, vmem)

    vector = small_out(features)
    result = call(
        last_kernel,
        (),
        dict(
            self=(jnp.stack(selves), smem),
            keep0=(ends[0][0], vmem),
            got0=(ends[0][1], vmem),
            keep1=(ends[1][0], vmem),
            got1=(ends[1][1], vmem),
        ),
        dict(
            o_in=out(features, 3 * features),
            o_bin=small_out(2 * features),
            o_out=out(features, features),
            o_bout=vector,
            o_g1=vector,
            o_s1=vector,
            o_up=out(features, 2 * features),
            o_bup=small_out(2 * features),
            o_down=out(2 * features, features),
            o_bdown=vector,
            o_g2=vector,
            o_s2=vector,
        ),
        dict(
            s_pieces=pltpu.VMEM((2, pieces, AT_ALL // pieces + 16, features), BF),
            s_both=pltpu.VMEM((2 * V_ALL, features), F32),
            s_in=pltpu.VMEM((layers, features, 3 * features), F32),
            s_out=pltpu.VMEM((layers, features, features), F32),
            s_up=pltpu.VMEM((layers, features, 2 * features), F32),
            s_down=pltpu.VMEM((layers, 2 * features, features), F32),
            sems=pltpu.SemaphoreType.DMA((4 * layers,)),
        ),
        1 << 30,
        20,
    )
    return (layer_output, input_grad) + tuple(vars(result).values())


def solution(mesh):
    rows = P("dp", "pipe", None)
    return jax.shard_map(
        body,
        mesh=mesh,
        in_specs=(rows, P("dp", None), rows) + (P(),) * 12,
        out_specs=(rows, rows) + (P(),) * 12,
        check_vma=False,
    )
```

```python
from types import SimpleNamespace

import jax
import jax.numpy as jnp
from jax import lax
from jax.experimental import pallas as pl
from jax.experimental.pallas import tpu as pltpu
from jax.sharding import PartitionSpec as P

HEADS = 4
EPSILON = 1e-12
MASKED = -1e30
DOCS = 8
REACH = 320
TB = 512
MOST_BLOCKS = 8
QB = 128
LANES = 128

BF = jnp.bfloat16
F32 = jnp.float32

KEPT = dict(
    x=(256, BF),
    qkv=(768, BF),
    ctx=(256, BF),
    n1=(256, BF),
    r1=(128, F32),
    mid=(256, BF),
    act=(512, BF),
    slope=(512, BF),
    n2=(256, BF),
    r2=(128, F32),
)
NAMES = tuple(KEPT)


def dot(a, b):
    return jnp.dot(a, b, preferred_element_type=F32)


def dot_nt(a, b):
    return lax.dot_general(a, b, (((1,), (1,)), ((), ())), preferred_element_type=F32)


def dot_tn(a, b):
    return lax.dot_general(a, b, (((0,), (0,)), ((), ())), preferred_element_type=F32)


def fold(v):
    return v.reshape(-1, 8, v.shape[-1]).sum(0)


def rows_at(start, count):
    return pl.ds(pl.multiple_of(start, 16), count)


ITEMS = 2 * DOCS
ROOM = ITEMS + 1


class Plan:
    def __init__(self, r):
        self.table = r.table
        self.count, self.blocks, self.odd, self.end = (r.table[4 * ROOM + k] for k in range(4))

    def start(self, d):
        return self.table[d]

    def length(self, d):
        return self.table[ROOM + d]

    def offset(self, d):
        return self.table[2 * ROOM + d]

    def tile(self, d):
        return self.table[3 * ROOM + d]

    def size(self, d):
        return lax.shift_right_logical(self.length(d) + (QB - 1), 7)

    def over_docs(self, most, visit):
        def one(d, _):
            size = self.size(d)
            for n in range(1, most + 1):

                @pl.when(size == n)
                def _():
                    visit(d, n, self.length(d))

            return 0

        lax.fori_loop(0, self.count, one, 0)

    def over_groups(self, most, visit):
        def one(d):
            size = jnp.maximum(self.size(d), 2)
            after = self.size(d + 1)
            two = (size == 2) & (after >= 1) & (after <= 2)

            @pl.when(two)
            def _():
                visit([(d, 2), (d + 1, 2)])

            for n in range(2, most + 1):

                @pl.when((size == n) & jnp.logical_not(two))
                def _():
                    visit([(d, n)])

            return d + 1 + two.astype(jnp.int32)

        lax.while_loop(lambda d: d < self.count, one, jnp.int32(0))

    def over_blocks(self, visit):
        def one(b, _):
            visit(b, rows_at(b * TB, TB))
            return 0

        lax.fori_loop(0, self.blocks, one, 0)

        @pl.when(self.odd == 1)
        def _():
            visit(self.blocks, rows_at(self.blocks * TB, TB // 2))


def window_copies(win, span, own, low, high, sems, out):
    reach, whole = low.shape[1], own.shape[1]
    found = []
    for k in range(own.shape[0]):
        at = k * span
        for far, count in ((low, reach), (own, whole), (high, reach)):
            ends = (win.at[pl.ds(at, count)], far.at[k])
            found.append(pltpu.make_async_copy(*(ends if out else ends[::-1]), sems.at[len(found)]))
            at += count
    return found


def with_halos(r, win, span, act):
    upper = lax.bitwise_and(r.place[0], 1)
    for side in range(2):

        @pl.when(upper == 1 - side)
        def _():
            low, high = (r.odd, r.even) if side else (r.even, r.odd)
            act(window_copies(win, span, r.own, low, high, r.window_sems, False))


def clear_between(win, span, count):
    used = span - 2 * QB
    for k in range(count):
        clear(win, pl.ds(k * span + used, 2 * QB))


SPREAD = QB + 16


def pack(plan, most, win, dst):
    plan.over_blocks(lambda b, rows: clear(dst, rows))

    def visit(d, n, length):
        start, offset = plan.start(d), plan.offset(d)
        shift = lax.bitwise_and(start, 15)
        row = lax.broadcasted_iota(jnp.int32, (QB, SPREAD), 0)
        col = lax.broadcasted_iota(jnp.int32, (QB, SPREAD), 1)
        taken = col == row + shift
        kept = jnp.where(taken & (row < length - (n - 1) * QB), 1.0, 0.0).astype(BF)
        taken = jnp.where(taken, 1.0, 0.0).astype(BF)
        rows = [win[rows_at(start - shift + q * QB, SPREAD), :] for q in range(n)]
        picked = [dot(taken if q < n - 1 else kept, v).astype(BF) for q, v in enumerate(rows)]
        for q, v in enumerate(picked):
            dst[rows_at(offset + q * QB, QB), :] = v

    plan.over_docs(most, visit)


def unpack(plan, most, src, win, r, span, which):
    win[...] = jnp.zeros(win.shape, BF)
    clear(src, rows_at(plan.end, QB))

    def visit(d, n, length):
        start, offset = plan.start(d), plan.offset(d)
        shift = lax.bitwise_and(start, 15)
        row = lax.broadcasted_iota(jnp.int32, (SPREAD, QB), 0)
        col = lax.broadcasted_iota(jnp.int32, (SPREAD, QB), 1)
        taken = row == col + shift
        kept = jnp.where(taken & (col < length - (n - 1) * QB), 1.0, 0.0).astype(BF)
        taken = jnp.where(taken, 1.0, 0.0).astype(BF)
        rows = [src[rows_at(offset + q * QB, QB), :] for q in range(n)]
        placed = [dot(taken if q < n - 1 else kept, v) for q, v in enumerate(rows)]
        for q, v in enumerate(placed):
            at = rows_at(start - shift + q * QB, SPREAD)
            win[at, :] = (win[at, :].astype(F32) + v).astype(BF)

    plan.over_docs(most, visit)
    ends = [v.at[which] for v in (r.o_own, r.o_left, r.o_right)]
    found = window_copies(win, span, *ends, r.window_sems.at[which], True)
    started(found)
    return found


def clear(ref, rows):
    ref[rows, :] = jnp.zeros((rows.size, ref.shape[1]), ref.dtype)


def head_masks():
    lane = lax.broadcasted_iota(jnp.int32, (1, LANES), 1)
    low = (lane < LANES // 2).astype(F32)
    return low.astype(BF), (1.0 - low).astype(BF)


def two_heads(v, masks):
    return jnp.concatenate([v * masks[0], v * masks[1]], axis=0)


def turned_back(v):
    row = lax.broadcasted_iota(jnp.int32, (LANES, QB), 0)
    return jnp.where(row < LANES // 2, v[:, :QB], v[:, QB:]).T


def turn(src, dst, first, width):
    for k in range(width // LANES):
        at = slice(k * LANES, (k + 1) * LANES)
        for g in range(2):
            here = slice(g * LANES, (g + 1) * LANES)
            dst[here, first + at.start : first + at.stop] = src[at, here].T


def project(plan, kept, weight, bias, before=None):
    scaling = (weight.shape[0] // HEADS) ** (-0.5)

    def visit(b, rows):
        if before is not None:
            before(b, rows)
        y = dot(kept.x[rows, :], weight[...])
        queries = (y[:, 0:256] + bias[:, 0:256]).astype(BF)
        kept.qkv[rows, 0:256] = queries * jnp.asarray(scaling, BF)
        kept.qkv[rows, 256:512] = y[:, 256:512].astype(BF)
        kept.qkv[rows, 512:768] = (y[:, 512:768] + bias[:, 256:512]).astype(BF)
        clear(kept.ctx, rows)

    plan.over_blocks(visit)
    clear(kept.qkv, rows_at(plan.end, 2 * QB))


GROUPS = tuple(slice(g * LANES, (g + 1) * LANES) for g in range(2))


def shifted(cols, by):
    return slice(cols.start + by, cols.stop + by)


def attend(plan, most, kept, weights_low, values_turned):
    masks = head_masks()

    def visit(docs):
        offset = [plan.offset(d) for d, _ in docs]
        length = [plan.length(d) for d, _ in docs]
        tile = [plan.tile(d) for d, _ in docs]
        width = [n * QB for _, n in docs]
        firsts = [sum(width[:i]) for i in range(len(docs))]
        spans = [rows_at(o, v) for o, v in zip(offset, width)]
        for i, first in enumerate(firsts):
            turn(kept.qkv[spans[i], 512:768], values_turned, first, width[i])
        chains = [(i, q, g) for i, (_, n) in enumerate(docs) for q in range(n) for g in range(2)]
        column = lax.broadcasted_iota(jnp.int32, (1, 2 * QB), 1)
        column = lax.bitwise_and(column, QB - 1)
        row = lax.broadcasted_iota(jnp.int32, (QB, 2 * QB), 0)
        keys = [[kept.qkv[at, shifted(c, 256)] for c in GROUPS] for at in spans]
        turned = [[values_turned[c, f : f + v] for c in GROUPS] for f, v in zip(firsts, width)]
        queries = [kept.qkv[rows_at(offset[i] + q * QB, QB), GROUPS[g]] for i, q, g in chains]
        queries = [two_heads(v, masks) for v in queries]
        scores = [dot_nt(keys[i][g], v) for v, (i, _, g) in zip(queries, chains)]
        probs = []
        for v, (i, q, g) in zip(scores, chains):
            parts = []
            for k in range(docs[i][1]):
                part = v[k * QB : (k + 1) * QB, :]
                if k == docs[i][1] - 1 or docs[i][1] == 2:
                    part = jnp.where(row < length[i] - k * QB, part, MASKED)
                parts.append(part)
            v = jnp.concatenate(parts, axis=0)
            raised = jnp.exp(v - jnp.max(v, axis=0, keepdims=True))
            total = jnp.sum(raised, axis=0, keepdims=True)
            share = jnp.where(column < length[i] - q * QB, 1.0 / total, 0.0)
            probs.append((raised * share).astype(BF))
        contexts = [dot(turned[i][g], v) for v, (i, _, g) in zip(probs, chains)]
        contexts = [turned_back(v).astype(BF) for v in contexts]
        for v, context, (i, q, g) in zip(probs, contexts, chains):
            kept.ctx[rows_at(offset[i] + q * QB, QB), GROUPS[g]] = context
            n = docs[i][1]
            for k in range(n):
                weights_low[tile[i] + q * n + k, g] = v[k * QB : (k + 1) * QB, :]

    plan.over_groups(most, visit)


def normal(v):
    centred = v - jnp.mean(v, axis=1, keepdims=True)
    spread = jnp.mean(centred * centred, axis=1, keepdims=True)
    rate = lax.rsqrt(spread + EPSILON)
    return centred * rate, rate


def parts_of(rows, count):
    step = rows.size // count
    return [rows_at(rows.start + k * step, step) for k in range(count)]


def feed(plan, kept, w, out, each=None):
    def visit(b, rows):
        chains = parts_of(rows, 1)
        wout, wup, wdown = w.wout[...], w.wup[...], w.wdown[...]
        x = [kept.x[at, :] for at in chains]
        ctx = [kept.ctx[at, :] for at in chains]
        attn_sum = [u.astype(F32) + dot(v, wout) + w.bout for u, v in zip(x, ctx)]
        first = [normal(v) for v in attn_sum]
        mid_low = [(n * w.g1 + w.s1).astype(BF) for n, _ in first]
        pre_up = [dot(v, wup) + w.bup for v in mid_low]
        share = [0.5 + 0.5 * lax.erf(v * (0.5**0.5)) for v in pre_up]
        active = [(v * p).astype(BF) for v, p in zip(pre_up, share)]
        density = [jnp.exp(v * v * -0.5) * 0.3989422804014327 for v in pre_up]
        slope = [(p + v * q).astype(BF) for v, p, q in zip(pre_up, share, density)]
        feed_sum = [u.astype(F32) + dot(v, wdown) + w.bdown for u, v in zip(mid_low, active)]
        second = [normal(v) for v in feed_sum]
        for k, at in enumerate(chains):
            kept.n1[at, :] = first[k][0].astype(BF)
            kept.r1[at, :] = jnp.broadcast_to(first[k][1], (at.size, LANES))
            kept.mid[at, :] = mid_low[k]
            kept.act[at, :] = active[k]
            kept.slope[at, :] = slope[k]
            kept.n2[at, :] = second[k][0].astype(BF)
            kept.r2[at, :] = jnp.broadcast_to(second[k][1], (at.size, LANES))
            out[at, :] = (second[k][0] * w.g2 + w.s2).astype(BF)
        if each is not None:
            each(b, rows)

    plan.over_blocks(visit)


AT_OUT, AT_UP, AT_DOWN, AT_ALL = 768, 1024, 1536, 2048
V_IN, V_OUT, V_G1, V_S1, V_UP, V_DOWN, V_G2, V_S2, V_ALL = 0, 2, 3, 4, 5, 7, 8, 9, 16


def norm_back(upstream, n, rate, gain):
    e = upstream * gain
    inner = jnp.mean(e * n, axis=1, keepdims=True)
    return (e - jnp.mean(e, axis=1, keepdims=True) - n * inner) * rate


def doubled(v):
    return jnp.concatenate([v, v], axis=1)


def joined(values):
    return jnp.concatenate(values, axis=0) if len(values) > 1 else values[0]


def feed_back(plan, kept, w, upstream, r, before=None):
    total, small, ctx_grad, sum_grad = r.s_total, r.s_small, r.s_ctx_grad, r.s_sum_grad

    def visit(b, rows):
        if before is not None:
            before(b, rows)
        chains = parts_of(rows, 2)
        wout, wup, wdown = w.wout[...], w.wup[...], w.wdown[...]
        up = [upstream[at, :].astype(F32) for at in chains]
        n2 = [kept.n2[at, :].astype(F32) for at in chains]
        r2 = [doubled(kept.r2[at, :]) for at in chains]
        slope = [kept.slope[at, :] for at in chains]
        n1 = [kept.n1[at, :].astype(F32) for at in chains]
        r1 = [doubled(kept.r1[at, :]) for at in chains]
        act, mid, ctx = kept.act[rows, :], kept.mid[rows, :], kept.ctx[rows, :]
        feed_grad = [norm_back(u, n, v, w.g2) for u, n, v in zip(up, n2, r2)]
        feed_low = [v.astype(BF) for v in feed_grad]
        active_grad = [dot_nt(v, wdown) for v in feed_low]
        pre_grad = [(v * p.astype(F32)).astype(BF) for v, p in zip(active_grad, slope)]
        mid_grad = [dot_nt(v, wup) + u for v, u in zip(pre_grad, feed_grad)]
        mid_grad = [v.astype(BF).astype(F32) for v in mid_grad]
        attn_grad = [norm_back(u, n, v, w.g1) for u, n, v in zip(mid_grad, n1, r1)]
        attn_low = [v.astype(BF) for v in attn_grad]
        back = [dot_nt(v, wout).astype(BF) for v in attn_low]
        down_total = dot_tn(act, joined(feed_low))
        up_total = dot_tn(mid, joined(pre_grad))
        out_total = dot_tn(ctx, joined(attn_low))
        up_sums = fold(joined(pre_grad).astype(F32))
        sums = [
            (V_G2, fold(joined([u * n for u, n in zip(up, n2)]))),
            (V_S2, fold(joined(up))),
            (V_DOWN, fold(joined(feed_low).astype(F32))),
            (V_UP, up_sums[:, :256]),
            (V_UP + 1, up_sums[:, 256:]),
            (V_G1, fold(joined([u * n for u, n in zip(mid_grad, n1)]))),
            (V_S1, fold(joined(mid_grad))),
            (V_OUT, fold(joined(attn_low).astype(F32))),
        ]
        for k, at in enumerate(chains):
            sum_grad[at, :] = attn_grad[k]
            ctx_grad[at, :] = back[k]
        total[AT_DOWN:AT_ALL, :] += down_total
        total[AT_UP : AT_UP + 256, :] += up_total[:, :256]
        total[AT_UP + 256 : AT_DOWN, :] += up_total[:, 256:]
        total[AT_OUT:AT_UP, :] += out_total
        for line, v in sums:
            small[line] += v

    plan.over_blocks(visit)
    clear(ctx_grad, rows_at(plan.end, 2 * QB))


def attend_back(plan, most, kept, r):
    weights_low, ctx_grad, qkv_grad, keys_turned = r.s_probs, r.s_ctx_grad, r.s_qkv_grad, r.s_turned
    masks = head_masks()
    scaling = (256 // HEADS) ** (-0.5)
    plan.over_blocks(lambda b, rows: clear(qkv_grad, rows))

    def visit(docs):
        offset = [plan.offset(d) for d, _ in docs]
        tile = [plan.tile(d) for d, _ in docs]
        width = [n * QB for _, n in docs]
        firsts = [sum(width[:i]) for i in range(len(docs))]
        spans = [rows_at(o, v) for o, v in zip(offset, width)]
        for i, first in enumerate(firsts):
            turn(kept.qkv[spans[i], 256:512], keys_turned, first, width[i])
        chains = [(i, q, g) for i, (_, n) in enumerate(docs) for q in range(n) for g in range(2)]
        values = [[kept.qkv[at, shifted(c, 512)] for c in GROUPS] for at in spans]
        turned = [[keys_turned[c, f : f + v] for c in GROUPS] for f, v in zip(firsts, width)]
        queries = [kept.qkv[rows_at(offset[i] + q * QB, QB), GROUPS[g]] for i, q, g in chains]
        grads = [ctx_grad[rows_at(offset[i] + q * QB, QB), GROUPS[g]] for i, q, g in chains]
        probs = []
        for i, q, g in chains:
            n = docs[i][1]
            probs.append(joined([weights_low[tile[i] + q * n + k, g] for k in range(n)]))
        queries = [two_heads(v, masks) for v in queries]
        grads = [two_heads(v, masks) for v in grads]
        prob_grads = [dot_nt(values[i][g], v) for v, (i, _, g) in zip(grads, chains)]
        score_grads = []
        for low, v in zip(probs, prob_grads):
            full = low.astype(F32)
            inner = jnp.sum(full * v, axis=0, keepdims=True)
            score_grads.append((full * (v - inner)).astype(BF))
        query_grads = [dot(turned[i][g], v) for v, (i, _, g) in zip(score_grads, chains)]
        query_grads = [(turned_back(v) * scaling).astype(BF) for v in query_grads]
        sums = []
        for i in range(len(docs)):
            for g in range(2):
                mine = [k for k, c in enumerate(chains) if (c[0], c[2]) == (i, g)]
                sides = jnp.concatenate([score_grads[k] for k in mine], axis=1)
                key_sum = dot(sides, joined([queries[k] for k in mine])).astype(BF)
                sides = jnp.concatenate([probs[k] for k in mine], axis=1)
                value_sum = dot(sides, joined([grads[k] for k in mine])).astype(BF)
                sums.append((i, g, key_sum, value_sum))
        for i in range(len(docs)):
            for v, (own, q, g) in zip(query_grads, chains):
                if own == i:
                    qkv_grad[rows_at(offset[i] + q * QB, QB), GROUPS[g]] = v
            for own, g, key_sum, value_sum in sums:
                if own == i:
                    qkv_grad[spans[i], shifted(GROUPS[g], 256)] = key_sum
                    qkv_grad[spans[i], shifted(GROUPS[g], 512)] = value_sum

    plan.over_groups(most, visit)


def project_back(plan, kept, w, r, out, after=None):
    qkv_grad, sum_grad, total, small = r.s_qkv_grad, r.s_sum_grad, r.s_total, r.s_small

    def visit(b, rows):
        grad = qkv_grad[rows, :]
        sums = fold(grad.astype(F32))
        small[V_IN] += sums[:, :256]
        small[V_IN + 1] += sums[:, 512:]
        in_grad = dot_tn(kept.x[rows, :], grad)
        for k in range(3):
            total[256 * k : 256 * (k + 1), :] += in_grad[:, 256 * k : 256 * (k + 1)]
        hidden_grad = dot_nt(grad, w.win[...]) + sum_grad[rows, :]
        out[rows, :] = hidden_grad.astype(BF)
        if after is not None:
            after(b, rows)

    plan.over_blocks(visit)


def copies(r, kept, plan, out):
    def one(name, rows, sem):
        near = getattr(r if name == "probs" else kept, "s_probs" if name == "probs" else name)
        far = getattr(r, ("o_" if out else "i_") + name)
        ends = (near.at[rows], far.at[rows])
        return pltpu.make_async_copy(*(ends if out else ends[::-1]), sem)

    def of_block(names, b, rows):
        return [one(k, rows, r.sems.at[NAMES.index(k), b]) for k in names]

    def of_doc(d, n):
        return one("probs", pl.ds(plan.tile(d), max(n, 2) ** 2), r.sems.at[len(NAMES), 0])

    return of_block, of_doc


def by_block(source, target, sems):
    return lambda b, rows: [pltpu.make_async_copy(source.at[rows], target.at[rows], sems.at[b])]


def started(found):
    for c in found:
        c.start()


def waited(found):
    for c in found:
        c.wait()


def first_kernel(most, span, r):
    with_halos(r, r.s_window, span, started)
    w = layer_of(r, 0)
    plan = Plan(r)
    kept = SimpleNamespace(**{k: getattr(r, "s_" + k) for k in NAMES})
    of_block, of_doc = copies(r, kept, plan, True)
    leaving = by_block(r.s_rows, r.o_next, r.out_sems)
    clear_between(r.s_window, span, r.own.shape[0])
    with_halos(r, r.s_window, span, waited)
    pack(plan, most, r.s_window, kept.x)
    waited(w.coming)
    project(plan, kept, w.win, w.bin)
    early, late = NAMES[:2], NAMES[2:]
    plan.over_blocks(lambda b, rows: started(of_block(early, b, rows)))
    attend(plan, most, kept, r.s_probs, r.s_turned)
    plan.over_docs(most, lambda d, n, length: of_doc(d, n).start())
    feed(plan, kept, w, r.s_rows, lambda b, rows: started(leaving(b, rows) + of_block(late, b, rows)))
    plan.over_blocks(lambda b, rows: waited(leaving(b, rows) + of_block(NAMES, b, rows)))
    plan.over_docs(most, lambda d, n, length: of_doc(d, n).wait())


def second_kernel(most, span, r):
    plan = Plan(r)
    kept = SimpleNamespace(**{k: getattr(r, "s_" + k) for k in NAMES})
    coming = by_block(r.x, kept.x, r.in_sems)
    plan.over_blocks(lambda b, rows: started(coming(b, rows)))
    w = layer_of(r, 1)
    with_halos(r, r.s_window, span, started)
    below = layer_of(r, 0)
    waited(w.coming)
    project(plan, kept, w.win, w.bin, lambda b, rows: waited(coming(b, rows)))
    attend(plan, most, kept, r.s_probs, r.s_turned)
    leaving = by_block(r.s_ctx_grad, r.o_out, r.out_sems)
    feed(plan, kept, w, r.s_ctx_grad, lambda b, rows: started(leaving(b, rows)))
    clear_between(r.s_window, span, r.own.shape[0])
    with_halos(r, r.s_window, span, waited)
    pack(plan, most, r.s_window, r.s_rows)
    clear_totals(r)
    plan.over_blocks(lambda b, rows: waited(leaving(b, rows)))
    feed_back(plan, kept, w, r.s_rows, r)
    of_block, of_doc = copies(r, kept, plan, False)
    fed = NAMES[2:]
    plan.over_blocks(lambda b, rows: started(of_block(fed, b, rows)))
    attend_back(plan, most, kept, r)
    plan.over_docs(most, lambda d, n, length: of_doc(d, n).start())
    plan.over_blocks(lambda b, rows: started(of_block(NAMES[1:2], b, rows)))
    project_back(plan, kept, w, r, r.s_rows)
    plan.over_blocks(lambda b, rows: started(of_block(NAMES[:1], b, rows)))
    send_pieces(r, r.o_keep1, r.o_send1, r.self[1])
    r.s_both[V_ALL : 2 * V_ALL, :] = r.s_small[...].sum(1)
    clear_totals(r)
    waited(below.coming)
    feed_back(plan, kept, below, r.s_rows, r, lambda b, rows: waited(of_block(fed, b, rows)))
    plan.over_docs(most, lambda d, n, length: of_doc(d, n).wait())
    plan.over_blocks(lambda b, rows: waited(of_block(NAMES[1:2], b, rows)))
    attend_back(plan, most, kept, r)
    plan.over_blocks(lambda b, rows: waited(of_block(NAMES[:1], b, rows)))
    leaving = by_block(r.s_ctx_grad, r.o_grad, r.out_sems)
    project_back(plan, kept, below, r, r.s_ctx_grad, lambda b, rows: started(leaving(b, rows)))
    send_pieces(r, r.o_keep0, r.o_send0, r.self[0])
    r.s_both[0:V_ALL, :] = r.s_small[...].sum(1)
    send_small(r, r.o_keep0, r.o_send0, r.self[0])
    plan.over_blocks(lambda b, rows: waited(leaving(b, rows)))


def third_kernel(most, span, r):
    plan = Plan(r)
    coming = [by_block(r.out, r.s_rows, r.in_sems), by_block(r.grad, r.s_sent, r.out_sems)]
    for one in coming:
        plan.over_blocks(lambda b, rows: started(one(b, rows)))
    found = []
    for k, (one, rows) in enumerate(zip(coming, (r.s_rows, r.s_sent))):
        plan.over_blocks(lambda b, at: waited(one(b, at)))
        found += unpack(plan, most, rows, r.s_window.at[k], r, span, k)
    waited(found)


def layer_of(r, layer):
    given = dict(win=r.win, wout=r.wout, wup=r.wup, wdown=r.wdown)
    near = dict(win=r.s_win, wout=r.s_wout, wup=r.s_wup, wdown=r.s_wdown)
    near = {k: v.at[layer] for k, v in near.items()}
    coming = []
    for k, name in enumerate(given):
        sem = r.weight_sems.at[4 * layer + k]
        coming.append(pltpu.make_async_copy(given[name].at[layer], near[name], sem))
    started(coming)
    vectors = dict(bin=r.bin, bout=r.bout, g1=r.g1, s1=r.s1, bup=r.bup, bdown=r.bdown, g2=r.g2, s2=r.s2)
    vectors = {k: v[layer : layer + 1, :] for k, v in vectors.items()}
    return SimpleNamespace(**near, **vectors, coming=coming)


def clear_totals(r):
    r.s_total[...] = jnp.zeros(r.s_total.shape, F32)
    r.s_small[...] = jnp.zeros(r.s_small.shape, F32)


def send_pieces(r, keep, send, own):
    half = keep.shape[0]
    rows = AT_ALL // (2 * half)
    for p in range(2 * half):
        out = keep if p < half else send
        at = pl.ds(pl.multiple_of(lax.bitwise_xor(jnp.int32(p), own) * rows, rows), rows)
        out[p % half, 0:rows, :] = r.s_total[at, :].astype(BF)


def send_small(r, keep, send, own):
    half = keep.shape[0]
    rows = AT_ALL // (2 * half)
    extra = keep.shape[1] - rows
    share = V_ALL // half
    for j in range(2 * half):
        line = r.s_both[j * share : (j + 1) * share, :]
        r.s_spread[j] = jnp.concatenate([line, jnp.zeros((extra - share, line.shape[1]), F32)], axis=0)
    for p in range(2 * half):
        out = keep if p < half else send
        out[p % half, rows : rows + extra, :] = r.s_spread[lax.bitwise_xor(jnp.int32(p), own)].astype(BF)


def last_kernel(r):
    half = r.keep0.shape[0]
    count = 2 * half
    rows = AT_ALL // count
    share = 2 * V_ALL // count
    big = (
        (0, AT_OUT, r.s_in, r.o_in),
        (AT_OUT, AT_UP, r.s_out, r.o_out),
        (AT_UP, AT_DOWN, r.s_up, r.o_up),
        (AT_DOWN, AT_ALL, r.s_down, r.o_down),
    )
    sent = []
    for layer, (keep, got) in enumerate(((r.keep0, r.got0), (r.keep1, r.got1))):
        for p in range(count):
            piece = lax.bitwise_xor(jnp.int32(p), r.self[layer])
            source = keep if p < half else got
            r.s_pieces[layer, piece, 0 : keep.shape[1], :] = source[p % half]
        for low, high, near, far in big:
            tall = near.shape[1]
            for at in range(low, high, rows):
                line, col = (at - low) % tall, (at - low) // tall * 256
                value = r.s_pieces[layer, at // rows, 0:rows, :].astype(F32)
                near[layer, line : line + rows, col : col + 256] = value
            copy = pltpu.make_async_copy(near.at[layer], far.at[layer], r.sems.at[len(sent)])
            copy.start()
            sent.append(copy)
    for j in range(count):
        tail = r.s_pieces[0, j, rows : rows + 16, :].astype(F32)
        r.s_both[j * share : (j + 1) * share, :] = tail[0:share]
    for layer in range(2):
        at = layer * V_ALL
        here = pl.ds(layer, 1)

        def line(k):
            return r.s_both[at + k : at + k + 1, :]

        r.o_bin[here, :] = jnp.concatenate([line(V_IN), line(V_IN + 1)], axis=1)
        r.o_bout[here, :] = line(V_OUT)
        r.o_g1[here, :] = line(V_G1)
        r.o_s1[here, :] = line(V_S1)
        r.o_bup[here, :] = jnp.concatenate([line(V_UP), line(V_UP + 1)], axis=1)
        r.o_bdown[here, :] = line(V_DOWN)
        r.o_g2[here, :] = line(V_G2)
        r.o_s2[here, :] = line(V_S2)
    waited(sent)


def call(kernel, consts, inputs, outputs, scratch, flops, megabytes):
    names = tuple(inputs) + tuple(outputs) + tuple(scratch)

    def run(*refs):
        kernel(*consts, SimpleNamespace(**dict(zip(names, refs))))

    got = pl.pallas_call(
        run,
        out_shape=[jax.ShapeDtypeStruct(s, d) for s, d, _ in outputs.values()],
        in_specs=[spec for _, spec in inputs.values()],
        out_specs=[spec for _, _, spec in outputs.values()],
        scratch_shapes=list(scratch.values()),
        compiler_params=pltpu.CompilerParams(vmem_limit_bytes=megabytes << 20),
        cost_estimate=pl.CostEstimate(flops=flops, bytes_accessed=8 << 20, transcendentals=0),
    )(*[a for a, _ in inputs.values()])
    return SimpleNamespace(**dict(zip(outputs, got)))


def plan_kernel(sections, whole, span, r):
    base = DOCS + 1
    huge = jnp.int32(1 << 20)
    for row in range(2):
        line = r.segments[row : row + 1, :]
        starts = [jnp.int32(0)]
        for doc in range(1, DOCS):
            below = jnp.where(line < doc, 1.0, 0.0)
            starts.append(jnp.sum(below).astype(jnp.int32))
        starts.append(jnp.int32(sections * whole))
        spent = jnp.int32(0)
        for doc in range(base):
            r.start[row * base + doc] = starts[doc]
            r.spent[row * base + doc] = spent
            if doc < DOCS:
                size = starts[doc + 1] - starts[doc]
                spent = spent + size + 230
                spent = spent + jnp.where(size > 2 * QB, 270, 0) + jnp.where(size > 3 * QB, 330, 0)
        for section in range(1, sections):
            low, high = jnp.int32(0), jnp.int32(0)
            for doc in range(base):
                away = starts[doc] - section * whole
                low = low + (away < -REACH).astype(jnp.int32)
                high = high + (away <= REACH).astype(jnp.int32)
            r.low[2 * section + row] = low
            r.high[2 * section + row] = high

    def over(section, visit, first):
        def outer(i, carry):
            inner = lambda j, c: visit(i, j, c)
            return lax.fori_loop(r.low[2 * section + 1], r.high[2 * section + 1], inner, carry)

        return lax.fori_loop(r.low[2 * section], r.high[2 * section], outer, first)

    def least(section, end, top, right):
        def visit(i, j, carry):
            cost, code = carry
            at = i * base + j
            step = end - r.spent[i] - r.spent[base + j]
            new = jnp.maximum(r.best[section * base * base + at], step)
            new = jnp.where((i <= top) & (j <= right), new, huge)
            better = new < cost
            return jnp.where(better, new, cost), jnp.where(better, at, code)

        return over(section, visit, (huge, jnp.int32(0)))

    for section in range(1, sections):

        def visit(i, j, carry):
            at = section * base * base + i * base + j
            end = r.spent[i] + r.spent[base + j]
            if section == 1:
                r.best[at] = end
            else:
                r.best[at], r.way[at] = least(section - 1, end, i, j)
            return carry

        over(section, visit, jnp.int32(0))
    _, code = least(sections - 1, r.spent[DOCS] + r.spent[base + DOCS], jnp.int32(DOCS), jnp.int32(DOCS))
    cuts = [jnp.int32(base * base - 1), code]
    for section in range(sections - 1, 1, -1):
        code = r.way[section * base * base + code]
        cuts.append(code)
    cuts = (cuts + [jnp.int32(0)])[::-1]
    place = r.place[0]
    low, high = jnp.int32(0), jnp.int32(0)
    for section in range(sections):
        low = jnp.where(place == section, cuts[section], low)
        high = jnp.where(place == section, cuts[section + 1], high)
    low, high = (low // base, low % base), (high // base, high % base)
    k, offset, tile = jnp.int32(0), jnp.int32(0), jnp.int32(0)
    table = r.table
    for row in range(2):

        def one(doc, carry):
            k, offset, tile = carry
            begin = r.start[row * base + doc]
            length = r.start[row * base + doc + 1] - begin
            table[k] = begin - place * whole + REACH + row * span
            table[ROOM + k] = length
            table[2 * ROOM + k] = offset
            table[3 * ROOM + k] = tile
            blocks = jnp.maximum(lax.shift_right_logical(length + (QB - 1), 7), 2)
            return k + 1, offset + lax.bitwise_and(length + 15, -16), tile + blocks * blocks

        k, offset, tile = lax.fori_loop(low[row], high[row], one, (k, offset, tile))
    table[ROOM + k] = 0
    halves = lax.shift_right_logical(offset + (TB // 2 - 1), 8)
    table[4 * ROOM] = k
    table[4 * ROOM + 1] = lax.shift_right_logical(halves, 1)
    table[4 * ROOM + 2] = lax.bitwise_and(halves, 1)
    table[4 * ROOM + 3] = halves * (TB // 2)


def halo_sent(low_part, high_part, place):
    upper = lax.rem(place, 2) == 1
    return jnp.where(upper, low_part, high_part), jnp.where(upper, high_part, low_part)


def halo(sent):
    count = lax.axis_size("pipe")
    got = []
    for odd, value in enumerate(sent):
        pairs = [(i, i + 1) for i in range(odd, count - 1, 2)]
        got.append(lax.ppermute(value, "pipe", [p for i, j in pairs for p in ((i, j), (j, i))]))
    return got


def orders():
    found = []
    for axis in ("dp", "pipe"):
        stride = 1
        while stride < lax.axis_size(axis):
            found.append((axis, stride))
            stride *= 2
    other = list(found)
    if len(found) > 2:
        other[1], other[2] = found[2], found[1]
    return found, other


SPLIT = 4


def self_index(order):
    index = jnp.int32(0)
    for axis, stride in order[:SPLIT]:
        index = 2 * index + lax.rem(lax.div(lax.axis_index(axis), stride), 2)
    return index.astype(jnp.int32)


def exchange(value, axis, stride):
    count = lax.axis_size(axis)
    return lax.ppermute(value, axis, [(i, i ^ stride) for i in range(count)])


def added(a, b):
    return (a.astype(F32) + b.astype(F32)).astype(BF)


def sum_steps(keep, send, order):
    total = None
    for k, (axis, stride) in enumerate(order[:SPLIT]):
        got = exchange(send, axis, stride)
        yield None
        half = keep.shape[0] // 2
        if half:
            send, keep = added(keep[half:], got[half:]), added(keep[:half], got[:half])
        else:
            total = added(keep, got)
    for axis, stride in order[SPLIT:]:
        got = exchange(total, axis, stride)
        yield None
        total = added(total, got)
    for k, (axis, stride) in enumerate(reversed(order[:SPLIT])):
        got = exchange(total, axis, stride)
        yield (total, got)
        total = jnp.concatenate([total, got], axis=0)


def body(
    tokens,
    segments,
    cotangent,
    attention_in,
    attention_in_bias,
    attention_out,
    attention_out_bias,
    attention_gain,
    attention_shift,
    expand_weight,
    expand_bias,
    contract_weight,
    contract_bias,
    feed_gain,
    feed_shift,
):
    section_count = lax.axis_size("pipe")
    place = lax.axis_index("pipe").astype(jnp.int32)
    row_count, whole, features = tokens.shape
    span = whole + 2 * REACH + 2 * QB
    most = whole // QB
    cap = row_count * (whole + 2 * REACH) + ITEMS * 15
    cap = (cap + TB // 2 - 1) // (TB // 2) * (TB // 2) + 2 * QB
    tiles = row_count * 53
    vmem = pl.BlockSpec(memory_space=pltpu.VMEM)
    smem = pl.BlockSpec(memory_space=pltpu.SMEM)
    hbm = pl.BlockSpec(memory_space=pltpu.HBM)
    anywhere = pl.BlockSpec(memory_space=pl.ANY)
    weights = dict(
        win=attention_in,
        bin=attention_in_bias,
        wout=attention_out,
        bout=attention_out_bias,
        g1=attention_gain,
        s1=attention_shift,
        wup=expand_weight,
        bup=expand_bias,
        wdown=contract_weight,
        bdown=contract_bias,
        g2=feed_gain,
        s2=feed_shift,
    )
    weights = {k: (v, vmem if v.ndim == 2 else hbm) for k, v in weights.items()}
    weight_scratch = dict(
        s_win=pltpu.VMEM(attention_in.shape, BF),
        s_wout=pltpu.VMEM(attention_out.shape, BF),
        s_wup=pltpu.VMEM(expand_weight.shape, BF),
        s_wdown=pltpu.VMEM(contract_weight.shape, BF),
        weight_sems=pltpu.SemaphoreType.DMA((4 * attention_in.shape[0],)),
    )

    order0, order1 = orders()
    selves = [self_index(order0), self_index(order1)]
    pieces = 1 << SPLIT
    even, odd = halo(halo_sent(tokens[:, :REACH], tokens[:, whole - REACH :], place))
    token_rows = dict(own=(tokens, anywhere), even=(even, anywhere), odd=(odd, anywhere))
    choices = section_count * (DOCS + 1) ** 2
    planned = call(
        plan_kernel,
        (section_count, whole, span),
        dict(segments=(segments, vmem), place=(place.reshape(1), smem)),
        dict(table=((4 * ROOM + 4,), jnp.int32, smem)),
        dict(
            start=pltpu.SMEM((2 * (DOCS + 1),), jnp.int32),
            spent=pltpu.SMEM((2 * (DOCS + 1),), jnp.int32),
            low=pltpu.SMEM((2 * section_count,), jnp.int32),
            high=pltpu.SMEM((2 * section_count,), jnp.int32),
            best=pltpu.SMEM((choices,), jnp.int32),
            way=pltpu.SMEM((choices,), jnp.int32),
        ),
        1 << 20,
        4,
    )
    plan = dict(table=(planned.table, smem), place=(place.reshape(1), smem))
    sent = halo_sent(cotangent[:, :REACH], cotangent[:, whole - REACH :], place)
    even, odd = halo(lax.optimization_barrier((*sent, planned.table))[:2])
    cotangent_rows = dict(own=(cotangent, anywhere), even=(even, anywhere), odd=(odd, anywhere))
    kept_scratch = {"s_" + k: pltpu.VMEM((cap, c), t) for k, (c, t) in KEPT.items()}
    kept_scratch.update(weight_scratch)
    probs_shape = (tiles, 2, QB, 2 * QB)
    kept_scratch.update(
        s_probs=pltpu.VMEM(probs_shape, BF),
        s_window=pltpu.VMEM((row_count * span, features), BF),
        s_turned=pltpu.VMEM((features, whole), BF),
    )
    sems = dict(sems=pltpu.SemaphoreType.DMA((len(NAMES) + 1, MOST_BLOCKS)))
    moved = dict(
        s_rows=pltpu.VMEM((cap, features), BF),
        window_sems=pltpu.SemaphoreType.DMA((3 * row_count,)),
        in_sems=pltpu.SemaphoreType.DMA((MOST_BLOCKS,)),
        out_sems=pltpu.SemaphoreType.DMA((MOST_BLOCKS,)),
    )
    back_scratch = dict(
        s_total=pltpu.VMEM((AT_ALL, features), F32),
        s_small=pltpu.VMEM((V_ALL, 8, features), F32),
        s_ctx_grad=pltpu.VMEM((cap, features), BF),
        s_sum_grad=pltpu.VMEM((cap, features), F32),
        s_qkv_grad=pltpu.VMEM((cap, 3 * features), BF),
    )
    def pieces_out(extra):
        return ((pieces // 2, AT_ALL // pieces + extra, features), BF, vmem)

    rows_out = ((cap, features), BF, hbm)
    kept_out = {"o_" + k: ((cap, c), t, hbm) for k, (c, t) in KEPT.items()}
    kept_out.update(o_probs=(probs_shape, BF, hbm), o_next=rows_out)
    shape = (most, span)

    first = call(
        first_kernel,
        shape,
        plan | token_rows | weights,
        kept_out,
        kept_scratch | sems | moved,
        12 << 30,
        60,
    )
    kept_in = {"i_" + k: (getattr(first, "o_" + k), hbm) for k in NAMES + ("probs",)}
    second = call(
        second_kernel,
        shape,
        plan
        | cotangent_rows
        | kept_in
        | dict(x=(first.o_next, hbm), self=(jnp.stack(selves), smem))
        | weights,
        dict(
            o_keep0=pieces_out(16),
            o_send0=pieces_out(16),
            o_keep1=pieces_out(0),
            o_send1=pieces_out(0),
            o_out=rows_out,
            o_grad=rows_out,
        ),
        kept_scratch
        | back_scratch
        | sems
        | moved
        | dict(
            s_both=pltpu.VMEM((2 * V_ALL, features), F32),
            s_spread=pltpu.VMEM((pieces, 16, features), F32),
        ),
        60 << 30,
        57,
    )
    sums = [sum_steps(second.o_keep0, second.o_send0, order0)]
    sums.append(sum_steps(second.o_keep1, second.o_send1, order1))
    third = call(
        third_kernel,
        shape,
        plan | dict(out=(second.o_out, hbm), grad=(second.o_grad, hbm)),
        dict(
            o_own=((2, row_count, whole, features), BF, anywhere),
            o_left=((2, row_count, REACH, features), BF, anywhere),
            o_right=((2, row_count, REACH, features), BF, anywhere),
        ),
        moved
        | dict(
            s_sent=pltpu.VMEM((cap, features), BF),
            s_window=pltpu.VMEM((2, row_count * span, features), BF),
                window_sems=pltpu.SemaphoreType.DMA((2, 3 * row_count)),
        ),
        2 << 30,
        20,
    )
    even, odd = halo(halo_sent(third.o_left, third.o_right, place))
    upper = lax.rem(place, 2) == 1
    gap = jnp.zeros((2, row_count, whole - REACH, features), BF)
    low = jnp.concatenate([jnp.where(upper, even, odd), gap], axis=2)
    high = jnp.concatenate([gap, jnp.where(upper, odd, even)], axis=2)
    layer_output, input_grad = [third.o_own[k] + low[k] + high[k] for k in range(2)]
    for ends in zip(*sums):
        pass
    layers = attention_in.shape[0]

    def out(*shape):
        return ((layers,) + shape, F32, hbm)

    def small_out(*shape):
        return ((layers,) + shape, F32, vmem)

    vector = small_out(features)
    result = call(
        last_kernel,
        (),
        dict(
            self=(jnp.stack(selves), smem),
            keep0=(ends[0][0], vmem),
            got0=(ends[0][1], vmem),
            keep1=(ends[1][0], vmem),
            got1=(ends[1][1], vmem),
        ),
        dict(
            o_in=out(features, 3 * features),
            o_bin=small_out(2 * features),
            o_out=out(features, features),
            o_bout=vector,
            o_g1=vector,
            o_s1=vector,
            o_up=out(features, 2 * features),
            o_bup=small_out(2 * features),
            o_down=out(2 * features, features),
            o_bdown=vector,
            o_g2=vector,
            o_s2=vector,
        ),
        dict(
            s_pieces=pltpu.VMEM((2, pieces, AT_ALL // pieces + 16, features), BF),
            s_both=pltpu.VMEM((2 * V_ALL, features), F32),
            s_in=pltpu.VMEM((layers, features, 3 * features), F32),
            s_out=pltpu.VMEM((layers, features, features), F32),
            s_up=pltpu.VMEM((layers, features, 2 * features), F32),
            s_down=pltpu.VMEM((layers, 2 * features, features), F32),
            sems=pltpu.SemaphoreType.DMA((4 * layers,)),
        ),
        1 << 30,
        20,
    )
    return (layer_output, input_grad) + tuple(vars(result).values())


def solution(mesh):
    rows = P("dp", "pipe", None)
    return jax.shard_map(
        body,
        mesh=mesh,
        in_specs=(rows, P("dp", None), rows) + (P(),) * 12,
        out_specs=(rows, rows) + (P(),) * 12,
        check_vma=False,
    )
```

```python
from types import SimpleNamespace

import jax
import jax.numpy as jnp
from jax import lax
from jax.experimental import pallas as pl
from jax.experimental.pallas import tpu as pltpu
from jax.sharding import PartitionSpec as P

HEADS = 4
EPSILON = 1e-12
MASKED = -1e30
DOCS = 8
REACH = 320
TB = 512
MOST_BLOCKS = 8
QB = 128
LANES = 128

BF = jnp.bfloat16
F32 = jnp.float32

KEPT = dict(
    x=(256, BF),
    qkv=(768, BF),
    ctx=(256, BF),
    n1=(256, BF),
    r1=(128, F32),
    mid=(256, BF),
    act=(512, BF),
    slope=(512, BF),
    n2=(256, BF),
    r2=(128, F32),
)
NAMES = tuple(KEPT)


def dot(a, b):
    return jnp.dot(a, b, preferred_element_type=F32)


def dot_nt(a, b):
    return lax.dot_general(a, b, (((1,), (1,)), ((), ())), preferred_element_type=F32)


def dot_tn(a, b):
    return lax.dot_general(a, b, (((0,), (0,)), ((), ())), preferred_element_type=F32)


def fold(v):
    return v.reshape(-1, 8, v.shape[-1]).sum(0)


def rows_at(start, count):
    return pl.ds(pl.multiple_of(start, 16), count)


ITEMS = 2 * DOCS
ROOM = ITEMS + 1


class Plan:
    def __init__(self, r):
        self.table = r.table
        self.count, self.blocks, self.odd, self.end = (r.table[4 * ROOM + k] for k in range(4))

    def start(self, d):
        return self.table[d]

    def length(self, d):
        return self.table[ROOM + d]

    def offset(self, d):
        return self.table[2 * ROOM + d]

    def tile(self, d):
        return self.table[3 * ROOM + d]

    def size(self, d):
        return lax.shift_right_logical(self.length(d) + (QB - 1), 7)

    def over_docs(self, most, visit):
        def one(d, _):
            size = self.size(d)
            for n in range(1, most + 1):

                @pl.when(size == n)
                def _():
                    visit(d, n, self.length(d))

            return 0

        lax.fori_loop(0, self.count, one, 0)

    def over_groups(self, most, visit):
        def one(d):
            size = jnp.maximum(self.size(d), 2)
            after = self.size(d + 1)
            two = (size == 2) & (after >= 1) & (after <= 2)

            @pl.when(two)
            def _():
                visit([(d, 2), (d + 1, 2)])

            for n in range(2, most + 1):

                @pl.when((size == n) & jnp.logical_not(two))
                def _():
                    visit([(d, n)])

            return d + 1 + two.astype(jnp.int32)

        lax.while_loop(lambda d: d < self.count, one, jnp.int32(0))

    def over_blocks(self, visit):
        def one(b, _):
            visit(b, rows_at(b * TB, TB))
            return 0

        lax.fori_loop(0, self.blocks, one, 0)

        @pl.when(self.odd == 1)
        def _():
            visit(self.blocks, rows_at(self.blocks * TB, TB // 2))


def window_copies(win, span, own, low, high, sems, out):
    reach, whole = low.shape[1], own.shape[1]
    found = []
    for k in range(own.shape[0]):
        at = k * span
        for far, count in ((low, reach), (own, whole), (high, reach)):
            ends = (win.at[pl.ds(at, count)], far.at[k])
            found.append(pltpu.make_async_copy(*(ends if out else ends[::-1]), sems.at[len(found)]))
            at += count
    return found


def with_halos(r, win, span, act):
    upper = lax.bitwise_and(r.place[0], 1)
    for side in range(2):

        @pl.when(upper == 1 - side)
        def _():
            low, high = (r.odd, r.even) if side else (r.even, r.odd)
            act(window_copies(win, span, r.own, low, high, r.window_sems, False))


def clear_between(win, span, count):
    used = span - 2 * QB
    for k in range(count):
        clear(win, pl.ds(k * span + used, 2 * QB))


SPREAD = QB + 16


def pack(plan, most, win, dst):
    plan.over_blocks(lambda b, rows: clear(dst, rows))

    def visit(d, n, length):
        start, offset = plan.start(d), plan.offset(d)
        shift = lax.bitwise_and(start, 15)
        row = lax.broadcasted_iota(jnp.int32, (QB, SPREAD), 0)
        col = lax.broadcasted_iota(jnp.int32, (QB, SPREAD), 1)
        taken = col == row + shift
        kept = jnp.where(taken & (row < length - (n - 1) * QB), 1.0, 0.0).astype(BF)
        taken = jnp.where(taken, 1.0, 0.0).astype(BF)
        rows = [win[rows_at(start - shift + q * QB, SPREAD), :] for q in range(n)]
        picked = [dot(taken if q < n - 1 else kept, v).astype(BF) for q, v in enumerate(rows)]
        for q, v in enumerate(picked):
            dst[rows_at(offset + q * QB, QB), :] = v

    plan.over_docs(most, visit)


def unpack(plan, most, src, win, r, span, which):
    win[...] = jnp.zeros(win.shape, BF)
    clear(src, rows_at(plan.end, QB))

    def visit(d, n, length):
        start, offset = plan.start(d), plan.offset(d)
        shift = lax.bitwise_and(start, 15)
        row = lax.broadcasted_iota(jnp.int32, (SPREAD, QB), 0)
        col = lax.broadcasted_iota(jnp.int32, (SPREAD, QB), 1)
        taken = row == col + shift
        kept = jnp.where(taken & (col < length - (n - 1) * QB), 1.0, 0.0).astype(BF)
        taken = jnp.where(taken, 1.0, 0.0).astype(BF)
        rows = [src[rows_at(offset + q * QB, QB), :] for q in range(n)]
        placed = [dot(taken if q < n - 1 else kept, v) for q, v in enumerate(rows)]
        for q, v in enumerate(placed):
            at = rows_at(start - shift + q * QB, SPREAD)
            win[at, :] = (win[at, :].astype(F32) + v).astype(BF)

    plan.over_docs(most, visit)
    ends = [v.at[which] for v in (r.o_own, r.o_left, r.o_right)]
    found = window_copies(win, span, *ends, r.window_sems.at[which], True)
    started(found)
    return found


def clear(ref, rows):
    ref[rows, :] = jnp.zeros((rows.size, ref.shape[1]), ref.dtype)


def head_masks():
    lane = lax.broadcasted_iota(jnp.int32, (1, LANES), 1)
    low = (lane < LANES // 2).astype(F32)
    return low.astype(BF), (1.0 - low).astype(BF)


def two_heads(v, masks):
    return jnp.concatenate([v * masks[0], v * masks[1]], axis=0)


def turned_back(v):
    row = lax.broadcasted_iota(jnp.int32, (LANES, QB), 0)
    return jnp.where(row < LANES // 2, v[:, :QB], v[:, QB:]).T


def turn(src, dst, first, width):
    for k in range(width // LANES):
        at = slice(k * LANES, (k + 1) * LANES)
        for g in range(2):
            here = slice(g * LANES, (g + 1) * LANES)
            dst[here, first + at.start : first + at.stop] = src[at, here].T


def project(plan, kept, w, before=None):
    scaling = (256 // HEADS) ** (-0.5)
    bias = w.bin

    def visit(b, rows):
        if before is not None:
            before(b, rows)
        y = dot(kept.x[rows, :], w.win[...])
        queries = (y[:, 0:256] + bias[:, 0:256]).astype(BF)
        kept.qkv[rows, 0:256] = queries * jnp.asarray(scaling, BF)
        kept.qkv[rows, 256:512] = y[:, 256:512].astype(BF)
        kept.qkv[rows, 512:768] = (y[:, 512:768] + bias[:, 256:512]).astype(BF)
        clear(kept.ctx, rows)

    plan.over_blocks(visit)
    clear(kept.qkv, rows_at(plan.end, 2 * QB))


GROUPS = tuple(slice(g * LANES, (g + 1) * LANES) for g in range(2))


def shifted(cols, by):
    return slice(cols.start + by, cols.stop + by)


def attend(plan, most, kept, weights_low, values_turned):
    masks = head_masks()

    def visit(docs):
        offset = [plan.offset(d) for d, _ in docs]
        length = [plan.length(d) for d, _ in docs]
        tile = [plan.tile(d) for d, _ in docs]
        width = [n * QB for _, n in docs]
        firsts = [sum(width[:i]) for i in range(len(docs))]
        spans = [rows_at(o, v) for o, v in zip(offset, width)]
        for i, first in enumerate(firsts):
            turn(kept.qkv[spans[i], 512:768], values_turned, first, width[i])
        chains = [(i, q, g) for i, (_, n) in enumerate(docs) for q in range(n) for g in range(2)]
        column = lax.broadcasted_iota(jnp.int32, (1, 2 * QB), 1)
        column = lax.bitwise_and(column, QB - 1)
        row = lax.broadcasted_iota(jnp.int32, (QB, 2 * QB), 0)
        keys = [[kept.qkv[at, shifted(c, 256)] for c in GROUPS] for at in spans]
        turned = [[values_turned[c, f : f + v] for c in GROUPS] for f, v in zip(firsts, width)]
        queries = [kept.qkv[rows_at(offset[i] + q * QB, QB), GROUPS[g]] for i, q, g in chains]
        queries = [two_heads(v, masks) for v in queries]
        scores = [dot_nt(keys[i][g], v) for v, (i, _, g) in zip(queries, chains)]
        probs = []
        for v, (i, q, g) in zip(scores, chains):
            parts = []
            for k in range(docs[i][1]):
                part = v[k * QB : (k + 1) * QB, :]
                if k == docs[i][1] - 1 or docs[i][1] == 2:
                    part = jnp.where(row < length[i] - k * QB, part, MASKED)
                parts.append(part)
            v = jnp.concatenate(parts, axis=0)
            raised = jnp.exp(v - jnp.max(v, axis=0, keepdims=True))
            total = jnp.sum(raised, axis=0, keepdims=True)
            share = jnp.where(column < length[i] - q * QB, 1.0 / total, 0.0)
            probs.append((raised * share).astype(BF))
        contexts = [dot(turned[i][g], v) for v, (i, _, g) in zip(probs, chains)]
        contexts = [turned_back(v).astype(BF) for v in contexts]
        for v, context, (i, q, g) in zip(probs, contexts, chains):
            kept.ctx[rows_at(offset[i] + q * QB, QB), GROUPS[g]] = context
            n = docs[i][1]
            for k in range(n):
                weights_low[tile[i] + q * n + k, g] = v[k * QB : (k + 1) * QB, :]

    plan.over_groups(most, visit)


def normal(v):
    centred = v - jnp.mean(v, axis=1, keepdims=True)
    spread = jnp.mean(centred * centred, axis=1, keepdims=True)
    rate = lax.rsqrt(spread + EPSILON)
    return centred * rate, rate


def parts_of(rows, count):
    step = rows.size // count
    return [rows_at(rows.start + k * step, step) for k in range(count)]


def feed(plan, kept, w, out, each=None):
    def visit(b, rows):
        chains = parts_of(rows, 1)
        wout, wup, wdown = w.wout[...], w.wup[...], w.wdown[...]
        x = [kept.x[at, :] for at in chains]
        ctx = [kept.ctx[at, :] for at in chains]
        attn_sum = [u.astype(F32) + dot(v, wout) + w.bout for u, v in zip(x, ctx)]
        first = [normal(v) for v in attn_sum]
        mid_low = [(n * w.g1 + w.s1).astype(BF) for n, _ in first]
        pre_up = [dot(v, wup) + w.bup for v in mid_low]
        share = [0.5 + 0.5 * lax.erf(v * (0.5**0.5)) for v in pre_up]
        active = [(v * p).astype(BF) for v, p in zip(pre_up, share)]
        density = [jnp.exp(v * v * -0.5) * 0.3989422804014327 for v in pre_up]
        slope = [(p + v * q).astype(BF) for v, p, q in zip(pre_up, share, density)]
        feed_sum = [u.astype(F32) + dot(v, wdown) + w.bdown for u, v in zip(mid_low, active)]
        second = [normal(v) for v in feed_sum]
        for k, at in enumerate(chains):
            kept.n1[at, :] = first[k][0].astype(BF)
            kept.r1[at, :] = jnp.broadcast_to(first[k][1], (at.size, LANES))
            kept.mid[at, :] = mid_low[k]
            kept.act[at, :] = active[k]
            kept.slope[at, :] = slope[k]
            kept.n2[at, :] = second[k][0].astype(BF)
            kept.r2[at, :] = jnp.broadcast_to(second[k][1], (at.size, LANES))
            out[at, :] = (second[k][0] * w.g2 + w.s2).astype(BF)
        if each is not None:
            each(b, rows)

    plan.over_blocks(visit)


AT_OUT, AT_UP, AT_DOWN, AT_ALL = 768, 1024, 1536, 2048
V_IN, V_OUT, V_G1, V_S1, V_UP, V_DOWN, V_G2, V_S2, V_ALL = 0, 2, 3, 4, 5, 7, 8, 9, 16


def norm_back(upstream, n, rate, gain):
    e = upstream * gain
    inner = jnp.mean(e * n, axis=1, keepdims=True)
    return (e - jnp.mean(e, axis=1, keepdims=True) - n * inner) * rate


def doubled(v):
    return jnp.concatenate([v, v], axis=1)


def joined(values):
    return jnp.concatenate(values, axis=0) if len(values) > 1 else values[0]


def feed_back(plan, kept, w, upstream, r, before=None):
    total, small, ctx_grad, sum_grad = r.s_total, r.s_small, r.s_ctx_grad, r.s_sum_grad

    def visit(b, rows):
        if before is not None:
            before(b, rows)
        chains = parts_of(rows, 2)
        wout, wup, wdown = w.wout[...], w.wup[...], w.wdown[...]
        up = [upstream[at, :].astype(F32) for at in chains]
        n2 = [kept.n2[at, :].astype(F32) for at in chains]
        r2 = [doubled(kept.r2[at, :]) for at in chains]
        slope = [kept.slope[at, :] for at in chains]
        n1 = [kept.n1[at, :].astype(F32) for at in chains]
        r1 = [doubled(kept.r1[at, :]) for at in chains]
        act, mid, ctx = kept.act[rows, :], kept.mid[rows, :], kept.ctx[rows, :]
        feed_grad = [norm_back(u, n, v, w.g2) for u, n, v in zip(up, n2, r2)]
        feed_low = [v.astype(BF) for v in feed_grad]
        active_grad = [dot_nt(v, wdown) for v in feed_low]
        pre_grad = [(v * p.astype(F32)).astype(BF) for v, p in zip(active_grad, slope)]
        mid_grad = [dot_nt(v, wup) + u for v, u in zip(pre_grad, feed_grad)]
        mid_grad = [v.astype(BF).astype(F32) for v in mid_grad]
        attn_grad = [norm_back(u, n, v, w.g1) for u, n, v in zip(mid_grad, n1, r1)]
        attn_low = [v.astype(BF) for v in attn_grad]
        back = [dot_nt(v, wout).astype(BF) for v in attn_low]
        down_total = dot_tn(act, joined(feed_low))
        up_total = dot_tn(mid, joined(pre_grad))
        out_total = dot_tn(ctx, joined(attn_low))
        up_sums = fold(joined(pre_grad).astype(F32))
        sums = [
            (V_G2, fold(joined([u * n for u, n in zip(up, n2)]))),
            (V_S2, fold(joined(up))),
            (V_DOWN, fold(joined(feed_low).astype(F32))),
            (V_UP, up_sums[:, :256]),
            (V_UP + 1, up_sums[:, 256:]),
            (V_G1, fold(joined([u * n for u, n in zip(mid_grad, n1)]))),
            (V_S1, fold(joined(mid_grad))),
            (V_OUT, fold(joined(attn_low).astype(F32))),
        ]
        for k, at in enumerate(chains):
            sum_grad[at, :] = attn_grad[k]
            ctx_grad[at, :] = back[k]
        total[AT_DOWN:AT_ALL, :] += down_total
        total[AT_UP : AT_UP + 256, :] += up_total[:, :256]
        total[AT_UP + 256 : AT_DOWN, :] += up_total[:, 256:]
        total[AT_OUT:AT_UP, :] += out_total
        for line, v in sums:
            small[line] += v

    plan.over_blocks(visit)
    clear(ctx_grad, rows_at(plan.end, 2 * QB))


def attend_back(plan, most, kept, r):
    weights_low, ctx_grad, qkv_grad, keys_turned = r.s_probs, r.s_ctx_grad, r.s_qkv_grad, r.s_turned
    masks = head_masks()
    scaling = (256 // HEADS) ** (-0.5)
    plan.over_blocks(lambda b, rows: clear(qkv_grad, rows))

    def visit(docs):
        offset = [plan.offset(d) for d, _ in docs]
        tile = [plan.tile(d) for d, _ in docs]
        width = [n * QB for _, n in docs]
        firsts = [sum(width[:i]) for i in range(len(docs))]
        spans = [rows_at(o, v) for o, v in zip(offset, width)]
        for i, first in enumerate(firsts):
            turn(kept.qkv[spans[i], 256:512], keys_turned, first, width[i])
        chains = [(i, q, g) for i, (_, n) in enumerate(docs) for q in range(n) for g in range(2)]
        values = [[kept.qkv[at, shifted(c, 512)] for c in GROUPS] for at in spans]
        turned = [[keys_turned[c, f : f + v] for c in GROUPS] for f, v in zip(firsts, width)]
        queries = [kept.qkv[rows_at(offset[i] + q * QB, QB), GROUPS[g]] for i, q, g in chains]
        grads = [ctx_grad[rows_at(offset[i] + q * QB, QB), GROUPS[g]] for i, q, g in chains]
        probs = []
        for i, q, g in chains:
            n = docs[i][1]
            probs.append(joined([weights_low[tile[i] + q * n + k, g] for k in range(n)]))
        queries = [two_heads(v, masks) for v in queries]
        grads = [two_heads(v, masks) for v in grads]
        prob_grads = [dot_nt(values[i][g], v) for v, (i, _, g) in zip(grads, chains)]
        score_grads = []
        for low, v in zip(probs, prob_grads):
            full = low.astype(F32)
            inner = jnp.sum(full * v, axis=0, keepdims=True)
            score_grads.append((full * (v - inner)).astype(BF))
        query_grads = [dot(turned[i][g], v) for v, (i, _, g) in zip(score_grads, chains)]
        query_grads = [(turned_back(v) * scaling).astype(BF) for v in query_grads]
        sums = []
        for i in range(len(docs)):
            for g in range(2):
                mine = [k for k, c in enumerate(chains) if (c[0], c[2]) == (i, g)]
                sides = jnp.concatenate([score_grads[k] for k in mine], axis=1)
                key_sum = dot(sides, joined([queries[k] for k in mine])).astype(BF)
                sides = jnp.concatenate([probs[k] for k in mine], axis=1)
                value_sum = dot(sides, joined([grads[k] for k in mine])).astype(BF)
                sums.append((i, g, key_sum, value_sum))
        for i in range(len(docs)):
            for v, (own, q, g) in zip(query_grads, chains):
                if own == i:
                    qkv_grad[rows_at(offset[i] + q * QB, QB), GROUPS[g]] = v
            for own, g, key_sum, value_sum in sums:
                if own == i:
                    qkv_grad[spans[i], shifted(GROUPS[g], 256)] = key_sum
                    qkv_grad[spans[i], shifted(GROUPS[g], 512)] = value_sum

    plan.over_groups(most, visit)


def project_back(plan, kept, w, r, out, after=None):
    qkv_grad, sum_grad, total, small = r.s_qkv_grad, r.s_sum_grad, r.s_total, r.s_small

    def visit(b, rows):
        grad = qkv_grad[rows, :]
        sums = fold(grad.astype(F32))
        small[V_IN] += sums[:, :256]
        small[V_IN + 1] += sums[:, 512:]
        in_grad = dot_tn(kept.x[rows, :], grad)
        for k in range(3):
            total[256 * k : 256 * (k + 1), :] += in_grad[:, 256 * k : 256 * (k + 1)]
        hidden_grad = dot_nt(grad, w.win[...]) + sum_grad[rows, :]
        out[rows, :] = hidden_grad.astype(BF)
        if after is not None:
            after(b, rows)

    plan.over_blocks(visit)


def copies(r, kept, plan, out):
    def one(name, rows, sem):
        near = getattr(r if name == "probs" else kept, "s_probs" if name == "probs" else name)
        far = getattr(r, ("o_" if out else "i_") + name)
        ends = (near.at[rows], far.at[rows])
        return pltpu.make_async_copy(*(ends if out else ends[::-1]), sem)

    def of_block(names, b, rows):
        return [one(k, rows, r.sems.at[NAMES.index(k), b]) for k in names]

    def of_doc(d, n):
        return one("probs", pl.ds(plan.tile(d), max(n, 2) ** 2), r.sems.at[len(NAMES), 0])

    return of_block, of_doc


def by_block(source, target, sems):
    return lambda b, rows: [pltpu.make_async_copy(source.at[rows], target.at[rows], sems.at[b])]


def started(found):
    for c in found:
        c.start()


def waited(found):
    for c in found:
        c.wait()


def first_kernel(most, span, r):
    with_halos(r, r.s_window, span, started)
    w = layer_of(r, 0)
    plan = Plan(r)
    kept = SimpleNamespace(**{k: getattr(r, "s_" + k) for k in NAMES})
    of_block, of_doc = copies(r, kept, plan, True)
    leaving = by_block(r.s_rows, r.o_next, r.out_sems)
    clear_between(r.s_window, span, r.own.shape[0])
    with_halos(r, r.s_window, span, waited)
    pack(plan, most, r.s_window, kept.x)
    waited(w.coming)
    project(plan, kept, w)
    early, late = NAMES[:2], NAMES[2:]
    plan.over_blocks(lambda b, rows: started(of_block(early, b, rows)))
    attend(plan, most, kept, r.s_probs, r.s_turned)
    plan.over_docs(most, lambda d, n, length: of_doc(d, n).start())
    feed(plan, kept, w, r.s_rows, lambda b, rows: started(leaving(b, rows) + of_block(late, b, rows)))
    plan.over_blocks(lambda b, rows: waited(leaving(b, rows) + of_block(NAMES, b, rows)))
    plan.over_docs(most, lambda d, n, length: of_doc(d, n).wait())


def second_kernel(most, span, r):
    plan = Plan(r)
    kept = SimpleNamespace(**{k: getattr(r, "s_" + k) for k in NAMES})
    coming = by_block(r.x, kept.x, r.in_sems)
    plan.over_blocks(lambda b, rows: started(coming(b, rows)))
    w = layer_of(r, 1)
    with_halos(r, r.s_window, span, started)
    below = layer_of(r, 0)
    waited(w.coming)
    project(plan, kept, w, lambda b, rows: waited(coming(b, rows)))
    attend(plan, most, kept, r.s_probs, r.s_turned)
    leaving = by_block(r.s_ctx_grad, r.o_out, r.out_sems)
    feed(plan, kept, w, r.s_ctx_grad, lambda b, rows: started(leaving(b, rows)))
    clear_between(r.s_window, span, r.own.shape[0])
    with_halos(r, r.s_window, span, waited)
    pack(plan, most, r.s_window, r.s_rows)
    plan.over_blocks(lambda b, rows: waited(leaving(b, rows)))
    of_block, of_doc = copies(r, kept, plan, False)
    fed, projected, given = NAMES[2:], NAMES[1:2], NAMES[:1]
    waited(below.coming)
    leaving = by_block(r.s_rows, r.o_grad, r.out_sems)

    def one(step, _):
        w = weights_of(r, 1 - step)

        def at(which, act):
            pl.when(step == which)(act)

        def come(names, act):
            plan.over_blocks(lambda b, rows: act(of_block(names, b, rows)))

        def before(b, rows):
            at(1, lambda: waited(of_block(fed, b, rows)))

        def after(b, rows):
            at(1, lambda: started(leaving(b, rows)))

        clear_totals(r)
        feed_back(plan, kept, w, r.s_rows, r, before)
        at(0, lambda: come(fed, started))

        @pl.when(step == 1)
        def _():
            plan.over_docs(most, lambda d, n, length: of_doc(d, n).wait())
            come(projected, waited)

        attend_back(plan, most, kept, r)

        @pl.when(step == 0)
        def _():
            plan.over_docs(most, lambda d, n, length: of_doc(d, n).start())
            come(projected, started)

        at(1, lambda: come(given, waited))
        project_back(plan, kept, w, r, r.s_rows, after)
        at(0, lambda: come(given, started))
        r.s_both[pl.ds(pl.multiple_of((1 - step) * V_ALL, V_ALL), V_ALL), :] = r.s_small[...].sum(1)
        at(0, lambda: send_pieces(r, r.o_keep1, r.o_send1, r.self[1]))
        at(1, lambda: send_pieces(r, r.o_keep0, r.o_send0, r.self[0]))
        return 0

    lax.fori_loop(0, 2, one, 0)
    send_small(r, r.o_keep0, r.o_send0, r.self[0])
    plan.over_blocks(lambda b, rows: waited(leaving(b, rows)))


def third_kernel(most, span, r):
    plan = Plan(r)
    coming = [by_block(r.out, r.s_rows, r.in_sems), by_block(r.grad, r.s_sent, r.out_sems)]
    for one in coming:
        plan.over_blocks(lambda b, rows: started(one(b, rows)))
    found = []
    for k, (one, rows) in enumerate(zip(coming, (r.s_rows, r.s_sent))):
        plan.over_blocks(lambda b, at: waited(one(b, at)))
        found += unpack(plan, most, rows, r.s_window.at[k], r, span, k)
    waited(found)


VECTORS = dict(bin=512, bout=256, g1=256, s1=256, bup=512, bdown=256, g2=256, s2=256)


def weights_of(r, layer):
    near = dict(win=r.s_win, wout=r.s_wout, wup=r.s_wup, wdown=r.s_wdown)
    near = {k: v.at[layer] for k, v in near.items()}
    vectors = {k: r.s_vectors[layer, i : i + 1, 0:n] for i, (k, n) in enumerate(VECTORS.items())}
    return SimpleNamespace(**near, **vectors)


def layer_of(r, layer):
    pairs = ((r.win, r.s_win), (r.wout, r.s_wout), (r.wup, r.s_wup), (r.wdown, r.s_wdown))
    coming = []
    for k, (far, near) in enumerate(pairs):
        sem = r.weight_sems.at[4 * layer + k]
        coming.append(pltpu.make_async_copy(far.at[layer], near.at[layer], sem))
    started(coming)
    for i, (k, n) in enumerate(VECTORS.items()):
        r.s_vectors[layer, i : i + 1, 0:n] = getattr(r, k)[layer : layer + 1, :]
    w = weights_of(r, layer)
    w.coming = coming
    return w


def clear_totals(r):
    r.s_total[...] = jnp.zeros(r.s_total.shape, F32)
    r.s_small[...] = jnp.zeros(r.s_small.shape, F32)


def send_pieces(r, keep, send, own):
    half = keep.shape[0]
    rows = AT_ALL // (2 * half)
    for p in range(2 * half):
        out = keep if p < half else send
        at = pl.ds(pl.multiple_of(lax.bitwise_xor(jnp.int32(p), own) * rows, rows), rows)
        out[p % half, 0:rows, :] = r.s_total[at, :].astype(BF)


def send_small(r, keep, send, own):
    half = keep.shape[0]
    rows = AT_ALL // (2 * half)
    extra = keep.shape[1] - rows
    share = V_ALL // half
    for j in range(2 * half):
        line = r.s_both[j * share : (j + 1) * share, :]
        r.s_spread[j] = jnp.concatenate([line, jnp.zeros((extra - share, line.shape[1]), F32)], axis=0)
    for p in range(2 * half):
        out = keep if p < half else send
        out[p % half, rows : rows + extra, :] = r.s_spread[lax.bitwise_xor(jnp.int32(p), own)].astype(BF)


def last_kernel(r):
    half = r.keep0.shape[0]
    count = 2 * half
    rows = AT_ALL // count
    share = 2 * V_ALL // count
    big = (
        (0, AT_OUT, r.s_in, r.o_in),
        (AT_OUT, AT_UP, r.s_out, r.o_out),
        (AT_UP, AT_DOWN, r.s_up, r.o_up),
        (AT_DOWN, AT_ALL, r.s_down, r.o_down),
    )
    sent = []
    for layer, (keep, got) in enumerate(((r.keep0, r.got0), (r.keep1, r.got1))):
        for p in range(count):
            piece = lax.bitwise_xor(jnp.int32(p), r.self[layer])
            source = keep if p < half else got
            r.s_pieces[layer, piece, 0 : keep.shape[1], :] = source[p % half]
        for low, high, near, far in big:
            tall = near.shape[1]
            for at in range(low, high, rows):
                line, col = (at - low) % tall, (at - low) // tall * 256
                value = r.s_pieces[layer, at // rows, 0:rows, :].astype(F32)
                near[layer, line : line + rows, col : col + 256] = value
            copy = pltpu.make_async_copy(near.at[layer], far.at[layer], r.sems.at[len(sent)])
            copy.start()
            sent.append(copy)
    for j in range(count):
        tail = r.s_pieces[0, j, rows : rows + 16, :].astype(F32)
        r.s_both[j * share : (j + 1) * share, :] = tail[0:share]
    for layer in range(2):
        at = layer * V_ALL
        here = pl.ds(layer, 1)

        def line(k):
            return r.s_both[at + k : at + k + 1, :]

        r.o_bin[here, :] = jnp.concatenate([line(V_IN), line(V_IN + 1)], axis=1)
        r.o_bout[here, :] = line(V_OUT)
        r.o_g1[here, :] = line(V_G1)
        r.o_s1[here, :] = line(V_S1)
        r.o_bup[here, :] = jnp.concatenate([line(V_UP), line(V_UP + 1)], axis=1)
        r.o_bdown[here, :] = line(V_DOWN)
        r.o_g2[here, :] = line(V_G2)
        r.o_s2[here, :] = line(V_S2)
    waited(sent)


def call(kernel, consts, inputs, outputs, scratch, flops, megabytes):
    names = tuple(inputs) + tuple(outputs) + tuple(scratch)

    def run(*refs):
        kernel(*consts, SimpleNamespace(**dict(zip(names, refs))))

    got = pl.pallas_call(
        run,
        out_shape=[jax.ShapeDtypeStruct(s, d) for s, d, _ in outputs.values()],
        in_specs=[spec for _, spec in inputs.values()],
        out_specs=[spec for _, _, spec in outputs.values()],
        scratch_shapes=list(scratch.values()),
        compiler_params=pltpu.CompilerParams(vmem_limit_bytes=megabytes << 20),
        cost_estimate=pl.CostEstimate(flops=flops, bytes_accessed=8 << 20, transcendentals=0),
    )(*[a for a, _ in inputs.values()])
    return SimpleNamespace(**dict(zip(outputs, got)))


def plan_kernel(sections, whole, span, r):
    base = DOCS + 1
    huge = jnp.int32(1 << 20)
    for row in range(2):
        line = r.segments[row : row + 1, :]
        starts = [jnp.int32(0)]
        for doc in range(1, DOCS):
            below = jnp.where(line < doc, 1.0, 0.0)
            starts.append(jnp.sum(below).astype(jnp.int32))
        starts.append(jnp.int32(sections * whole))
        spent = jnp.int32(0)
        for doc in range(base):
            r.start[row * base + doc] = starts[doc]
            r.spent[row * base + doc] = spent
            if doc < DOCS:
                size = starts[doc + 1] - starts[doc]
                spent = spent + size + 230
                spent = spent + jnp.where(size > 2 * QB, 270, 0) + jnp.where(size > 3 * QB, 330, 0)
        for section in range(1, sections):
            low, high = jnp.int32(0), jnp.int32(0)
            for doc in range(base):
                away = starts[doc] - section * whole
                low = low + (away < -REACH).astype(jnp.int32)
                high = high + (away <= REACH).astype(jnp.int32)
            r.low[2 * section + row] = low
            r.high[2 * section + row] = high

    def over(section, visit, first):
        def outer(i, carry):
            inner = lambda j, c: visit(i, j, c)
            return lax.fori_loop(r.low[2 * section + 1], r.high[2 * section + 1], inner, carry)

        return lax.fori_loop(r.low[2 * section], r.high[2 * section], outer, first)

    def least(section, end, top, right):
        def visit(i, j, carry):
            cost, code = carry
            at = i * base + j
            step = end - r.spent[i] - r.spent[base + j]
            new = jnp.maximum(r.best[section * base * base + at], step)
            new = jnp.where((i <= top) & (j <= right), new, huge)
            better = new < cost
            return jnp.where(better, new, cost), jnp.where(better, at, code)

        return over(section, visit, (huge, jnp.int32(0)))

    for section in range(1, sections):

        def visit(i, j, carry):
            at = section * base * base + i * base + j
            end = r.spent[i] + r.spent[base + j]
            if section == 1:
                r.best[at] = end
            else:
                r.best[at], r.way[at] = least(section - 1, end, i, j)
            return carry

        over(section, visit, jnp.int32(0))
    _, code = least(sections - 1, r.spent[DOCS] + r.spent[base + DOCS], jnp.int32(DOCS), jnp.int32(DOCS))
    cuts = [jnp.int32(base * base - 1), code]
    for section in range(sections - 1, 1, -1):
        code = r.way[section * base * base + code]
        cuts.append(code)
    cuts = (cuts + [jnp.int32(0)])[::-1]
    place = r.place[0]
    low, high = jnp.int32(0), jnp.int32(0)
    for section in range(sections):
        low = jnp.where(place == section, cuts[section], low)
        high = jnp.where(place == section, cuts[section + 1], high)
    low, high = (low // base, low % base), (high // base, high % base)
    k, offset, tile = jnp.int32(0), jnp.int32(0), jnp.int32(0)
    table = r.table
    for row in range(2):

        def one(doc, carry):
            k, offset, tile = carry
            begin = r.start[row * base + doc]
            length = r.start[row * base + doc + 1] - begin
            table[k] = begin - place * whole + REACH + row * span
            table[ROOM + k] = length
            table[2 * ROOM + k] = offset
            table[3 * ROOM + k] = tile
            blocks = jnp.maximum(lax.shift_right_logical(length + (QB - 1), 7), 2)
            return k + 1, offset + lax.bitwise_and(length + 15, -16), tile + blocks * blocks

        k, offset, tile = lax.fori_loop(low[row], high[row], one, (k, offset, tile))
    table[ROOM + k] = 0
    halves = lax.shift_right_logical(offset + (TB // 2 - 1), 8)
    table[4 * ROOM] = k
    table[4 * ROOM + 1] = lax.shift_right_logical(halves, 1)
    table[4 * ROOM + 2] = lax.bitwise_and(halves, 1)
    table[4 * ROOM + 3] = halves * (TB // 2)


def halo_sent(low_part, high_part, place):
    upper = lax.rem(place, 2) == 1
    return jnp.where(upper, low_part, high_part), jnp.where(upper, high_part, low_part)


def halo(sent):
    count = lax.axis_size("pipe")
    got = []
    for odd, value in enumerate(sent):
        pairs = [(i, i + 1) for i in range(odd, count - 1, 2)]
        got.append(lax.ppermute(value, "pipe", [p for i, j in pairs for p in ((i, j), (j, i))]))
    return got


def orders():
    found = []
    for axis in ("dp", "pipe"):
        stride = 1
        while stride < lax.axis_size(axis):
            found.append((axis, stride))
            stride *= 2
    other = list(found)
    if len(found) > 2:
        other[1], other[2] = found[2], found[1]
    return found, other


SPLIT = 4


def self_index(order):
    index = jnp.int32(0)
    for axis, stride in order[:SPLIT]:
        index = 2 * index + lax.rem(lax.div(lax.axis_index(axis), stride), 2)
    return index.astype(jnp.int32)


def exchange(value, axis, stride):
    count = lax.axis_size(axis)
    return lax.ppermute(value, axis, [(i, i ^ stride) for i in range(count)])


def added(a, b):
    return (a.astype(F32) + b.astype(F32)).astype(BF)


def sum_steps(keep, send, order):
    total = None
    for k, (axis, stride) in enumerate(order[:SPLIT]):
        got = exchange(send, axis, stride)
        yield None
        half = keep.shape[0] // 2
        if half:
            send, keep = added(keep[half:], got[half:]), added(keep[:half], got[:half])
        else:
            total = added(keep, got)
    for axis, stride in order[SPLIT:]:
        got = exchange(total, axis, stride)
        yield None
        total = added(total, got)
    for k, (axis, stride) in enumerate(reversed(order[:SPLIT])):
        got = exchange(total, axis, stride)
        yield (total, got)
        total = jnp.concatenate([total, got], axis=0)


def body(
    tokens,
    segments,
    cotangent,
    attention_in,
    attention_in_bias,
    attention_out,
    attention_out_bias,
    attention_gain,
    attention_shift,
    expand_weight,
    expand_bias,
    contract_weight,
    contract_bias,
    feed_gain,
    feed_shift,
):
    section_count = lax.axis_size("pipe")
    place = lax.axis_index("pipe").astype(jnp.int32)
    row_count, whole, features = tokens.shape
    span = whole + 2 * REACH + 2 * QB
    most = whole // QB
    cap = row_count * (whole + 2 * REACH) + ITEMS * 15
    cap = (cap + TB // 2 - 1) // (TB // 2) * (TB // 2) + 2 * QB
    tiles = row_count * 53
    vmem = pl.BlockSpec(memory_space=pltpu.VMEM)
    smem = pl.BlockSpec(memory_space=pltpu.SMEM)
    hbm = pl.BlockSpec(memory_space=pltpu.HBM)
    anywhere = pl.BlockSpec(memory_space=pl.ANY)
    weights = dict(
        win=attention_in,
        bin=attention_in_bias,
        wout=attention_out,
        bout=attention_out_bias,
        g1=attention_gain,
        s1=attention_shift,
        wup=expand_weight,
        bup=expand_bias,
        wdown=contract_weight,
        bdown=contract_bias,
        g2=feed_gain,
        s2=feed_shift,
    )
    weights = {k: (v, vmem if v.ndim == 2 else hbm) for k, v in weights.items()}
    weight_scratch = dict(
        s_win=pltpu.VMEM(attention_in.shape, BF),
        s_wout=pltpu.VMEM(attention_out.shape, BF),
        s_wup=pltpu.VMEM(expand_weight.shape, BF),
        s_wdown=pltpu.VMEM(contract_weight.shape, BF),
        s_vectors=pltpu.VMEM((attention_in.shape[0], len(VECTORS), 2 * features), F32),
        weight_sems=pltpu.SemaphoreType.DMA((4 * attention_in.shape[0],)),
    )

    order0, order1 = orders()
    selves = [self_index(order0), self_index(order1)]
    pieces = 1 << SPLIT
    even, odd = halo(halo_sent(tokens[:, :REACH], tokens[:, whole - REACH :], place))
    token_rows = dict(own=(tokens, anywhere), even=(even, anywhere), odd=(odd, anywhere))
    choices = section_count * (DOCS + 1) ** 2
    planned = call(
        plan_kernel,
        (section_count, whole, span),
        dict(segments=(segments, vmem), place=(place.reshape(1), smem)),
        dict(table=((4 * ROOM + 4,), jnp.int32, smem)),
        dict(
            start=pltpu.SMEM((2 * (DOCS + 1),), jnp.int32),
            spent=pltpu.SMEM((2 * (DOCS + 1),), jnp.int32),
            low=pltpu.SMEM((2 * section_count,), jnp.int32),
            high=pltpu.SMEM((2 * section_count,), jnp.int32),
            best=pltpu.SMEM((choices,), jnp.int32),
            way=pltpu.SMEM((choices,), jnp.int32),
        ),
        1 << 20,
        4,
    )
    plan = dict(table=(planned.table, smem), place=(place.reshape(1), smem))
    sent = halo_sent(cotangent[:, :REACH], cotangent[:, whole - REACH :], place)
    even, odd = halo(lax.optimization_barrier((*sent, planned.table))[:2])
    cotangent_rows = dict(own=(cotangent, anywhere), even=(even, anywhere), odd=(odd, anywhere))
    kept_scratch = {"s_" + k: pltpu.VMEM((cap, c), t) for k, (c, t) in KEPT.items()}
    kept_scratch.update(weight_scratch)
    probs_shape = (tiles, 2, QB, 2 * QB)
    kept_scratch.update(
        s_probs=pltpu.VMEM(probs_shape, BF),
        s_window=pltpu.VMEM((row_count * span, features), BF),
        s_turned=pltpu.VMEM((features, whole), BF),
    )
    sems = dict(sems=pltpu.SemaphoreType.DMA((len(NAMES) + 1, MOST_BLOCKS)))
    moved = dict(
        s_rows=pltpu.VMEM((cap, features), BF),
        window_sems=pltpu.SemaphoreType.DMA((3 * row_count,)),
        in_sems=pltpu.SemaphoreType.DMA((MOST_BLOCKS,)),
        out_sems=pltpu.SemaphoreType.DMA((MOST_BLOCKS,)),
    )
    back_scratch = dict(
        s_total=pltpu.VMEM((AT_ALL, features), F32),
        s_small=pltpu.VMEM((V_ALL, 8, features), F32),
        s_ctx_grad=pltpu.VMEM((cap, features), BF),
        s_sum_grad=pltpu.VMEM((cap, features), F32),
        s_qkv_grad=pltpu.VMEM((cap, 3 * features), BF),
    )
    def pieces_out(extra):
        return ((pieces // 2, AT_ALL // pieces + extra, features), BF, vmem)

    rows_out = ((cap, features), BF, hbm)
    kept_out = {"o_" + k: ((cap, c), t, hbm) for k, (c, t) in KEPT.items()}
    kept_out.update(o_probs=(probs_shape, BF, hbm), o_next=rows_out)
    shape = (most, span)

    first = call(
        first_kernel,
        shape,
        plan | token_rows | weights,
        kept_out,
        kept_scratch | sems | moved,
        12 << 30,
        60,
    )
    kept_in = {"i_" + k: (getattr(first, "o_" + k), hbm) for k in NAMES + ("probs",)}
    second = call(
        second_kernel,
        shape,
        plan
        | cotangent_rows
        | kept_in
        | dict(x=(first.o_next, hbm), self=(jnp.stack(selves), smem))
        | weights,
        dict(
            o_keep0=pieces_out(16),
            o_send0=pieces_out(16),
            o_keep1=pieces_out(0),
            o_send1=pieces_out(0),
            o_out=rows_out,
            o_grad=rows_out,
        ),
        kept_scratch
        | back_scratch
        | sems
        | moved
        | dict(
            s_both=pltpu.VMEM((2 * V_ALL, features), F32),
            s_spread=pltpu.VMEM((pieces, 16, features), F32),
        ),
        60 << 30,
        57,
    )
    sums = [sum_steps(second.o_keep0, second.o_send0, order0)]
    sums.append(sum_steps(second.o_keep1, second.o_send1, order1))
    third = call(
        third_kernel,
        shape,
        plan | dict(out=(second.o_out, hbm), grad=(second.o_grad, hbm)),
        dict(
            o_own=((2, row_count, whole, features), BF, anywhere),
            o_left=((2, row_count, REACH, features), BF, anywhere),
            o_right=((2, row_count, REACH, features), BF, anywhere),
        ),
        moved
        | dict(
            s_sent=pltpu.VMEM((cap, features), BF),
            s_window=pltpu.VMEM((2, row_count * span, features), BF),
                window_sems=pltpu.SemaphoreType.DMA((2, 3 * row_count)),
        ),
        2 << 30,
        20,
    )
    even, odd = halo(halo_sent(third.o_left, third.o_right, place))
    upper = lax.rem(place, 2) == 1
    gap = jnp.zeros((2, row_count, whole - REACH, features), BF)
    low = jnp.concatenate([jnp.where(upper, even, odd), gap], axis=2)
    high = jnp.concatenate([gap, jnp.where(upper, odd, even)], axis=2)
    layer_output, input_grad = [third.o_own[k] + low[k] + high[k] for k in range(2)]
    for ends in zip(*sums):
        pass
    layers = attention_in.shape[0]

    def out(*shape):
        return ((layers,) + shape, F32, hbm)

    def small_out(*shape):
        return ((layers,) + shape, F32, vmem)

    vector = small_out(features)
    result = call(
        last_kernel,
        (),
        dict(
            self=(jnp.stack(selves), smem),
            keep0=(ends[0][0], vmem),
            got0=(ends[0][1], vmem),
            keep1=(ends[1][0], vmem),
            got1=(ends[1][1], vmem),
        ),
        dict(
            o_in=out(features, 3 * features),
            o_bin=small_out(2 * features),
            o_out=out(features, features),
            o_bout=vector,
            o_g1=vector,
            o_s1=vector,
            o_up=out(features, 2 * features),
            o_bup=small_out(2 * features),
            o_down=out(2 * features, features),
            o_bdown=vector,
            o_g2=vector,
            o_s2=vector,
        ),
        dict(
            s_pieces=pltpu.VMEM((2, pieces, AT_ALL // pieces + 16, features), BF),
            s_both=pltpu.VMEM((2 * V_ALL, features), F32),
            s_in=pltpu.VMEM((layers, features, 3 * features), F32),
            s_out=pltpu.VMEM((layers, features, features), F32),
            s_up=pltpu.VMEM((layers, features, 2 * features), F32),
            s_down=pltpu.VMEM((layers, 2 * features, features), F32),
            sems=pltpu.SemaphoreType.DMA((4 * layers,)),
        ),
        1 << 30,
        20,
    )
    return (layer_output, input_grad) + tuple(vars(result).values())


def solution(mesh):
    rows = P("dp", "pipe", None)
    return jax.shard_map(
        body,
        mesh=mesh,
        in_specs=(rows, P("dp", None), rows) + (P(),) * 12,
        out_specs=(rows, rows) + (P(),) * 12,
        check_vma=False,
    )
```

```python
from types import SimpleNamespace

import jax
import jax.numpy as jnp
from jax import lax
from jax.experimental import pallas as pl
from jax.experimental.pallas import tpu as pltpu
from jax.sharding import PartitionSpec as P

HEADS = 4
EPSILON = 1e-12
MASKED = -1e30
DOCS = 8
REACH = 320
TB = 640
TAIL = 256
MOST_BLOCKS = 8
QB = 128
LANES = 128

BF = jnp.bfloat16
F32 = jnp.float32

KEPT = dict(
    ahead=(BF, dict(x=256, qkv=768)),
    fed=(BF, dict(ctx=256, n1=256, mid=256, act=512, slope=512, n2=256)),
    rates=(F32, dict(r1=128, r2=128)),
)
NAMES = tuple(KEPT)


def kept_of(r):
    found = {}
    for name, (_, parts) in KEPT.items():
        first = 0
        for part, columns in parts.items():
            found[part] = getattr(r, "s_" + name).at[:, first : first + columns]
            first += columns
    return SimpleNamespace(**found)


def dot(a, b):
    return jnp.dot(a, b, preferred_element_type=F32)


def dot_nt(a, b):
    return lax.dot_general(a, b, (((1,), (1,)), ((), ())), preferred_element_type=F32)


def dot_tn(a, b):
    return lax.dot_general(a, b, (((0,), (0,)), ((), ())), preferred_element_type=F32)


def fold(v):
    return v.reshape(-1, 8, v.shape[-1]).sum(0)


def rows_at(start, count):
    return pl.ds(pl.multiple_of(start, 16), count)


ITEMS = 2 * DOCS
ROOM = ITEMS + 1
SELF = 4 * ROOM + 4


class Plan:
    def __init__(self, r):
        self.table = r.table
        self.count, self.blocks, self.odd, self.end = (r.table[4 * ROOM + k] for k in range(4))

    def start(self, d):
        return self.table[d]

    def length(self, d):
        return self.table[ROOM + d]

    def offset(self, d):
        return self.table[2 * ROOM + d]

    def tile(self, d):
        return self.table[3 * ROOM + d]

    def size(self, d):
        return lax.shift_right_logical(self.length(d) + (QB - 1), 7)

    def over_docs(self, most, visit):
        def one(d, _):
            size = self.size(d)
            for n in range(1, most + 1):

                @pl.when(size == n)
                def _():
                    visit(d, n, self.length(d))

            return 0

        lax.fori_loop(0, self.count, one, 0)

    def over_groups(self, most, visit):
        def one(d):
            size = jnp.maximum(self.size(d), 2)
            after = self.size(d + 1)
            two = (size == 2) & (after >= 1) & (after <= 2)

            @pl.when(two)
            def _():
                visit([(d, 2), (d + 1, 2)])

            for n in range(2, most + 1):

                @pl.when((size == n) & jnp.logical_not(two))
                def _():
                    visit([(d, n)])

            return d + 1 + two.astype(jnp.int32)

        lax.while_loop(lambda d: d < self.count, one, jnp.int32(0))

    def over_blocks(self, visit):
        def one(b, _):
            visit(b, rows_at(b * TB, TB))
            return 0

        lax.fori_loop(0, self.blocks, one, 0)

        @pl.when(self.odd == 1)
        def _():
            visit(self.blocks, rows_at(self.blocks * TB, TAIL))


def window_copies(win, span, own, low, high, sems, out):
    reach, whole = low.shape[1], own.shape[1]
    found = []
    for k in range(own.shape[0]):
        at = k * span
        for far, count in ((low, reach), (own, whole), (high, reach)):
            ends = (win.at[pl.ds(at, count)], far.at[k])
            found.append(pltpu.make_async_copy(*(ends if out else ends[::-1]), sems.at[len(found)]))
            at += count
    return found


def with_halos(r, win, span, act):
    upper = lax.bitwise_and(r.place[0], 1)
    for side in range(2):

        @pl.when(upper == 1 - side)
        def _():
            low, high = (r.odd, r.even) if side else (r.even, r.odd)
            act(window_copies(win, span, r.own, low, high, r.window_sems, False))


def clear_between(win, span, count):
    used = span - 2 * QB
    for k in range(count):
        clear(win, pl.ds(k * span + used, 2 * QB))


SPREAD = QB + 16


def pack(plan, most, win, dst):
    plan.over_blocks(lambda b, rows: clear(dst, rows))

    def visit(docs):
        row = lax.broadcasted_iota(jnp.int32, (QB, SPREAD), 0)
        col = lax.broadcasted_iota(jnp.int32, (QB, SPREAD), 1)
        parts = []
        for d, n in docs:
            start, length = plan.start(d), plan.length(d)
            shift = lax.bitwise_and(start, 15)
            whole = col == row + shift
            for q in range(n):
                inside = row < length - q * QB
                taken = jnp.where(whole & inside if q == n - 1 or n == 2 else whole, 1.0, 0.0)
                rows = win[rows_at(start - shift + q * QB, SPREAD), :]
                parts.append((taken.astype(BF), rows, plan.offset(d) + q * QB))
        picked = [dot(taken, rows).astype(BF) for taken, rows, _ in parts]
        for v, (_, _, at) in zip(picked, parts):
            dst[rows_at(at, QB), :] = v

    plan.over_groups(most, visit)


def unpack(plan, most, src, win, r, span, which):
    win[...] = jnp.zeros(win.shape, BF)
    clear(src, rows_at(plan.end, QB))

    def visit(d, n, length):
        start, offset = plan.start(d), plan.offset(d)
        shift = lax.bitwise_and(start, 15)
        row = lax.broadcasted_iota(jnp.int32, (SPREAD, QB), 0)
        col = lax.broadcasted_iota(jnp.int32, (SPREAD, QB), 1)
        taken = row == col + shift
        kept = jnp.where(taken & (col < length - (n - 1) * QB), 1.0, 0.0).astype(BF)
        taken = jnp.where(taken, 1.0, 0.0).astype(BF)
        rows = [src[rows_at(offset + q * QB, QB), :] for q in range(n)]
        placed = [dot(taken if q < n - 1 else kept, v) for q, v in enumerate(rows)]
        for q, v in enumerate(placed):
            at = rows_at(start - shift + q * QB, SPREAD)
            win[at, :] = (win[at, :].astype(F32) + v).astype(BF)

    plan.over_docs(most, visit)
    ends = [v.at[which] for v in (r.o_own, r.o_left, r.o_right)]
    found = window_copies(win, span, *ends, r.window_sems.at[which], True)
    started(found)
    return found


def clear(ref, rows):
    ref[rows, :] = jnp.zeros((rows.size, ref.shape[1]), ref.dtype)


def head_masks():
    lane = lax.broadcasted_iota(jnp.int32, (1, LANES), 1)
    low = (lane < LANES // 2).astype(F32)
    return low.astype(BF), (1.0 - low).astype(BF)


def two_heads(v, masks):
    return jnp.concatenate([v * masks[0], v * masks[1]], axis=0)


def turned_back(v):
    row = lax.broadcasted_iota(jnp.int32, (LANES, QB), 0)
    return jnp.where(row < LANES // 2, v[:, :QB], v[:, QB:]).astype(BF).T


def turn(src, dst, first, width):
    for k in range(width // LANES):
        at = slice(k * LANES, (k + 1) * LANES)
        for g in range(2):
            here = slice(g * LANES, (g + 1) * LANES)
            dst[here, first + at.start : first + at.stop] = src[at, here].T


def project(plan, kept, w, before=None):
    scaling = (256 // HEADS) ** (-0.5)
    bias = w.bin

    def visit(b, rows):
        if before is not None:
            before(b, rows)
        y = dot(kept.x[rows, :], w.win[...])
        queries = (y[:, 0:256] + bias[:, 0:256]).astype(BF)
        kept.qkv[rows, 0:256] = queries * jnp.asarray(scaling, BF)
        kept.qkv[rows, 256:512] = y[:, 256:512].astype(BF)
        kept.qkv[rows, 512:768] = (y[:, 512:768] + bias[:, 256:512]).astype(BF)
        clear(kept.ctx, rows)

    plan.over_blocks(visit)
    clear(kept.qkv, rows_at(plan.end, 2 * QB))


GROUPS = tuple(slice(g * LANES, (g + 1) * LANES) for g in range(2))


def shifted(cols, by):
    return slice(cols.start + by, cols.stop + by)


def attend(plan, most, kept, weights_low, values_turned):
    masks = head_masks()

    def visit(docs):
        offset = [plan.offset(d) for d, _ in docs]
        length = [plan.length(d) for d, _ in docs]
        tile = [plan.tile(d) for d, _ in docs]
        width = [n * QB for _, n in docs]
        firsts = [sum(width[:i]) for i in range(len(docs))]
        spans = [rows_at(o, v) for o, v in zip(offset, width)]
        for i, first in enumerate(firsts):
            turn(kept.qkv[spans[i], 512:768], values_turned, first, width[i])
        chains = [(i, q, g) for i, (_, n) in enumerate(docs) for q in range(n) for g in range(2)]
        column = lax.broadcasted_iota(jnp.int32, (1, 2 * QB), 1)
        column = lax.bitwise_and(column, QB - 1)
        row = lax.broadcasted_iota(jnp.int32, (QB, 2 * QB), 0)
        keys = [[kept.qkv[at, shifted(c, 256)] for c in GROUPS] for at in spans]
        turned = [[values_turned[c, f : f + v] for c in GROUPS] for f, v in zip(firsts, width)]
        queries = [kept.qkv[rows_at(offset[i] + q * QB, QB), GROUPS[g]] for i, q, g in chains]
        queries = [two_heads(v, masks) for v in queries]
        scores = [dot_nt(keys[i][g], v) for v, (i, _, g) in zip(queries, chains)]
        probs = []
        for v, (i, q, g) in zip(scores, chains):
            parts = []
            for k in range(docs[i][1]):
                part = v[k * QB : (k + 1) * QB, :]
                if k == docs[i][1] - 1 or docs[i][1] == 2:
                    part = jnp.where(row < length[i] - k * QB, part, MASKED)
                parts.append(part)
            v = jnp.concatenate(parts, axis=0)
            raised = jnp.exp(v - jnp.max(v, axis=0, keepdims=True))
            total = jnp.sum(raised, axis=0, keepdims=True)
            share = jnp.where(column < length[i] - q * QB, 1.0 / total, 0.0)
            probs.append((raised * share).astype(BF))
        contexts = [dot(turned[i][g], v) for v, (i, _, g) in zip(probs, chains)]
        contexts = [turned_back(v) for v in contexts]
        for v, context, (i, q, g) in zip(probs, contexts, chains):
            kept.ctx[rows_at(offset[i] + q * QB, QB), GROUPS[g]] = context
            n = docs[i][1]
            for k in range(n):
                weights_low[tile[i] + q * n + k, g] = v[k * QB : (k + 1) * QB, :]

    plan.over_groups(most, visit)


def normal(v):
    centred = v - jnp.mean(v, axis=1, keepdims=True)
    spread = jnp.mean(centred * centred, axis=1, keepdims=True)
    rate = lax.rsqrt(spread + EPSILON)
    return centred * rate, rate


def parts_of(rows, count):
    step = rows.size // count
    return [rows_at(rows.start + k * step, step) for k in range(count)]


def feed(plan, kept, w, out, each=None):
    def visit(b, rows):
        chains = parts_of(rows, 1)
        wout, wup, wdown = w.wout[...], w.wup[...], w.wdown[...]
        x = [kept.x[at, :] for at in chains]
        ctx = [kept.ctx[at, :] for at in chains]
        attn_sum = [u.astype(F32) + dot(v, wout) + w.bout for u, v in zip(x, ctx)]
        first = [normal(v) for v in attn_sum]
        mid_low = [(n * w.g1 + w.s1).astype(BF) for n, _ in first]
        pre_up = [dot(v, wup) + w.bup for v in mid_low]
        share = [0.5 + 0.5 * lax.erf(v * (0.5**0.5)) for v in pre_up]
        active = [(v * p).astype(BF) for v, p in zip(pre_up, share)]
        density = [jnp.exp(v * v * -0.5) * 0.3989422804014327 for v in pre_up]
        slope = [(p + v * q).astype(BF) for v, p, q in zip(pre_up, share, density)]
        feed_sum = [u.astype(F32) + dot(v, wdown) + w.bdown for u, v in zip(mid_low, active)]
        second = [normal(v) for v in feed_sum]
        for k, at in enumerate(chains):
            kept.n1[at, :] = first[k][0].astype(BF)
            kept.r1[at, :] = jnp.broadcast_to(first[k][1], (at.size, LANES))
            kept.mid[at, :] = mid_low[k]
            kept.act[at, :] = active[k]
            kept.slope[at, :] = slope[k]
            kept.n2[at, :] = second[k][0].astype(BF)
            kept.r2[at, :] = jnp.broadcast_to(second[k][1], (at.size, LANES))
            out[at, :] = (second[k][0] * w.g2 + w.s2).astype(BF)
        if each is not None:
            each(b, rows)

    plan.over_blocks(visit)


AT_OUT, AT_UP, AT_DOWN, AT_ALL = 768, 1024, 1536, 2048
V_IN, V_OUT, V_G1, V_S1, V_UP, V_DOWN, V_G2, V_S2, V_ALL = 0, 2, 3, 4, 5, 7, 8, 9, 16


def norm_back(upstream, n, rate, gain):
    e = upstream * gain
    inner = jnp.mean(e * n, axis=1, keepdims=True)
    return (e - jnp.mean(e, axis=1, keepdims=True) - n * inner) * rate


def doubled(v):
    return jnp.concatenate([v, v], axis=1)


def joined(values):
    return jnp.concatenate(values, axis=0) if len(values) > 1 else values[0]


def feed_back(plan, kept, w, upstream, r, before=None):
    total, small, ctx_grad, sum_grad = r.s_total, r.s_small, r.s_ctx_grad, r.s_sum_grad

    def visit(b, rows):
        if before is not None:
            before(b, rows)
        chains = parts_of(rows, 2)
        wout, wup, wdown = w.wout[...], w.wup[...], w.wdown[...]
        up = [upstream[at, :].astype(F32) for at in chains]
        n2 = [kept.n2[at, :].astype(F32) for at in chains]
        r2 = [doubled(kept.r2[at, :]) for at in chains]
        slope = [kept.slope[at, :] for at in chains]
        n1 = [kept.n1[at, :].astype(F32) for at in chains]
        r1 = [doubled(kept.r1[at, :]) for at in chains]
        act, mid, ctx = kept.act[rows, :], kept.mid[rows, :], kept.ctx[rows, :]
        feed_grad = [norm_back(u, n, v, w.g2) for u, n, v in zip(up, n2, r2)]
        feed_low = [v.astype(BF) for v in feed_grad]
        active_grad = [dot_nt(v, wdown) for v in feed_low]
        pre_grad = [(v * p.astype(F32)).astype(BF) for v, p in zip(active_grad, slope)]
        mid_grad = [dot_nt(v, wup) + u for v, u in zip(pre_grad, feed_grad)]
        mid_grad = [v.astype(BF).astype(F32) for v in mid_grad]
        attn_grad = [norm_back(u, n, v, w.g1) for u, n, v in zip(mid_grad, n1, r1)]
        attn_low = [v.astype(BF) for v in attn_grad]
        back = [dot_nt(v, wout).astype(BF) for v in attn_low]
        down_total = dot_tn(act, joined(feed_low))
        up_total = dot_tn(mid, joined(pre_grad))
        out_total = dot_tn(ctx, joined(attn_low))
        up_sums = fold(joined(pre_grad).astype(F32))
        sums = [
            (V_G2, fold(joined([u * n for u, n in zip(up, n2)]))),
            (V_S2, fold(joined(up))),
            (V_DOWN, fold(joined(feed_low).astype(F32))),
            (V_UP, up_sums[:, :256]),
            (V_UP + 1, up_sums[:, 256:]),
            (V_G1, fold(joined([u * n for u, n in zip(mid_grad, n1)]))),
            (V_S1, fold(joined(mid_grad))),
            (V_OUT, fold(joined(attn_low).astype(F32))),
        ]
        for k, at in enumerate(chains):
            sum_grad[at, :] = attn_grad[k]
            ctx_grad[at, :] = back[k]
        total[AT_DOWN:AT_ALL, :] += down_total
        total[AT_UP : AT_UP + 256, :] += up_total[:, :256]
        total[AT_UP + 256 : AT_DOWN, :] += up_total[:, 256:]
        total[AT_OUT:AT_UP, :] += out_total
        for line, v in sums:
            small[line] += v

    plan.over_blocks(visit)
    clear(ctx_grad, rows_at(plan.end, 2 * QB))


def attend_back(plan, most, kept, r):
    weights_low, ctx_grad, qkv_grad, keys_turned = r.s_probs, r.s_ctx_grad, r.s_qkv_grad, r.s_turned
    masks = head_masks()
    scaling = (256 // HEADS) ** (-0.5)
    plan.over_blocks(lambda b, rows: clear(qkv_grad, rows))

    def visit(docs):
        offset = [plan.offset(d) for d, _ in docs]
        tile = [plan.tile(d) for d, _ in docs]
        width = [n * QB for _, n in docs]
        firsts = [sum(width[:i]) for i in range(len(docs))]
        spans = [rows_at(o, v) for o, v in zip(offset, width)]
        for i, first in enumerate(firsts):
            turn(kept.qkv[spans[i], 256:512], keys_turned, first, width[i])
        chains = [(i, q, g) for i, (_, n) in enumerate(docs) for q in range(n) for g in range(2)]
        values = [[kept.qkv[at, shifted(c, 512)] for c in GROUPS] for at in spans]
        turned = [[keys_turned[c, f : f + v] for c in GROUPS] for f, v in zip(firsts, width)]
        queries = [kept.qkv[rows_at(offset[i] + q * QB, QB), GROUPS[g]] for i, q, g in chains]
        grads = [ctx_grad[rows_at(offset[i] + q * QB, QB), GROUPS[g]] for i, q, g in chains]
        probs = []
        for i, q, g in chains:
            n = docs[i][1]
            probs.append(joined([weights_low[tile[i] + q * n + k, g] for k in range(n)]))
        queries = [two_heads(v, masks) for v in queries]
        grads = [two_heads(v, masks) for v in grads]
        prob_grads = [dot_nt(values[i][g], v) for v, (i, _, g) in zip(grads, chains)]
        score_grads = []
        for low, v in zip(probs, prob_grads):
            full = low.astype(F32)
            inner = jnp.sum(full * v, axis=0, keepdims=True)
            score_grads.append((full * (v - inner)).astype(BF))
        query_grads = [dot(turned[i][g], v) for v, (i, _, g) in zip(score_grads, chains)]
        query_grads = [turned_back(v * scaling) for v in query_grads]
        sums = []
        for i in range(len(docs)):
            for g in range(2):
                mine = [k for k, c in enumerate(chains) if (c[0], c[2]) == (i, g)]
                sides = jnp.concatenate([score_grads[k] for k in mine], axis=1)
                key_sum = dot(sides, joined([queries[k] for k in mine])).astype(BF)
                sides = jnp.concatenate([probs[k] for k in mine], axis=1)
                value_sum = dot(sides, joined([grads[k] for k in mine])).astype(BF)
                sums.append((i, g, key_sum, value_sum))
        for i in range(len(docs)):
            for v, (own, q, g) in zip(query_grads, chains):
                if own == i:
                    qkv_grad[rows_at(offset[i] + q * QB, QB), GROUPS[g]] = v
            for own, g, key_sum, value_sum in sums:
                if own == i:
                    qkv_grad[spans[i], shifted(GROUPS[g], 256)] = key_sum
                    qkv_grad[spans[i], shifted(GROUPS[g], 512)] = value_sum

    plan.over_groups(most, visit)


def project_back(plan, kept, w, r, out, after=None):
    qkv_grad, sum_grad, total, small = r.s_qkv_grad, r.s_sum_grad, r.s_total, r.s_small

    def visit(b, rows):
        grad = qkv_grad[rows, :]
        sums = fold(grad.astype(F32))
        small[V_IN] += sums[:, :256]
        small[V_IN + 1] += sums[:, 512:]
        in_grad = dot_tn(kept.x[rows, :], grad)
        for k in range(3):
            total[256 * k : 256 * (k + 1), :] += in_grad[:, 256 * k : 256 * (k + 1)]
        hidden_grad = dot_nt(grad, w.win[...]) + sum_grad[rows, :]
        out[rows, :] = hidden_grad.astype(BF)
        if after is not None:
            after(b, rows)

    plan.over_blocks(visit)


def copies(r, plan, out):
    def one(near, far, sem):
        return pltpu.make_async_copy(*((near, far) if out else (far, near)), sem)

    def of_block(k, b, rows, first=0, columns=None):
        near, far = (getattr(r, side + NAMES[k]) for side in ("s_", "o_" if out else "i_"))
        at = (rows, slice(first, columns or near.shape[1]))
        return [one(near.at[at], far.at[at], r.sems.at[k + (3 if columns else 0), b])]

    def of_doc(d, n):
        at = pl.ds(plan.tile(d), max(n, 2) ** 2)
        return one(r.s_probs.at[at], (r.o_probs if out else r.i_probs).at[at], r.sems.at[4, 0])

    return of_block, of_doc


def by_block(source, target, sems):
    return lambda b, rows: [pltpu.make_async_copy(source.at[rows], target.at[rows], sems.at[b])]


def started(found):
    for c in found:
        c.start()


def waited(found):
    for c in found:
        c.wait()


def first_kernel(most, span, r):
    with_halos(r, r.s_window, span, started)
    w = layer_of(r, 0)
    plan = Plan(r)
    kept = kept_of(r)
    of_block, of_doc = copies(r, plan, True)
    leaving = by_block(r.s_rows, r.o_next, r.out_sems)
    clear_between(r.s_window, span, r.own.shape[0])
    with_halos(r, r.s_window, span, waited)
    pack(plan, most, r.s_window, kept.x)
    waited(w.coming)
    project(plan, kept, w)
    plan.over_blocks(lambda b, rows: started(of_block(0, b, rows)))
    attend(plan, most, kept, r.s_probs, r.s_turned)
    plan.over_docs(most, lambda d, n, length: of_doc(d, n).start())

    def late(b, rows):
        return leaving(b, rows) + of_block(1, b, rows) + of_block(2, b, rows)

    feed(plan, kept, w, r.s_rows, lambda b, rows: started(late(b, rows)))
    plan.over_blocks(lambda b, rows: waited(late(b, rows) + of_block(0, b, rows)))
    plan.over_docs(most, lambda d, n, length: of_doc(d, n).wait())


def second_kernel(most, span, r):
    plan = Plan(r)
    kept = kept_of(r)
    coming = by_block(r.x, kept.x, r.in_sems)
    plan.over_blocks(lambda b, rows: started(coming(b, rows)))
    w = layer_of(r, 1)
    with_halos(r, r.s_window, span, started)
    below = layer_of(r, 0)
    waited(w.coming)
    project(plan, kept, w, lambda b, rows: waited(coming(b, rows)))
    attend(plan, most, kept, r.s_probs, r.s_turned)
    leaving = by_block(r.s_ctx_grad, r.o_out, r.out_sems)
    feed(plan, kept, w, r.s_ctx_grad, lambda b, rows: started(leaving(b, rows)))
    clear_between(r.s_window, span, r.own.shape[0])
    with_halos(r, r.s_window, span, waited)
    pack(plan, most, r.s_window, r.s_rows)
    plan.over_blocks(lambda b, rows: waited(leaving(b, rows)))
    of_block, of_doc = copies(r, plan, False)

    def fed(b, rows):
        return of_block(1, b, rows) + of_block(2, b, rows)

    def projected(b, rows):
        return of_block(0, b, rows, 256)

    def given(b, rows):
        return of_block(0, b, rows, 0, 256)

    waited(below.coming)
    leaving = by_block(r.s_rows, r.o_grad, r.out_sems)

    def one(step, _):
        w = weights_of(r, 1 - step)

        def at(which, act):
            pl.when(step == which)(act)

        def come(found, act):
            plan.over_blocks(lambda b, rows: act(found(b, rows)))

        def before(b, rows):
            at(1, lambda: waited(fed(b, rows)))

        def after(b, rows):
            at(1, lambda: started(leaving(b, rows)))

        clear_totals(r)
        feed_back(plan, kept, w, r.s_rows, r, before)
        at(0, lambda: come(fed, started))

        @pl.when(step == 1)
        def _():
            plan.over_docs(most, lambda d, n, length: of_doc(d, n).wait())
            come(projected, waited)

        attend_back(plan, most, kept, r)

        @pl.when(step == 0)
        def _():
            plan.over_docs(most, lambda d, n, length: of_doc(d, n).start())
            come(projected, started)

        at(1, lambda: come(given, waited))
        project_back(plan, kept, w, r, r.s_rows, after)
        at(0, lambda: come(given, started))
        r.s_both[pl.ds(pl.multiple_of((1 - step) * V_ALL, V_ALL), V_ALL), :] = r.s_small[...].sum(1)
        at(0, lambda: send_pieces(r, r.o_keep1, r.o_send1, r.table[SELF + 1]))
        at(1, lambda: send_pieces(r, r.o_keep0, r.o_send0, r.table[SELF]))
        return 0

    lax.fori_loop(0, 2, one, 0)
    send_small(r, r.o_keep0, r.o_send0, r.table[SELF])
    plan.over_blocks(lambda b, rows: waited(leaving(b, rows)))


def third_kernel(most, span, r):
    plan = Plan(r)
    coming = [by_block(r.out, r.s_rows, r.in_sems), by_block(r.grad, r.s_sent, r.out_sems)]
    for one in coming:
        plan.over_blocks(lambda b, rows: started(one(b, rows)))
    found = []
    for k, (one, rows) in enumerate(zip(coming, (r.s_rows, r.s_sent))):
        plan.over_blocks(lambda b, at: waited(one(b, at)))
        found += unpack(plan, most, rows, r.s_window.at[k], r, span, k)
    waited(found)


VECTORS = dict(bin=512, bout=256, g1=256, s1=256, bup=512, bdown=256, g2=256, s2=256)


def weights_of(r, layer):
    near = dict(win=r.s_win, wout=r.s_wout, wup=r.s_wup, wdown=r.s_wdown)
    near = {k: v.at[layer] for k, v in near.items()}
    vectors = {k: r.s_vectors[layer, i : i + 1, 0:n] for i, (k, n) in enumerate(VECTORS.items())}
    return SimpleNamespace(**near, **vectors)


def layer_of(r, layer):
    pairs = ((r.win, r.s_win), (r.wout, r.s_wout), (r.wup, r.s_wup), (r.wdown, r.s_wdown))
    coming = []
    for k, (far, near) in enumerate(pairs):
        sem = r.weight_sems.at[4 * layer + k]
        coming.append(pltpu.make_async_copy(far.at[layer], near.at[layer], sem))
    started(coming)
    for i, (k, n) in enumerate(VECTORS.items()):
        r.s_vectors[layer, i : i + 1, 0:n] = getattr(r, k)[layer : layer + 1, :]
    w = weights_of(r, layer)
    w.coming = coming
    return w


def clear_totals(r):
    r.s_total[...] = jnp.zeros(r.s_total.shape, F32)
    r.s_small[...] = jnp.zeros(r.s_small.shape, F32)


def send_pieces(r, keep, send, own):
    half = keep.shape[0]
    rows = AT_ALL // (2 * half)
    for p in range(2 * half):
        out = keep if p < half else send
        at = pl.ds(pl.multiple_of(lax.bitwise_xor(jnp.int32(p), own) * rows, rows), rows)
        out[p % half, 0:rows, :] = r.s_total[at, :].astype(BF)


def send_small(r, keep, send, own):
    half = keep.shape[0]
    rows = AT_ALL // (2 * half)
    extra = keep.shape[1] - rows
    share = V_ALL // half
    for j in range(2 * half):
        line = r.s_both[j * share : (j + 1) * share, :]
        r.s_spread[j] = jnp.concatenate([line, jnp.zeros((extra - share, line.shape[1]), F32)], axis=0)
    for p in range(2 * half):
        out = keep if p < half else send
        out[p % half, rows : rows + extra, :] = r.s_spread[lax.bitwise_xor(jnp.int32(p), own)].astype(BF)


def last_kernel(r):
    half = r.keep0.shape[0]
    count = 2 * half
    rows = AT_ALL // count
    share = 2 * V_ALL // count
    big = (
        (0, AT_OUT, r.s_in, r.o_in),
        (AT_OUT, AT_UP, r.s_out, r.o_out),
        (AT_UP, AT_DOWN, r.s_up, r.o_up),
        (AT_DOWN, AT_ALL, r.s_down, r.o_down),
    )
    sent = []
    for layer, (keep, got) in enumerate(((r.keep0, r.got0), (r.keep1, r.got1))):
        for p in range(count):
            piece = lax.bitwise_xor(jnp.int32(p), r.table[SELF + layer])
            source = keep if p < half else got
            r.s_pieces[layer, piece, 0 : keep.shape[1], :] = source[p % half]
        for low, high, near, far in big:
            tall = near.shape[1]
            for at in range(low, high, rows):
                line, col = (at - low) % tall, (at - low) // tall * 256
                value = r.s_pieces[layer, at // rows, 0:rows, :].astype(F32)
                near[layer, line : line + rows, col : col + 256] = value
            copy = pltpu.make_async_copy(near.at[layer], far.at[layer], r.sems.at[len(sent)])
            copy.start()
            sent.append(copy)
    for j in range(count):
        tail = r.s_pieces[0, j, rows : rows + 16, :].astype(F32)
        r.s_both[j * share : (j + 1) * share, :] = tail[0:share]
    for layer in range(2):
        at = layer * V_ALL
        here = pl.ds(layer, 1)

        def line(k):
            return r.s_both[at + k : at + k + 1, :]

        r.o_bin[here, :] = jnp.concatenate([line(V_IN), line(V_IN + 1)], axis=1)
        r.o_bout[here, :] = line(V_OUT)
        r.o_g1[here, :] = line(V_G1)
        r.o_s1[here, :] = line(V_S1)
        r.o_bup[here, :] = jnp.concatenate([line(V_UP), line(V_UP + 1)], axis=1)
        r.o_bdown[here, :] = line(V_DOWN)
        r.o_g2[here, :] = line(V_G2)
        r.o_s2[here, :] = line(V_S2)
    waited(sent)


def call(kernel, consts, inputs, outputs, scratch, flops, megabytes):
    names = tuple(inputs) + tuple(outputs) + tuple(scratch)

    def run(*refs):
        kernel(*consts, SimpleNamespace(**dict(zip(names, refs))))

    got = pl.pallas_call(
        run,
        out_shape=[jax.ShapeDtypeStruct(s, d) for s, d, _ in outputs.values()],
        in_specs=[spec for _, spec in inputs.values()],
        out_specs=[spec for _, _, spec in outputs.values()],
        scratch_shapes=list(scratch.values()),
        compiler_params=pltpu.CompilerParams(vmem_limit_bytes=megabytes << 20),
        cost_estimate=pl.CostEstimate(flops=flops, bytes_accessed=8 << 20, transcendentals=0),
    )(*[a for a, _ in inputs.values()])
    return SimpleNamespace(**dict(zip(outputs, got)))


def plan_kernel(sections, whole, span, ways, r):
    base = DOCS + 1
    huge = jnp.int32(1 << 20)
    for row in range(2):
        line = r.segments[row : row + 1, :]
        starts = [jnp.int32(0)]
        for doc in range(1, DOCS):
            below = jnp.where(line < doc, 1.0, 0.0)
            starts.append(jnp.sum(below).astype(jnp.int32))
        starts.append(jnp.int32(sections * whole))
        spent = jnp.int32(0)
        for doc in range(base):
            r.start[row * base + doc] = starts[doc]
            r.spent[row * base + doc] = spent
            if doc < DOCS:
                size = starts[doc + 1] - starts[doc]
                spent = spent + size + 180
                spent = spent + jnp.where(size > 2 * QB, 160, 0) + jnp.where(size > 3 * QB, 190, 0)
        for section in range(1, sections):
            low, high = jnp.int32(0), jnp.int32(0)
            for doc in range(base):
                away = starts[doc] - section * whole
                low = low + (away < -REACH).astype(jnp.int32)
                high = high + (away <= REACH).astype(jnp.int32)
            r.low[2 * section + row] = low
            r.high[2 * section + row] = high

    def over(section, visit, first):
        def outer(i, carry):
            inner = lambda j, c: visit(i, j, c)
            return lax.fori_loop(r.low[2 * section + 1], r.high[2 * section + 1], inner, carry)

        return lax.fori_loop(r.low[2 * section], r.high[2 * section], outer, first)

    def least(section, end, top, right):
        def visit(i, j, carry):
            cost, code = carry
            at = i * base + j
            step = end - r.spent[i] - r.spent[base + j]
            new = jnp.maximum(r.best[section * base * base + at], step)
            new = jnp.where((i <= top) & (j <= right), new, huge)
            better = new < cost
            return jnp.where(better, new, cost), jnp.where(better, at, code)

        return over(section, visit, (huge, jnp.int32(0)))

    for section in range(1, sections):

        def visit(i, j, carry):
            at = section * base * base + i * base + j
            end = r.spent[i] + r.spent[base + j]
            if section == 1:
                r.best[at] = end
            else:
                r.best[at], r.way[at] = least(section - 1, end, i, j)
            return carry

        over(section, visit, jnp.int32(0))
    _, code = least(sections - 1, r.spent[DOCS] + r.spent[base + DOCS], jnp.int32(DOCS), jnp.int32(DOCS))
    cuts = [jnp.int32(base * base - 1), code]
    for section in range(sections - 1, 1, -1):
        code = r.way[section * base * base + code]
        cuts.append(code)
    cuts = (cuts + [jnp.int32(0)])[::-1]
    place = r.place[0]
    low, high = jnp.int32(0), jnp.int32(0)
    for section in range(sections):
        low = jnp.where(place == section, cuts[section], low)
        high = jnp.where(place == section, cuts[section + 1], high)
    low, high = (low // base, low % base), (high // base, high % base)
    table = r.table
    carry = (jnp.int32(0), jnp.int32(0), jnp.int32(0))
    for kind in range(2, whole // QB + 1):
        for row in range(2):

            def one(doc, carry):
                k, offset, tile = carry
                begin = r.start[row * base + doc]
                length = r.start[row * base + doc + 1] - begin
                blocks = jnp.maximum(lax.shift_right_logical(length + (QB - 1), 7), 2)
                table[k] = begin - place * whole + REACH + row * span
                table[ROOM + k] = length
                table[2 * ROOM + k] = offset
                table[3 * ROOM + k] = tile
                taken = (blocks == kind).astype(jnp.int32)
                offset = offset + taken * lax.bitwise_and(length + 15, -16)
                return k + taken, offset, tile + taken * blocks * blocks

            carry = lax.fori_loop(low[row], high[row], one, carry)
    k, offset, _ = carry
    table[ROOM + k] = 0
    blocks = offset // TB
    rest = offset - blocks * TB
    blocks = blocks + (rest > TAIL).astype(jnp.int32)
    odd = ((rest > 0) & (rest <= TAIL)).astype(jnp.int32)
    table[4 * ROOM] = k
    table[4 * ROOM + 1] = blocks
    table[4 * ROOM + 2] = odd
    table[4 * ROOM + 3] = blocks * TB + odd * TAIL
    for i, order in enumerate(ways):
        own = jnp.int32(0)
        for axis, stride in order[:SPLIT]:
            index = r.place[0] if axis == "pipe" else r.group[0]
            own = 2 * own + lax.bitwise_and(index // stride, 1)
        table[4 * ROOM + 4 + i] = own


def halo_sent(low_part, high_part, place):
    upper = lax.rem(place, 2) == 1
    return jnp.where(upper, low_part, high_part), jnp.where(upper, high_part, low_part)


def halo(sent):
    count = lax.axis_size("pipe")
    got = []
    for odd, value in enumerate(sent):
        pairs = [(i, i + 1) for i in range(odd, count - 1, 2)]
        got.append(lax.ppermute(value, "pipe", [p for i, j in pairs for p in ((i, j), (j, i))]))
    return got


def orders():
    found = []
    for axis in ("dp", "pipe"):
        stride = 1
        while stride < lax.axis_size(axis):
            found.append((axis, stride))
            stride *= 2
    other = list(found)
    if len(found) > 2:
        other[1], other[2] = found[2], found[1]
    return found, other


SPLIT = 4


def exchange(value, axis, stride):
    count = lax.axis_size(axis)
    return lax.ppermute(value, axis, [(i, i ^ stride) for i in range(count)])


def added(a, b):
    return (a.astype(F32) + b.astype(F32)).astype(BF)


def sum_steps(keep, send, order):
    total = None
    for k, (axis, stride) in enumerate(order[:SPLIT]):
        got = exchange(send, axis, stride)
        yield None
        half = keep.shape[0] // 2
        if half:
            send, keep = added(keep[half:], got[half:]), added(keep[:half], got[:half])
        else:
            total = added(keep, got)
    for axis, stride in order[SPLIT:]:
        got = exchange(total, axis, stride)
        yield None
        total = added(total, got)
    for k, (axis, stride) in enumerate(reversed(order[:SPLIT])):
        got = exchange(total, axis, stride)
        yield (total, got)
        total = jnp.concatenate([total, got], axis=0)


def body(
    tokens,
    segments,
    cotangent,
    attention_in,
    attention_in_bias,
    attention_out,
    attention_out_bias,
    attention_gain,
    attention_shift,
    expand_weight,
    expand_bias,
    contract_weight,
    contract_bias,
    feed_gain,
    feed_shift,
):
    section_count = lax.axis_size("pipe")
    place = lax.axis_index("pipe").astype(jnp.int32)
    row_count, whole, features = tokens.shape
    span = whole + 2 * REACH + 2 * QB
    most = whole // QB
    cap = row_count * (whole + 2 * REACH) + ITEMS * 15
    cap = (cap + TB - 1) // TB * TB + 2 * QB
    tiles = row_count * 53
    vmem = pl.BlockSpec(memory_space=pltpu.VMEM)
    smem = pl.BlockSpec(memory_space=pltpu.SMEM)
    hbm = pl.BlockSpec(memory_space=pltpu.HBM)
    anywhere = pl.BlockSpec(memory_space=pl.ANY)
    weights = dict(
        win=attention_in,
        bin=attention_in_bias,
        wout=attention_out,
        bout=attention_out_bias,
        g1=attention_gain,
        s1=attention_shift,
        wup=expand_weight,
        bup=expand_bias,
        wdown=contract_weight,
        bdown=contract_bias,
        g2=feed_gain,
        s2=feed_shift,
    )
    weights = {k: (v, vmem if v.ndim == 2 else hbm) for k, v in weights.items()}
    weight_scratch = dict(
        s_win=pltpu.VMEM(attention_in.shape, BF),
        s_wout=pltpu.VMEM(attention_out.shape, BF),
        s_wup=pltpu.VMEM(expand_weight.shape, BF),
        s_wdown=pltpu.VMEM(contract_weight.shape, BF),
        s_vectors=pltpu.VMEM((attention_in.shape[0], len(VECTORS), 2 * features), F32),
        weight_sems=pltpu.SemaphoreType.DMA((4 * attention_in.shape[0],)),
    )

    ways = orders()
    pieces = 1 << SPLIT
    even, odd = halo(halo_sent(tokens[:, :REACH], tokens[:, whole - REACH :], place))
    token_rows = dict(own=(tokens, anywhere), even=(even, anywhere), odd=(odd, anywhere))
    choices = section_count * (DOCS + 1) ** 2
    planned = call(
        plan_kernel,
        (section_count, whole, span, ways),
        dict(
            segments=(segments, vmem),
            place=(place.reshape(1), smem),
            group=(lax.axis_index("dp").astype(jnp.int32).reshape(1), smem),
        ),
        dict(table=((4 * ROOM + 6,), jnp.int32, smem)),
        dict(
            start=pltpu.SMEM((2 * (DOCS + 1),), jnp.int32),
            spent=pltpu.SMEM((2 * (DOCS + 1),), jnp.int32),
            low=pltpu.SMEM((2 * section_count,), jnp.int32),
            high=pltpu.SMEM((2 * section_count,), jnp.int32),
            best=pltpu.SMEM((choices,), jnp.int32),
            way=pltpu.SMEM((choices,), jnp.int32),
        ),
        1 << 20,
        4,
    )
    plan = dict(table=(planned.table, smem), place=(place.reshape(1), smem))
    sent = halo_sent(cotangent[:, :REACH], cotangent[:, whole - REACH :], place)
    even, odd = halo(lax.optimization_barrier((*sent, planned.table))[:2])
    cotangent_rows = dict(own=(cotangent, anywhere), even=(even, anywhere), odd=(odd, anywhere))
    kept_scratch = {"s_" + k: pltpu.VMEM((cap, sum(c.values())), t) for k, (t, c) in KEPT.items()}
    kept_scratch.update(weight_scratch)
    probs_shape = (tiles, 2, QB, 2 * QB)
    kept_scratch.update(
        s_probs=pltpu.VMEM(probs_shape, BF),
        s_window=pltpu.VMEM((row_count * span, features), BF),
        s_turned=pltpu.VMEM((features, whole), BF),
    )
    sems = dict(sems=pltpu.SemaphoreType.DMA((5, MOST_BLOCKS)))
    moved = dict(
        s_rows=pltpu.VMEM((cap, features), BF),
        window_sems=pltpu.SemaphoreType.DMA((3 * row_count,)),
        in_sems=pltpu.SemaphoreType.DMA((MOST_BLOCKS,)),
        out_sems=pltpu.SemaphoreType.DMA((MOST_BLOCKS,)),
    )
    back_scratch = dict(
        s_total=pltpu.VMEM((AT_ALL, features), F32),
        s_small=pltpu.VMEM((V_ALL, 8, features), F32),
        s_ctx_grad=pltpu.VMEM((cap, features), BF),
        s_sum_grad=pltpu.VMEM((cap, features), F32),
        s_qkv_grad=pltpu.VMEM((cap, 3 * features), BF),
    )
    def pieces_out(extra):
        return ((pieces // 2, AT_ALL // pieces + extra, features), BF, vmem)

    rows_out = ((cap, features), BF, hbm)
    kept_out = {"o_" + k: ((cap, sum(c.values())), t, hbm) for k, (t, c) in KEPT.items()}
    kept_out.update(o_probs=(probs_shape, BF, hbm), o_next=rows_out)
    shape = (most, span)

    first = call(
        first_kernel,
        shape,
        plan | token_rows | weights,
        kept_out,
        kept_scratch | sems | moved,
        12 << 30,
        60,
    )
    kept_in = {"i_" + k: (getattr(first, "o_" + k), hbm) for k in NAMES + ("probs",)}
    second = call(
        second_kernel,
        shape,
        plan
        | cotangent_rows
        | kept_in
        | dict(x=(first.o_next, hbm))
        | weights,
        dict(
            o_keep0=pieces_out(16),
            o_send0=pieces_out(16),
            o_keep1=pieces_out(0),
            o_send1=pieces_out(0),
            o_out=rows_out,
            o_grad=rows_out,
        ),
        kept_scratch
        | back_scratch
        | sems
        | moved
        | dict(
            s_both=pltpu.VMEM((2 * V_ALL, features), F32),
            s_spread=pltpu.VMEM((pieces, 16, features), F32),
        ),
        60 << 30,
        60,
    )
    sums = [sum_steps(second.o_keep0, second.o_send0, ways[0])]
    sums.append(sum_steps(second.o_keep1, second.o_send1, ways[1]))
    third = call(
        third_kernel,
        shape,
        plan | dict(out=(second.o_out, hbm), grad=(second.o_grad, hbm)),
        dict(
            o_own=((2, row_count, whole, features), BF, anywhere),
            o_left=((2, row_count, REACH, features), BF, anywhere),
            o_right=((2, row_count, REACH, features), BF, anywhere),
        ),
        moved
        | dict(
            s_sent=pltpu.VMEM((cap, features), BF),
            s_window=pltpu.VMEM((2, row_count * span, features), BF),
                window_sems=pltpu.SemaphoreType.DMA((2, 3 * row_count)),
        ),
        2 << 30,
        20,
    )
    even, odd = halo(halo_sent(third.o_left, third.o_right, place))
    upper = lax.rem(place, 2) == 1
    gap = jnp.zeros((2, row_count, whole - REACH, features), BF)
    low = jnp.concatenate([jnp.where(upper, even, odd), gap], axis=2)
    high = jnp.concatenate([gap, jnp.where(upper, odd, even)], axis=2)
    layer_output, input_grad = [third.o_own[k] + low[k] + high[k] for k in range(2)]
    for ends in zip(*sums):
        pass
    layers = attention_in.shape[0]

    def out(*shape):
        return ((layers,) + shape, F32, hbm)

    def small_out(*shape):
        return ((layers,) + shape, F32, vmem)

    vector = small_out(features)
    result = call(
        last_kernel,
        (),
        dict(
            table=(planned.table, smem),
            keep0=(ends[0][0], vmem),
            got0=(ends[0][1], vmem),
            keep1=(ends[1][0], vmem),
            got1=(ends[1][1], vmem),
        ),
        dict(
            o_in=out(features, 3 * features),
            o_bin=small_out(2 * features),
            o_out=out(features, features),
            o_bout=vector,
            o_g1=vector,
            o_s1=vector,
            o_up=out(features, 2 * features),
            o_bup=small_out(2 * features),
            o_down=out(2 * features, features),
            o_bdown=vector,
            o_g2=vector,
            o_s2=vector,
        ),
        dict(
            s_pieces=pltpu.VMEM((2, pieces, AT_ALL // pieces + 16, features), BF),
            s_both=pltpu.VMEM((2 * V_ALL, features), F32),
            s_in=pltpu.VMEM((layers, features, 3 * features), F32),
            s_out=pltpu.VMEM((layers, features, features), F32),
            s_up=pltpu.VMEM((layers, features, 2 * features), F32),
            s_down=pltpu.VMEM((layers, 2 * features, features), F32),
            sems=pltpu.SemaphoreType.DMA((4 * layers,)),
        ),
        1 << 30,
        20,
    )
    return (layer_output, input_grad) + tuple(vars(result).values())


def solution(mesh):
    rows = P("dp", "pipe", None)
    return jax.shard_map(
        body,
        mesh=mesh,
        in_specs=(rows, P("dp", None), rows) + (P(),) * 12,
        out_specs=(rows, rows) + (P(),) * 12,
        check_vma=False,
    )
```

```python
from types import SimpleNamespace

import jax
import jax.numpy as jnp
from jax import lax
from jax.experimental import pallas as pl
from jax.experimental.pallas import tpu as pltpu
from jax.sharding import PartitionSpec as P

HEADS = 4
EPSILON = 1e-12
MASKED = -1e30
DOCS = 8
REACH = 320
TB = 640
TAIL = 256
MOST_BLOCKS = 8
QB = 128
LANES = 128

BF = jnp.bfloat16
F32 = jnp.float32

KEPT = dict(
    ahead=(BF, dict(x=256, qkv=768)),
    fed=(BF, dict(ctx=256, n1=256, mid=256, act=512, slope=512, n2=256)),
    rates=(F32, dict(r1=128, r2=128)),
)
NAMES = tuple(KEPT)


def kept_of(r):
    found = {}
    for name, (_, parts) in KEPT.items():
        first = 0
        for part, columns in parts.items():
            found[part] = getattr(r, "s_" + name).at[:, first : first + columns]
            first += columns
    return SimpleNamespace(**found)


def dot(a, b):
    return jnp.dot(a, b, preferred_element_type=F32)


def dot_nt(a, b):
    return lax.dot_general(a, b, (((1,), (1,)), ((), ())), preferred_element_type=F32)


def dot_tn(a, b):
    return lax.dot_general(a, b, (((0,), (0,)), ((), ())), preferred_element_type=F32)


def fold(v):
    return v.reshape(-1, 8, v.shape[-1]).sum(0)


def rows_at(start, count):
    return pl.ds(pl.multiple_of(start, 16), count)


ITEMS = 2 * DOCS
ROOM = ITEMS + 1
SELF = 4 * ROOM + 4


class Plan:
    def __init__(self, r):
        self.table = r.table
        self.count, self.blocks, self.odd, self.end = (r.table[4 * ROOM + k] for k in range(4))

    def start(self, d):
        return self.table[d]

    def length(self, d):
        return self.table[ROOM + d]

    def offset(self, d):
        return self.table[2 * ROOM + d]

    def tile(self, d):
        return self.table[3 * ROOM + d]

    def size(self, d):
        return lax.shift_right_logical(self.length(d) + (QB - 1), 7)

    def over_docs(self, most, visit):
        def one(d, _):
            size = self.size(d)
            for n in range(1, most + 1):

                @pl.when(size == n)
                def _():
                    visit(d, n, self.length(d))

            return 0

        lax.fori_loop(0, self.count, one, 0)

    def over_groups(self, most, visit):
        def one(d):
            size = jnp.maximum(self.size(d), 2)
            after = self.size(d + 1)
            two = (size == 2) & (after >= 1) & (after <= 2)

            @pl.when(two)
            def _():
                visit([(d, 2), (d + 1, 2)])

            for n in range(2, most + 1):

                @pl.when((size == n) & jnp.logical_not(two))
                def _():
                    visit([(d, n)])

            return d + 1 + two.astype(jnp.int32)

        lax.while_loop(lambda d: d < self.count, one, jnp.int32(0))

    def over_blocks(self, visit):
        def one(b, _):
            visit(b, rows_at(b * TB, TB))
            return 0

        lax.fori_loop(0, self.blocks, one, 0)

        @pl.when(self.odd == 1)
        def _():
            visit(self.blocks, rows_at(self.blocks * TB, TAIL))


def window_copies(win, span, own, low, high, sems, out):
    reach, whole = low.shape[1], own.shape[1]
    found = []
    for k in range(own.shape[0]):
        at = k * span
        for far, count in ((low, reach), (own, whole), (high, reach)):
            ends = (win.at[pl.ds(at, count)], far.at[k])
            found.append(pltpu.make_async_copy(*(ends if out else ends[::-1]), sems.at[len(found)]))
            at += count
    return found


def with_halos(r, win, span, act):
    upper = lax.bitwise_and(r.place[0], 1)
    for side in range(2):

        @pl.when(upper == 1 - side)
        def _():
            low, high = (r.odd, r.even) if side else (r.even, r.odd)
            act(window_copies(win, span, r.own, low, high, r.window_sems, False))


def clear_between(win, span, count):
    used = span - 2 * QB
    for k in range(count):
        clear(win, pl.ds(k * span + used, 2 * QB))


SPREAD = QB + 16


def pack(plan, most, win, dst):
    plan.over_blocks(lambda b, rows: clear(dst, rows))

    def visit(docs):
        row = lax.broadcasted_iota(jnp.int32, (QB, SPREAD), 0)
        col = lax.broadcasted_iota(jnp.int32, (QB, SPREAD), 1)
        parts = []
        for d, n in docs:
            start, length = plan.start(d), plan.length(d)
            shift = lax.bitwise_and(start, 15)
            whole = col == row + shift
            for q in range(n):
                inside = row < length - q * QB
                taken = jnp.where(whole & inside if q == n - 1 or n == 2 else whole, 1.0, 0.0)
                rows = win[rows_at(start - shift + q * QB, SPREAD), :]
                parts.append((taken.astype(BF), rows, plan.offset(d) + q * QB))
        picked = [dot(taken, rows).astype(BF) for taken, rows, _ in parts]
        for v, (_, _, at) in zip(picked, parts):
            dst[rows_at(at, QB), :] = v

    plan.over_groups(most, visit)


def unpack(plan, most, src, win, r, span, which):
    win[...] = jnp.zeros(win.shape, BF)
    clear(src, rows_at(plan.end, QB))

    def visit(d, n, length):
        start, offset = plan.start(d), plan.offset(d)
        shift = lax.bitwise_and(start, 15)
        row = lax.broadcasted_iota(jnp.int32, (SPREAD, QB), 0)
        col = lax.broadcasted_iota(jnp.int32, (SPREAD, QB), 1)
        taken = row == col + shift
        kept = jnp.where(taken & (col < length - (n - 1) * QB), 1.0, 0.0).astype(BF)
        taken = jnp.where(taken, 1.0, 0.0).astype(BF)
        rows = [src[rows_at(offset + q * QB, QB), :] for q in range(n)]
        placed = [dot(taken if q < n - 1 else kept, v) for q, v in enumerate(rows)]
        for q, v in enumerate(placed):
            at = rows_at(start - shift + q * QB, SPREAD)
            win[at, :] = (win[at, :].astype(F32) + v).astype(BF)

    plan.over_docs(most, visit)
    ends = [v.at[which] for v in (r.o_own, r.o_left, r.o_right)]
    found = window_copies(win, span, *ends, r.window_sems.at[which], True)
    started(found)
    return found


def clear(ref, rows):
    ref[rows, :] = jnp.zeros((rows.size, ref.shape[1]), ref.dtype)


def head_masks():
    lane = lax.broadcasted_iota(jnp.int32, (1, LANES), 1)
    low = (lane < LANES // 2).astype(F32)
    return low.astype(BF), (1.0 - low).astype(BF)


def two_heads(v, masks):
    return jnp.concatenate([v * masks[0], v * masks[1]], axis=0)


def turned_back(v):
    row = lax.broadcasted_iota(jnp.int32, (LANES, QB), 0)
    return jnp.where(row < LANES // 2, v[:, :QB], v[:, QB:]).astype(BF).T


def turn(src, dst, first, width):
    for k in range(width // LANES):
        at = slice(k * LANES, (k + 1) * LANES)
        for g in range(2):
            here = slice(g * LANES, (g + 1) * LANES)
            dst[here, first + at.start : first + at.stop] = src[at, here].T


def project(plan, kept, w, before=None):
    scaling = (256 // HEADS) ** (-0.5)
    bias = w.bin

    def visit(b, rows):
        if before is not None:
            before(b, rows)
        y = dot(kept.x[rows, :], w.win[...])
        queries = (y[:, 0:256] + bias[:, 0:256]).astype(BF)
        kept.qkv[rows, 0:256] = queries * jnp.asarray(scaling, BF)
        kept.qkv[rows, 256:512] = y[:, 256:512].astype(BF)
        kept.qkv[rows, 512:768] = (y[:, 512:768] + bias[:, 256:512]).astype(BF)
        clear(kept.ctx, rows)

    plan.over_blocks(visit)
    clear(kept.qkv, rows_at(plan.end, 2 * QB))


GROUPS = tuple(slice(g * LANES, (g + 1) * LANES) for g in range(2))


def shifted(cols, by):
    return slice(cols.start + by, cols.stop + by)


def attend(plan, most, kept, weights_low, values_turned):
    masks = head_masks()

    def visit(docs):
        offset = [plan.offset(d) for d, _ in docs]
        length = [plan.length(d) for d, _ in docs]
        tile = [plan.tile(d) for d, _ in docs]
        width = [n * QB for _, n in docs]
        firsts = [sum(width[:i]) for i in range(len(docs))]
        spans = [rows_at(o, v) for o, v in zip(offset, width)]
        for i, first in enumerate(firsts):
            turn(kept.qkv[spans[i], 512:768], values_turned, first, width[i])
        chains = [(i, q, g) for i, (_, n) in enumerate(docs) for q in range(n) for g in range(2)]
        column = lax.broadcasted_iota(jnp.int32, (1, 2 * QB), 1)
        column = lax.bitwise_and(column, QB - 1)
        row = lax.broadcasted_iota(jnp.int32, (QB, 2 * QB), 0)
        keys = [[kept.qkv[at, shifted(c, 256)] for c in GROUPS] for at in spans]
        turned = [[values_turned[c, f : f + v] for c in GROUPS] for f, v in zip(firsts, width)]
        queries = [kept.qkv[rows_at(offset[i] + q * QB, QB), GROUPS[g]] for i, q, g in chains]
        queries = [two_heads(v, masks) for v in queries]
        scores = [dot_nt(keys[i][g], v) for v, (i, _, g) in zip(queries, chains)]
        probs = []
        for v, (i, q, g) in zip(scores, chains):
            parts = []
            for k in range(docs[i][1]):
                part = v[k * QB : (k + 1) * QB, :]
                if k == docs[i][1] - 1 or docs[i][1] == 2:
                    part = jnp.where(row < length[i] - k * QB, part, MASKED)
                parts.append(part)
            v = jnp.concatenate(parts, axis=0)
            raised = jnp.exp(v - jnp.max(v, axis=0, keepdims=True))
            total = jnp.sum(raised, axis=0, keepdims=True)
            share = jnp.where(column < length[i] - q * QB, 1.0 / total, 0.0)
            probs.append((raised * share).astype(BF))
        contexts = [dot(turned[i][g], v) for v, (i, _, g) in zip(probs, chains)]
        contexts = [turned_back(v) for v in contexts]
        for v, context, (i, q, g) in zip(probs, contexts, chains):
            kept.ctx[rows_at(offset[i] + q * QB, QB), GROUPS[g]] = context
            n = docs[i][1]
            for k in range(n):
                weights_low[tile[i] + q * n + k, g] = v[k * QB : (k + 1) * QB, :]

    plan.over_groups(most, visit)


def normal(v):
    centred = v - jnp.mean(v, axis=1, keepdims=True)
    spread = jnp.mean(centred * centred, axis=1, keepdims=True)
    rate = lax.rsqrt(spread + EPSILON)
    return centred * rate, rate


def parts_of(rows, count):
    step = rows.size // count
    return [rows_at(rows.start + k * step, step) for k in range(count)]


def feed(plan, kept, w, out, each=None):
    def visit(b, rows):
        chains = parts_of(rows, 1)
        wout, wup, wdown = w.wout[...], w.wup[...], w.wdown[...]
        x = [kept.x[at, :] for at in chains]
        ctx = [kept.ctx[at, :] for at in chains]
        attn_sum = [u.astype(F32) + dot(v, wout) + w.bout for u, v in zip(x, ctx)]
        first = [normal(v) for v in attn_sum]
        mid_low = [(n * w.g1 + w.s1).astype(BF) for n, _ in first]
        pre_up = [dot(v, wup) + w.bup for v in mid_low]
        share = [0.5 + 0.5 * lax.erf(v * (0.5**0.5)) for v in pre_up]
        active = [(v * p).astype(BF) for v, p in zip(pre_up, share)]
        density = [jnp.exp(v * v * -0.5) * 0.3989422804014327 for v in pre_up]
        slope = [(p + v * q).astype(BF) for v, p, q in zip(pre_up, share, density)]
        feed_sum = [u.astype(F32) + dot(v, wdown) + w.bdown for u, v in zip(mid_low, active)]
        second = [normal(v) for v in feed_sum]
        for k, at in enumerate(chains):
            kept.n1[at, :] = first[k][0].astype(BF)
            kept.r1[at, :] = jnp.broadcast_to(first[k][1], (at.size, LANES))
            kept.mid[at, :] = mid_low[k]
            kept.act[at, :] = active[k]
            kept.slope[at, :] = slope[k]
            kept.n2[at, :] = second[k][0].astype(BF)
            kept.r2[at, :] = jnp.broadcast_to(second[k][1], (at.size, LANES))
            out[at, :] = (second[k][0] * w.g2 + w.s2).astype(BF)
        if each is not None:
            each(b, rows)

    plan.over_blocks(visit)


AT_OUT, AT_UP, AT_DOWN, AT_ALL = 768, 1024, 1536, 2048
V_IN, V_OUT, V_G1, V_S1, V_UP, V_DOWN, V_G2, V_S2, V_ALL = 0, 2, 3, 4, 5, 7, 8, 9, 16


def norm_back(upstream, n, rate, gain):
    e = upstream * gain
    inner = jnp.mean(e * n, axis=1, keepdims=True)
    return (e - jnp.mean(e, axis=1, keepdims=True) - n * inner) * rate


def doubled(v):
    return jnp.concatenate([v, v], axis=1)


def joined(values):
    return jnp.concatenate(values, axis=0) if len(values) > 1 else values[0]


def feed_back(plan, kept, w, upstream, r, before=None):
    total, small, ctx_grad, sum_grad = r.s_total, r.s_small, r.s_ctx_grad, r.s_sum_grad

    def visit(b, rows):
        if before is not None:
            before(b, rows)
        chains = parts_of(rows, 2)
        wout, wup, wdown = w.wout[...], w.wup[...], w.wdown[...]
        up = [upstream[at, :].astype(F32) for at in chains]
        n2 = [kept.n2[at, :].astype(F32) for at in chains]
        r2 = [doubled(kept.r2[at, :]) for at in chains]
        slope = [kept.slope[at, :] for at in chains]
        n1 = [kept.n1[at, :].astype(F32) for at in chains]
        r1 = [doubled(kept.r1[at, :]) for at in chains]
        act, mid, ctx = kept.act[rows, :], kept.mid[rows, :], kept.ctx[rows, :]
        feed_grad = [norm_back(u, n, v, w.g2) for u, n, v in zip(up, n2, r2)]
        feed_low = [v.astype(BF) for v in feed_grad]
        active_grad = [dot_nt(v, wdown) for v in feed_low]
        pre_grad = [(v * p.astype(F32)).astype(BF) for v, p in zip(active_grad, slope)]
        mid_grad = [dot_nt(v, wup) + u for v, u in zip(pre_grad, feed_grad)]
        mid_grad = [v.astype(BF).astype(F32) for v in mid_grad]
        attn_grad = [norm_back(u, n, v, w.g1) for u, n, v in zip(mid_grad, n1, r1)]
        attn_low = [v.astype(BF) for v in attn_grad]
        back = [dot_nt(v, wout).astype(BF) for v in attn_low]
        down_total = dot_tn(act, joined(feed_low))
        up_total = dot_tn(mid, joined(pre_grad))
        out_total = dot_tn(ctx, joined(attn_low))
        up_sums = fold(joined(pre_grad).astype(F32))
        sums = [
            (V_G2, fold(joined([u * n for u, n in zip(up, n2)]))),
            (V_S2, fold(joined(up))),
            (V_DOWN, fold(joined(feed_low).astype(F32))),
            (V_UP, up_sums[:, :256]),
            (V_UP + 1, up_sums[:, 256:]),
            (V_G1, fold(joined([u * n for u, n in zip(mid_grad, n1)]))),
            (V_S1, fold(joined(mid_grad))),
            (V_OUT, fold(joined(attn_low).astype(F32))),
        ]
        for k, at in enumerate(chains):
            sum_grad[at, :] = attn_grad[k]
            ctx_grad[at, :] = back[k]
        total[AT_DOWN:AT_ALL, :] += down_total
        total[AT_UP : AT_UP + 256, :] += up_total[:, :256]
        total[AT_UP + 256 : AT_DOWN, :] += up_total[:, 256:]
        total[AT_OUT:AT_UP, :] += out_total
        for line, v in sums:
            small[line] += v

    plan.over_blocks(visit)
    clear(ctx_grad, rows_at(plan.end, 2 * QB))


def attend_back(plan, most, kept, r):
    weights_low, ctx_grad, qkv_grad, keys_turned = r.s_probs, r.s_ctx_grad, r.s_qkv_grad, r.s_turned
    masks = head_masks()
    scaling = (256 // HEADS) ** (-0.5)
    plan.over_blocks(lambda b, rows: clear(qkv_grad, rows))

    def visit(docs):
        offset = [plan.offset(d) for d, _ in docs]
        tile = [plan.tile(d) for d, _ in docs]
        width = [n * QB for _, n in docs]
        firsts = [sum(width[:i]) for i in range(len(docs))]
        spans = [rows_at(o, v) for o, v in zip(offset, width)]
        for i, first in enumerate(firsts):
            turn(kept.qkv[spans[i], 256:512], keys_turned, first, width[i])
        chains = [(i, q, g) for i, (_, n) in enumerate(docs) for q in range(n) for g in range(2)]
        values = [[kept.qkv[at, shifted(c, 512)] for c in GROUPS] for at in spans]
        turned = [[keys_turned[c, f : f + v] for c in GROUPS] for f, v in zip(firsts, width)]
        queries = [kept.qkv[rows_at(offset[i] + q * QB, QB), GROUPS[g]] for i, q, g in chains]
        grads = [ctx_grad[rows_at(offset[i] + q * QB, QB), GROUPS[g]] for i, q, g in chains]
        probs = []
        for i, q, g in chains:
            n = docs[i][1]
            probs.append(joined([weights_low[tile[i] + q * n + k, g] for k in range(n)]))
        queries = [two_heads(v, masks) for v in queries]
        grads = [two_heads(v, masks) for v in grads]
        prob_grads = [dot_nt(values[i][g], v) for v, (i, _, g) in zip(grads, chains)]
        score_grads = []
        for low, v in zip(probs, prob_grads):
            full = low.astype(F32)
            inner = jnp.sum(full * v, axis=0, keepdims=True)
            score_grads.append((full * (v - inner)).astype(BF))
        query_grads = [dot(turned[i][g], v) for v, (i, _, g) in zip(score_grads, chains)]
        query_grads = [turned_back(v * scaling) for v in query_grads]
        sums = []
        for i in range(len(docs)):
            for g in range(2):
                mine = [k for k, c in enumerate(chains) if (c[0], c[2]) == (i, g)]
                sides = jnp.concatenate([score_grads[k] for k in mine], axis=1)
                key_sum = dot(sides, joined([queries[k] for k in mine])).astype(BF)
                sides = jnp.concatenate([probs[k] for k in mine], axis=1)
                value_sum = dot(sides, joined([grads[k] for k in mine])).astype(BF)
                sums.append((i, g, key_sum, value_sum))
        for i in range(len(docs)):
            for v, (own, q, g) in zip(query_grads, chains):
                if own == i:
                    qkv_grad[rows_at(offset[i] + q * QB, QB), GROUPS[g]] = v
            for own, g, key_sum, value_sum in sums:
                if own == i:
                    qkv_grad[spans[i], shifted(GROUPS[g], 256)] = key_sum
                    qkv_grad[spans[i], shifted(GROUPS[g], 512)] = value_sum

    plan.over_groups(most, visit)


def project_back(plan, kept, w, r, out, after=None):
    qkv_grad, sum_grad, total, small = r.s_qkv_grad, r.s_sum_grad, r.s_total, r.s_small

    def visit(b, rows):
        grad = qkv_grad[rows, :]
        sums = fold(grad.astype(F32))
        small[V_IN] += sums[:, :256]
        small[V_IN + 1] += sums[:, 512:]
        in_grad = dot_tn(kept.x[rows, :], grad)
        for k in range(3):
            total[256 * k : 256 * (k + 1), :] += in_grad[:, 256 * k : 256 * (k + 1)]
        hidden_grad = dot_nt(grad, w.win[...]) + sum_grad[rows, :]
        out[rows, :] = hidden_grad.astype(BF)
        if after is not None:
            after(b, rows)

    plan.over_blocks(visit)


def copies(r, plan, out):
    def one(near, far, sem):
        return pltpu.make_async_copy(*((near, far) if out else (far, near)), sem)

    def of_block(k, b, rows, first=0, columns=None):
        near, far = (getattr(r, side + NAMES[k]) for side in ("s_", "o_" if out else "i_"))
        at = (rows, slice(first, columns or near.shape[1]))
        return [one(near.at[at], far.at[at], r.sems.at[k + (3 if columns else 0), b])]

    def of_doc(d, n):
        at = pl.ds(plan.tile(d), max(n, 2) ** 2)
        return one(r.s_probs.at[at], (r.o_probs if out else r.i_probs).at[at], r.sems.at[4, 0])

    return of_block, of_doc


def by_block(source, target, sems):
    return lambda b, rows: [pltpu.make_async_copy(source.at[rows], target.at[rows], sems.at[b])]


def started(found):
    for c in found:
        c.start()


def waited(found):
    for c in found:
        c.wait()


def first_kernel(most, span, r):
    with_halos(r, r.s_window, span, started)
    w = layer_of(r, 0)
    plan = Plan(r)
    kept = kept_of(r)
    of_block, of_doc = copies(r, plan, True)
    leaving = by_block(r.s_rows, r.o_next, r.out_sems)
    clear_between(r.s_window, span, r.own.shape[0])
    with_halos(r, r.s_window, span, waited)
    pack(plan, most, r.s_window, kept.x)
    waited(w.coming)
    project(plan, kept, w)
    plan.over_blocks(lambda b, rows: started(of_block(0, b, rows)))
    attend(plan, most, kept, r.s_probs, r.s_turned)
    plan.over_docs(most, lambda d, n, length: of_doc(d, n).start())

    def late(b, rows):
        return leaving(b, rows) + of_block(1, b, rows) + of_block(2, b, rows)

    feed(plan, kept, w, r.s_rows, lambda b, rows: started(late(b, rows)))
    plan.over_blocks(lambda b, rows: waited(late(b, rows) + of_block(0, b, rows)))
    plan.over_docs(most, lambda d, n, length: of_doc(d, n).wait())


def second_kernel(most, span, r):
    plan = Plan(r)
    kept = kept_of(r)
    coming = by_block(r.x, kept.x, r.in_sems)
    plan.over_blocks(lambda b, rows: started(coming(b, rows)))
    w = layer_of(r, 1)
    with_halos(r, r.s_window, span, started)
    below = layer_of(r, 0)
    waited(w.coming)
    project(plan, kept, w, lambda b, rows: waited(coming(b, rows)))
    attend(plan, most, kept, r.s_probs, r.s_turned)
    leaving = by_block(r.s_ctx_grad, r.o_out, r.out_sems)
    feed(plan, kept, w, r.s_ctx_grad, lambda b, rows: started(leaving(b, rows)))
    clear_between(r.s_window, span, r.own.shape[0])
    with_halos(r, r.s_window, span, waited)
    pack(plan, most, r.s_window, r.s_rows)
    plan.over_blocks(lambda b, rows: waited(leaving(b, rows)))
    of_block, of_doc = copies(r, plan, False)

    def fed(b, rows):
        return of_block(1, b, rows) + of_block(2, b, rows)

    def projected(b, rows):
        return of_block(0, b, rows, 256)

    def given(b, rows):
        return of_block(0, b, rows, 0, 256)

    waited(below.coming)
    leaving = by_block(r.s_rows, r.o_grad, r.out_sems)

    def one(step, _):
        w = weights_of(r, 1 - step)

        def at(which, act):
            pl.when(step == which)(act)

        def come(found, act):
            plan.over_blocks(lambda b, rows: act(found(b, rows)))

        def before(b, rows):
            at(1, lambda: waited(fed(b, rows)))

        def after(b, rows):
            at(1, lambda: started(leaving(b, rows)))

        clear_totals(r)
        feed_back(plan, kept, w, r.s_rows, r, before)
        at(0, lambda: come(fed, started))

        @pl.when(step == 1)
        def _():
            plan.over_docs(most, lambda d, n, length: of_doc(d, n).wait())
            come(projected, waited)

        attend_back(plan, most, kept, r)

        @pl.when(step == 0)
        def _():
            plan.over_docs(most, lambda d, n, length: of_doc(d, n).start())
            come(projected, started)

        at(1, lambda: come(given, waited))
        project_back(plan, kept, w, r, r.s_rows, after)
        at(0, lambda: come(given, started))
        r.s_both[pl.ds(pl.multiple_of((1 - step) * V_ALL, V_ALL), V_ALL), :] = r.s_small[...].sum(1)
        at(0, lambda: send_pieces(r, r.o_keep1, r.o_send1, r.table[SELF + 1]))
        at(1, lambda: send_pieces(r, r.o_keep0, r.o_send0, r.table[SELF]))
        return 0

    lax.fori_loop(0, 2, one, 0)
    send_small(r, r.o_keep0, r.o_send0, r.table[SELF])
    plan.over_blocks(lambda b, rows: waited(leaving(b, rows)))


def third_kernel(most, span, r):
    plan = Plan(r)
    coming = [by_block(r.out, r.s_rows, r.in_sems), by_block(r.grad, r.s_sent, r.out_sems)]
    for one in coming:
        plan.over_blocks(lambda b, rows: started(one(b, rows)))
    found = []
    for k, (one, rows) in enumerate(zip(coming, (r.s_rows, r.s_sent))):
        plan.over_blocks(lambda b, at: waited(one(b, at)))
        found += unpack(plan, most, rows, r.s_window.at[k], r, span, k)
    waited(found)


VECTORS = dict(bin=512, bout=256, g1=256, s1=256, bup=512, bdown=256, g2=256, s2=256)


def weights_of(r, layer):
    near = dict(win=r.s_win, wout=r.s_wout, wup=r.s_wup, wdown=r.s_wdown)
    near = {k: v.at[layer] for k, v in near.items()}
    vectors = {k: r.s_vectors[layer, i : i + 1, 0:n] for i, (k, n) in enumerate(VECTORS.items())}
    return SimpleNamespace(**near, **vectors)


def layer_of(r, layer):
    pairs = ((r.win, r.s_win), (r.wout, r.s_wout), (r.wup, r.s_wup), (r.wdown, r.s_wdown))
    coming = []
    for k, (far, near) in enumerate(pairs):
        sem = r.weight_sems.at[4 * layer + k]
        coming.append(pltpu.make_async_copy(far.at[layer], near.at[layer], sem))
    started(coming)
    for i, (k, n) in enumerate(VECTORS.items()):
        r.s_vectors[layer, i : i + 1, 0:n] = getattr(r, k)[layer : layer + 1, :]
    w = weights_of(r, layer)
    w.coming = coming
    return w


def clear_totals(r):
    r.s_total[...] = jnp.zeros(r.s_total.shape, F32)
    r.s_small[...] = jnp.zeros(r.s_small.shape, F32)


def send_pieces(r, keep, send, own):
    half = keep.shape[0]
    rows = AT_ALL // (2 * half)
    for p in range(2 * half):
        out = keep if p < half else send
        at = pl.ds(pl.multiple_of(lax.bitwise_xor(jnp.int32(p), own) * rows, rows), rows)
        out[p % half, 0:rows, :] = r.s_total[at, :].astype(BF)


def send_small(r, keep, send, own):
    half = keep.shape[0]
    rows = AT_ALL // (2 * half)
    extra = keep.shape[1] - rows
    share = V_ALL // half
    for j in range(2 * half):
        line = r.s_both[j * share : (j + 1) * share, :]
        r.s_spread[j] = jnp.concatenate([line, jnp.zeros((extra - share, line.shape[1]), F32)], axis=0)
    for p in range(2 * half):
        out = keep if p < half else send
        out[p % half, rows : rows + extra, :] = r.s_spread[lax.bitwise_xor(jnp.int32(p), own)].astype(BF)


def last_kernel(r):
    half = r.keep0.shape[0]
    count = 2 * half
    rows = AT_ALL // count
    share = 2 * V_ALL // count
    big = (
        (0, AT_OUT, r.s_in, r.o_in),
        (AT_OUT, AT_UP, r.s_out, r.o_out),
        (AT_UP, AT_DOWN, r.s_up, r.o_up),
        (AT_DOWN, AT_ALL, r.s_down, r.o_down),
    )
    sent = []
    for layer, (keep, got) in enumerate(((r.keep0, r.got0), (r.keep1, r.got1))):
        for p in range(count):
            piece = lax.bitwise_xor(jnp.int32(p), r.table[SELF + layer])
            source = keep if p < half else got
            r.s_pieces[layer, piece, 0 : keep.shape[1], :] = source[p % half]
        for low, high, near, far in big:
            tall = near.shape[1]
            for at in range(low, high, rows):
                line, col = (at - low) % tall, (at - low) // tall * 256
                value = r.s_pieces[layer, at // rows, 0:rows, :].astype(F32)
                near[layer, line : line + rows, col : col + 256] = value
            copy = pltpu.make_async_copy(near.at[layer], far.at[layer], r.sems.at[len(sent)])
            copy.start()
            sent.append(copy)
    for j in range(count):
        tail = r.s_pieces[0, j, rows : rows + 16, :].astype(F32)
        r.s_both[j * share : (j + 1) * share, :] = tail[0:share]
    for layer in range(2):
        at = layer * V_ALL
        here = pl.ds(layer, 1)

        def line(k):
            return r.s_both[at + k : at + k + 1, :]

        r.o_bin[here, :] = jnp.concatenate([line(V_IN), line(V_IN + 1)], axis=1)
        r.o_bout[here, :] = line(V_OUT)
        r.o_g1[here, :] = line(V_G1)
        r.o_s1[here, :] = line(V_S1)
        r.o_bup[here, :] = jnp.concatenate([line(V_UP), line(V_UP + 1)], axis=1)
        r.o_bdown[here, :] = line(V_DOWN)
        r.o_g2[here, :] = line(V_G2)
        r.o_s2[here, :] = line(V_S2)
    waited(sent)


def call(kernel, consts, inputs, outputs, scratch, flops, megabytes):
    names = tuple(inputs) + tuple(outputs) + tuple(scratch)

    def run(*refs):
        kernel(*consts, SimpleNamespace(**dict(zip(names, refs))))

    got = pl.pallas_call(
        run,
        out_shape=[jax.ShapeDtypeStruct(s, d) for s, d, _ in outputs.values()],
        in_specs=[spec for _, spec in inputs.values()],
        out_specs=[spec for _, _, spec in outputs.values()],
        scratch_shapes=list(scratch.values()),
        compiler_params=pltpu.CompilerParams(vmem_limit_bytes=megabytes << 20),
        cost_estimate=pl.CostEstimate(flops=flops, bytes_accessed=8 << 20, transcendentals=0),
    )(*[a for a, _ in inputs.values()])
    return SimpleNamespace(**dict(zip(outputs, got)))


def plan_kernel(sections, whole, span, ways, r):
    base = DOCS + 1
    huge = jnp.int32(1 << 20)
    for row in range(2):
        line = r.segments[row : row + 1, :]
        starts = [jnp.int32(0)]
        for doc in range(1, DOCS):
            below = jnp.where(line < doc, 1.0, 0.0)
            starts.append(jnp.sum(below).astype(jnp.int32))
        starts.append(jnp.int32(sections * whole))
        spent = jnp.int32(0)
        for doc in range(base):
            r.start[row * base + doc] = starts[doc]
            r.spent[row * base + doc] = spent
            if doc < DOCS:
                size = starts[doc + 1] - starts[doc]
                spent = spent + size + 180
                spent = spent + jnp.where(size > 2 * QB, 160, 0) + jnp.where(size > 3 * QB, 190, 0)
        for section in range(1, sections):
            low, high = jnp.int32(0), jnp.int32(0)
            for doc in range(base):
                away = starts[doc] - section * whole
                low = low + (away < -REACH).astype(jnp.int32)
                high = high + (away <= REACH).astype(jnp.int32)
            r.low[2 * section + row] = low
            r.high[2 * section + row] = high

    def over(section, visit, first):
        def outer(i, carry):
            inner = lambda j, c: visit(i, j, c)
            return lax.fori_loop(r.low[2 * section + 1], r.high[2 * section + 1], inner, carry)

        return lax.fori_loop(r.low[2 * section], r.high[2 * section], outer, first)

    def least(section, end, top, right):
        def visit(i, j, carry):
            cost, code = carry
            at = i * base + j
            step = end - r.spent[i] - r.spent[base + j]
            new = jnp.maximum(r.best[section * base * base + at], step)
            new = jnp.where((i <= top) & (j <= right), new, huge)
            better = new < cost
            return jnp.where(better, new, cost), jnp.where(better, at, code)

        return over(section, visit, (huge, jnp.int32(0)))

    for section in range(1, sections):

        def visit(i, j, carry):
            at = section * base * base + i * base + j
            end = r.spent[i] + r.spent[base + j]
            if section == 1:
                r.best[at] = end
            else:
                r.best[at], r.way[at] = least(section - 1, end, i, j)
            return carry

        over(section, visit, jnp.int32(0))
    _, code = least(sections - 1, r.spent[DOCS] + r.spent[base + DOCS], jnp.int32(DOCS), jnp.int32(DOCS))
    cuts = [jnp.int32(base * base - 1), code]
    for section in range(sections - 1, 1, -1):
        code = r.way[section * base * base + code]
        cuts.append(code)
    cuts = (cuts + [jnp.int32(0)])[::-1]
    place = r.place[0]
    low, high = jnp.int32(0), jnp.int32(0)
    for section in range(sections):
        low = jnp.where(place == section, cuts[section], low)
        high = jnp.where(place == section, cuts[section + 1], high)
    low, high = (low // base, low % base), (high // base, high % base)
    table = r.table
    carry = (jnp.int32(0), jnp.int32(0), jnp.int32(0))
    for kind in range(2, whole // QB + 1):
        for row in range(2):

            def one(doc, carry):
                k, offset, tile = carry
                begin = r.start[row * base + doc]
                length = r.start[row * base + doc + 1] - begin
                blocks = jnp.maximum(lax.shift_right_logical(length + (QB - 1), 7), 2)
                table[k] = begin - place * whole + REACH + row * span
                table[ROOM + k] = length
                table[2 * ROOM + k] = offset
                table[3 * ROOM + k] = tile
                taken = (blocks == kind).astype(jnp.int32)
                offset = offset + taken * lax.bitwise_and(length + 15, -16)
                return k + taken, offset, tile + taken * blocks * blocks

            carry = lax.fori_loop(low[row], high[row], one, carry)
    k, offset, _ = carry
    table[ROOM + k] = 0
    blocks = offset // TB
    rest = offset - blocks * TB
    blocks = blocks + (rest > TAIL).astype(jnp.int32)
    odd = ((rest > 0) & (rest <= TAIL)).astype(jnp.int32)
    table[4 * ROOM] = k
    table[4 * ROOM + 1] = blocks
    table[4 * ROOM + 2] = odd
    table[4 * ROOM + 3] = blocks * TB + odd * TAIL
    for i, order in enumerate(ways):
        own = jnp.int32(0)
        for axis, stride in order[:SPLIT]:
            index = r.place[0] if axis == "pipe" else r.group[0]
            own = 2 * own + lax.bitwise_and(index // stride, 1)
        table[4 * ROOM + 4 + i] = own


def halo_sent(low_part, high_part, place):
    upper = lax.rem(place, 2) == 1
    return jnp.where(upper, low_part, high_part), jnp.where(upper, high_part, low_part)


def halo(sent):
    count = lax.axis_size("pipe")
    got = []
    for odd, value in enumerate(sent):
        pairs = [(i, i + 1) for i in range(odd, count - 1, 2)]
        got.append(lax.ppermute(value, "pipe", [p for i, j in pairs for p in ((i, j), (j, i))]))
    return got


def orders():
    found = []
    for axis in ("dp", "pipe"):
        stride = 1
        while stride < lax.axis_size(axis):
            found.append((axis, stride))
            stride *= 2
    other = list(found)
    if len(found) > 2:
        other[1], other[2] = found[2], found[1]
    return found, other


SPLIT = 4


def exchange(value, axis, stride):
    count = lax.axis_size(axis)
    return lax.ppermute(value, axis, [(i, i ^ stride) for i in range(count)])


def added(a, b):
    return (a.astype(F32) + b.astype(F32)).astype(BF)


def sum_steps(keep, send, order):
    total = None
    for k, (axis, stride) in enumerate(order[:SPLIT]):
        got = exchange(send, axis, stride)
        yield None
        half = keep.shape[0] // 2
        if half:
            send, keep = added(keep[half:], got[half:]), added(keep[:half], got[:half])
        else:
            total = added(keep, got)
    for axis, stride in order[SPLIT:]:
        got = exchange(total, axis, stride)
        yield None
        total = added(total, got)
    for k, (axis, stride) in enumerate(reversed(order[:SPLIT])):
        got = exchange(total, axis, stride)
        yield (total, got)
        total = jnp.concatenate([total, got], axis=0)


def body(
    tokens,
    segments,
    cotangent,
    attention_in,
    attention_in_bias,
    attention_out,
    attention_out_bias,
    attention_gain,
    attention_shift,
    expand_weight,
    expand_bias,
    contract_weight,
    contract_bias,
    feed_gain,
    feed_shift,
):
    section_count = lax.axis_size("pipe")
    place = lax.axis_index("pipe").astype(jnp.int32)
    row_count, whole, features = tokens.shape
    span = whole + 2 * REACH + 2 * QB
    most = whole // QB
    cap = row_count * (whole + 2 * REACH) + ITEMS * 15
    cap = (cap + TB - 1) // TB * TB + 2 * QB
    tiles = row_count * 53
    vmem = pl.BlockSpec(memory_space=pltpu.VMEM)
    smem = pl.BlockSpec(memory_space=pltpu.SMEM)
    hbm = pl.BlockSpec(memory_space=pltpu.HBM)
    anywhere = pl.BlockSpec(memory_space=pl.ANY)
    weights = dict(
        win=attention_in,
        bin=attention_in_bias,
        wout=attention_out,
        bout=attention_out_bias,
        g1=attention_gain,
        s1=attention_shift,
        wup=expand_weight,
        bup=expand_bias,
        wdown=contract_weight,
        bdown=contract_bias,
        g2=feed_gain,
        s2=feed_shift,
    )
    weights = {k: (v, vmem if v.ndim == 2 else hbm) for k, v in weights.items()}
    weight_scratch = dict(
        s_win=pltpu.VMEM(attention_in.shape, BF),
        s_wout=pltpu.VMEM(attention_out.shape, BF),
        s_wup=pltpu.VMEM(expand_weight.shape, BF),
        s_wdown=pltpu.VMEM(contract_weight.shape, BF),
        s_vectors=pltpu.VMEM((attention_in.shape[0], len(VECTORS), 2 * features), F32),
        weight_sems=pltpu.SemaphoreType.DMA((4 * attention_in.shape[0],)),
    )

    ways = orders()
    pieces = 1 << SPLIT
    even, odd = halo(halo_sent(tokens[:, :REACH], tokens[:, whole - REACH :], place))
    token_rows = dict(own=(tokens, anywhere), even=(even, anywhere), odd=(odd, anywhere))
    choices = section_count * (DOCS + 1) ** 2
    planned = call(
        plan_kernel,
        (section_count, whole, span, ways),
        dict(
            segments=(segments, vmem),
            place=(place.reshape(1), smem),
            group=(lax.axis_index("dp").astype(jnp.int32).reshape(1), smem),
        ),
        dict(table=((4 * ROOM + 6,), jnp.int32, smem)),
        dict(
            start=pltpu.SMEM((2 * (DOCS + 1),), jnp.int32),
            spent=pltpu.SMEM((2 * (DOCS + 1),), jnp.int32),
            low=pltpu.SMEM((2 * section_count,), jnp.int32),
            high=pltpu.SMEM((2 * section_count,), jnp.int32),
            best=pltpu.SMEM((choices,), jnp.int32),
            way=pltpu.SMEM((choices,), jnp.int32),
        ),
        1 << 20,
        4,
    )
    plan = dict(table=(planned.table, smem), place=(place.reshape(1), smem))
    sent = halo_sent(cotangent[:, :REACH], cotangent[:, whole - REACH :], place)
    even, odd = halo(lax.optimization_barrier((*sent, planned.table))[:2])
    cotangent_rows = dict(own=(cotangent, anywhere), even=(even, anywhere), odd=(odd, anywhere))
    kept_scratch = {"s_" + k: pltpu.VMEM((cap, sum(c.values())), t) for k, (t, c) in KEPT.items()}
    kept_scratch.update(weight_scratch)
    probs_shape = (tiles, 2, QB, 2 * QB)
    kept_scratch.update(
        s_probs=pltpu.VMEM(probs_shape, BF),
        s_window=pltpu.VMEM((row_count * span, features), BF),
        s_turned=pltpu.VMEM((features, whole), BF),
    )
    sems = dict(sems=pltpu.SemaphoreType.DMA((5, MOST_BLOCKS)))
    moved = dict(
        s_rows=pltpu.VMEM((cap, features), BF),
        window_sems=pltpu.SemaphoreType.DMA((3 * row_count,)),
        in_sems=pltpu.SemaphoreType.DMA((MOST_BLOCKS,)),
        out_sems=pltpu.SemaphoreType.DMA((MOST_BLOCKS,)),
    )
    back_scratch = dict(
        s_total=pltpu.VMEM((AT_ALL, features), F32),
        s_small=pltpu.VMEM((V_ALL, 8, features), F32),
        s_ctx_grad=pltpu.VMEM((cap, features), BF),
        s_sum_grad=pltpu.VMEM((cap, features), F32),
        s_qkv_grad=pltpu.VMEM((cap, 3 * features), BF),
    )
    def pieces_out(extra):
        return ((pieces // 2, AT_ALL // pieces + extra, features), BF, vmem)

    rows_out = ((cap, features), BF, hbm)
    kept_out = {"o_" + k: ((cap, sum(c.values())), t, hbm) for k, (t, c) in KEPT.items()}
    kept_out.update(o_probs=(probs_shape, BF, hbm), o_next=rows_out)
    shape = (most, span)

    first = call(
        first_kernel,
        shape,
        plan | token_rows | weights,
        kept_out,
        kept_scratch | sems | moved,
        12 << 30,
        63,
    )
    kept_in = {"i_" + k: (getattr(first, "o_" + k), hbm) for k in NAMES + ("probs",)}
    second = call(
        second_kernel,
        shape,
        plan
        | cotangent_rows
        | kept_in
        | dict(x=(first.o_next, hbm))
        | weights,
        dict(
            o_keep0=pieces_out(16),
            o_send0=pieces_out(16),
            o_keep1=pieces_out(0),
            o_send1=pieces_out(0),
            o_out=rows_out,
            o_grad=rows_out,
        ),
        kept_scratch
        | back_scratch
        | sems
        | moved
        | dict(
            s_both=pltpu.VMEM((2 * V_ALL, features), F32),
            s_spread=pltpu.VMEM((pieces, 16, features), F32),
        ),
        60 << 30,
        63,
    )
    sums = [sum_steps(second.o_keep0, second.o_send0, ways[0])]
    sums.append(sum_steps(second.o_keep1, second.o_send1, ways[1]))
    third = call(
        third_kernel,
        shape,
        plan | dict(out=(second.o_out, hbm), grad=(second.o_grad, hbm)),
        dict(
            o_own=((2, row_count, whole, features), BF, anywhere),
            o_left=((2, row_count, REACH, features), BF, anywhere),
            o_right=((2, row_count, REACH, features), BF, anywhere),
        ),
        moved
        | dict(
            s_sent=pltpu.VMEM((cap, features), BF),
            s_window=pltpu.VMEM((2, row_count * span, features), BF),
                window_sems=pltpu.SemaphoreType.DMA((2, 3 * row_count)),
        ),
        2 << 30,
        20,
    )
    even, odd = halo(halo_sent(third.o_left, third.o_right, place))
    upper = lax.rem(place, 2) == 1
    gap = jnp.zeros((2, row_count, whole - REACH, features), BF)
    low = jnp.concatenate([jnp.where(upper, even, odd), gap], axis=2)
    high = jnp.concatenate([gap, jnp.where(upper, odd, even)], axis=2)
    layer_output, input_grad = [third.o_own[k] + low[k] + high[k] for k in range(2)]
    for ends in zip(*sums):
        pass
    layers = attention_in.shape[0]

    def out(*shape):
        return ((layers,) + shape, F32, hbm)

    def small_out(*shape):
        return ((layers,) + shape, F32, vmem)

    vector = small_out(features)
    result = call(
        last_kernel,
        (),
        dict(
            table=(planned.table, smem),
            keep0=(ends[0][0], vmem),
            got0=(ends[0][1], vmem),
            keep1=(ends[1][0], vmem),
            got1=(ends[1][1], vmem),
        ),
        dict(
            o_in=out(features, 3 * features),
            o_bin=small_out(2 * features),
            o_out=out(features, features),
            o_bout=vector,
            o_g1=vector,
            o_s1=vector,
            o_up=out(features, 2 * features),
            o_bup=small_out(2 * features),
            o_down=out(2 * features, features),
            o_bdown=vector,
            o_g2=vector,
            o_s2=vector,
        ),
        dict(
            s_pieces=pltpu.VMEM((2, pieces, AT_ALL // pieces + 16, features), BF),
            s_both=pltpu.VMEM((2 * V_ALL, features), F32),
            s_in=pltpu.VMEM((layers, features, 3 * features), F32),
            s_out=pltpu.VMEM((layers, features, features), F32),
            s_up=pltpu.VMEM((layers, features, 2 * features), F32),
            s_down=pltpu.VMEM((layers, 2 * features, features), F32),
            sems=pltpu.SemaphoreType.DMA((4 * layers,)),
        ),
        1 << 30,
        20,
    )
    return (layer_output, input_grad) + tuple(vars(result).values())


def solution(mesh):
    rows = P("dp", "pipe", None)
    return jax.shard_map(
        body,
        mesh=mesh,
        in_specs=(rows, P("dp", None), rows) + (P(),) * 12,
        out_specs=(rows, rows) + (P(),) * 12,
        check_vma=False,
    )
```

```python
from types import SimpleNamespace

import jax
import jax.numpy as jnp
from jax import lax
from jax.experimental import pallas as pl
from jax.experimental.pallas import tpu as pltpu
from jax.sharding import PartitionSpec as P

HEADS = 4
EPSILON = 1e-12
MASKED = -1e30
DOCS = 8
REACH = 320
TB = 640
TAIL = 256
MOST_BLOCKS = 8
QB = 128
LANES = 128

BF = jnp.bfloat16
F32 = jnp.float32

KEPT = dict(
    ahead=(BF, dict(x=256, qkv=768)),
    fed=(BF, dict(ctx=256, n1=256, mid=256, act=512, slope=512, n2=256)),
    rates=(F32, dict(r1=128, r2=128)),
)
NAMES = tuple(KEPT)


def kept_of(r):
    found = {}
    for name, (_, parts) in KEPT.items():
        first = 0
        for part, columns in parts.items():
            found[part] = getattr(r, "s_" + name).at[:, first : first + columns]
            first += columns
    return SimpleNamespace(**found)


def dot(a, b):
    return jnp.dot(a, b, preferred_element_type=F32)


def dot_nt(a, b):
    return lax.dot_general(a, b, (((1,), (1,)), ((), ())), preferred_element_type=F32)


def dot_tn(a, b):
    return lax.dot_general(a, b, (((0,), (0,)), ((), ())), preferred_element_type=F32)


def fold(v):
    return v.reshape(-1, 8, v.shape[-1]).sum(0)


def rows_at(start, count):
    return pl.ds(pl.multiple_of(start, 16), count)


ITEMS = 2 * DOCS
ROOM = ITEMS + 1
SELF = 4 * ROOM + 4


class Plan:
    def __init__(self, r):
        self.table = r.table
        self.count, self.blocks, self.odd, self.end = (r.table[4 * ROOM + k] for k in range(4))

    def start(self, d):
        return self.table[d]

    def length(self, d):
        return self.table[ROOM + d]

    def offset(self, d):
        return self.table[2 * ROOM + d]

    def tile(self, d):
        return self.table[3 * ROOM + d]

    def size(self, d):
        return lax.shift_right_logical(self.length(d) + (QB - 1), 7)

    def over_docs(self, most, visit):
        def one(d, _):
            size = self.size(d)
            for n in range(1, most + 1):

                @pl.when(size == n)
                def _():
                    visit(d, n, self.length(d))

            return 0

        lax.fori_loop(0, self.count, one, 0)

    def over_groups(self, most, visit):
        def one(d):
            size, after = self.size(d), self.size(d + 1)
            two = (size <= 2) & (after >= 1) & (after <= 2)

            @pl.when(two & (size == 1))
            def _():
                visit([(d, 1), (d + 1, 2)])

            @pl.when(two & (size == 2))
            def _():
                visit([(d, 2), (d + 1, 2)])

            for n in range(2, most + 1):

                @pl.when((jnp.maximum(size, 2) == n) & jnp.logical_not(two))
                def _():
                    visit([(d, n)])

            return d + 1 + two.astype(jnp.int32)

        lax.while_loop(lambda d: d < self.count, one, jnp.int32(0))

    def over_blocks(self, visit):
        def one(b, _):
            visit(b, rows_at(b * TB, TB))
            return 0

        lax.fori_loop(0, self.blocks, one, 0)

        @pl.when(self.odd == 1)
        def _():
            visit(self.blocks, rows_at(self.blocks * TB, TAIL))


def window_copies(win, span, own, low, high, sems, out):
    reach, whole = low.shape[1], own.shape[1]
    found = []
    for k in range(own.shape[0]):
        at = k * span
        for far, count in ((low, reach), (own, whole), (high, reach)):
            ends = (win.at[pl.ds(at, count)], far.at[k])
            found.append(pltpu.make_async_copy(*(ends if out else ends[::-1]), sems.at[len(found)]))
            at += count
    return found


def with_halos(r, win, span, act):
    upper = lax.bitwise_and(r.place[0], 1)
    for side in range(2):

        @pl.when(upper == 1 - side)
        def _():
            low, high = (r.odd, r.even) if side else (r.even, r.odd)
            act(window_copies(win, span, r.own, low, high, r.window_sems, False))


def clear_between(win, span, count):
    used = span - 2 * QB
    for k in range(count):
        clear(win, pl.ds(k * span + used, 2 * QB))


SPREAD = QB + 16


def pack(plan, most, win, dst):
    plan.over_blocks(lambda b, rows: clear(dst, rows))

    def visit(docs):
        row = lax.broadcasted_iota(jnp.int32, (QB, SPREAD), 0)
        col = lax.broadcasted_iota(jnp.int32, (QB, SPREAD), 1)
        parts = []
        for d, n in docs:
            start, length = plan.start(d), plan.length(d)
            shift = lax.bitwise_and(start, 15)
            whole = col == row + shift
            for q in range(n):
                inside = row < length - q * QB
                taken = jnp.where(whole & inside if q == n - 1 or n == 2 else whole, 1.0, 0.0)
                rows = win[rows_at(start - shift + q * QB, SPREAD), :]
                parts.append((taken.astype(BF), rows, plan.offset(d) + q * QB))
        picked = [dot(taken, rows).astype(BF) for taken, rows, _ in parts]
        for v, (_, _, at) in zip(picked, parts):
            dst[rows_at(at, QB), :] = v

    plan.over_groups(most, visit)


def unpack(plan, most, src, win, r, span, which):
    win[...] = jnp.zeros(win.shape, BF)
    clear(src, rows_at(plan.end, QB))

    def visit(d, n, length):
        start, offset = plan.start(d), plan.offset(d)
        shift = lax.bitwise_and(start, 15)
        row = lax.broadcasted_iota(jnp.int32, (SPREAD, QB), 0)
        col = lax.broadcasted_iota(jnp.int32, (SPREAD, QB), 1)
        taken = row == col + shift
        kept = jnp.where(taken & (col < length - (n - 1) * QB), 1.0, 0.0).astype(BF)
        taken = jnp.where(taken, 1.0, 0.0).astype(BF)
        rows = [src[rows_at(offset + q * QB, QB), :] for q in range(n)]
        placed = [dot(taken if q < n - 1 else kept, v) for q, v in enumerate(rows)]
        for q, v in enumerate(placed):
            at = rows_at(start - shift + q * QB, SPREAD)
            win[at, :] = (win[at, :].astype(F32) + v).astype(BF)

    plan.over_docs(most, visit)
    ends = [v.at[which] for v in (r.o_own, r.o_left, r.o_right)]
    found = window_copies(win, span, *ends, r.window_sems.at[which], True)
    started(found)
    return found


def clear(ref, rows):
    ref[rows, :] = jnp.zeros((rows.size, ref.shape[1]), ref.dtype)


def head_masks():
    lane = lax.broadcasted_iota(jnp.int32, (1, LANES), 1)
    low = (lane < LANES // 2).astype(F32)
    return low.astype(BF), (1.0 - low).astype(BF)


def two_heads(v, masks):
    return jnp.concatenate([v * masks[0], v * masks[1]], axis=0)


def turned_back(v):
    row = lax.broadcasted_iota(jnp.int32, (LANES, QB), 0)
    return jnp.where(row < LANES // 2, v[:, :QB], v[:, QB:]).astype(BF).T


def turn(src, dst, first, width):
    for k in range(width // LANES):
        at = slice(k * LANES, (k + 1) * LANES)
        for g in range(2):
            here = slice(g * LANES, (g + 1) * LANES)
            dst[here, first + at.start : first + at.stop] = src[at, here].T


def project(plan, kept, w, before=None):
    scaling = (256 // HEADS) ** (-0.5)
    bias = w.bin

    def visit(b, rows):
        if before is not None:
            before(b, rows)
        y = dot(kept.x[rows, :], w.win[...])
        queries = (y[:, 0:256] + bias[:, 0:256]).astype(BF)
        kept.qkv[rows, 0:256] = queries * jnp.asarray(scaling, BF)
        kept.qkv[rows, 256:512] = y[:, 256:512].astype(BF)
        kept.qkv[rows, 512:768] = (y[:, 512:768] + bias[:, 256:512]).astype(BF)
        clear(kept.ctx, rows)

    plan.over_blocks(visit)
    clear(kept.qkv, rows_at(plan.end, 2 * QB))


GROUPS = tuple(slice(g * LANES, (g + 1) * LANES) for g in range(2))


def shifted(cols, by):
    return slice(cols.start + by, cols.stop + by)


def attend(plan, most, kept, weights_low, values_turned):
    masks = head_masks()

    def visit(docs):
        offset = [plan.offset(d) for d, _ in docs]
        length = [plan.length(d) for d, _ in docs]
        tile = [plan.tile(d) for d, _ in docs]
        width = [n * QB for _, n in docs]
        firsts = [sum(width[:i]) for i in range(len(docs))]
        spans = [rows_at(o, v) for o, v in zip(offset, width)]
        for i, first in enumerate(firsts):
            turn(kept.qkv[spans[i], 512:768], values_turned, first, width[i])
        chains = [(i, q, g) for i, (_, n) in enumerate(docs) for q in range(n) for g in range(2)]
        column = lax.broadcasted_iota(jnp.int32, (1, 2 * QB), 1)
        column = lax.bitwise_and(column, QB - 1)
        row = lax.broadcasted_iota(jnp.int32, (QB, 2 * QB), 0)
        keys = [[kept.qkv[at, shifted(c, 256)] for c in GROUPS] for at in spans]
        turned = [[values_turned[c, f : f + v] for c in GROUPS] for f, v in zip(firsts, width)]
        queries = [kept.qkv[rows_at(offset[i] + q * QB, QB), GROUPS[g]] for i, q, g in chains]
        queries = [two_heads(v, masks) for v in queries]
        scores = [dot_nt(keys[i][g], v) for v, (i, _, g) in zip(queries, chains)]
        probs = []
        for v, (i, q, g) in zip(scores, chains):
            parts = []
            for k in range(docs[i][1]):
                part = v[k * QB : (k + 1) * QB, :]
                if k == docs[i][1] - 1 or docs[i][1] == 2:
                    part = jnp.where(row < length[i] - k * QB, part, MASKED)
                parts.append(part)
            v = jnp.concatenate(parts, axis=0)
            raised = jnp.exp(v - jnp.max(v, axis=0, keepdims=True))
            total = jnp.sum(raised, axis=0, keepdims=True)
            share = jnp.where(column < length[i] - q * QB, 1.0 / total, 0.0)
            probs.append((raised * share).astype(BF))
        contexts = [dot(turned[i][g], v) for v, (i, _, g) in zip(probs, chains)]
        contexts = [turned_back(v) for v in contexts]
        for v, context, (i, q, g) in zip(probs, contexts, chains):
            kept.ctx[rows_at(offset[i] + q * QB, QB), GROUPS[g]] = context
            n = docs[i][1]
            for k in range(n):
                weights_low[tile[i] + q * n + k, g] = v[k * QB : (k + 1) * QB, :]

    plan.over_groups(most, visit)


def normal(v):
    centred = v - jnp.mean(v, axis=1, keepdims=True)
    spread = jnp.mean(centred * centred, axis=1, keepdims=True)
    rate = lax.rsqrt(spread + EPSILON)
    return centred * rate, rate


def parts_of(rows, count):
    step = rows.size // count
    return [rows_at(rows.start + k * step, step) for k in range(count)]


def feed(plan, kept, w, out, each=None):
    def visit(b, rows):
        chains = parts_of(rows, 1)
        wout, wup, wdown = w.wout[...], w.wup[...], w.wdown[...]
        x = [kept.x[at, :] for at in chains]
        ctx = [kept.ctx[at, :] for at in chains]
        attn_sum = [u.astype(F32) + dot(v, wout) + w.bout for u, v in zip(x, ctx)]
        first = [normal(v) for v in attn_sum]
        mid_low = [(n * w.g1 + w.s1).astype(BF) for n, _ in first]
        pre_up = [dot(v, wup) + w.bup for v in mid_low]
        share = [0.5 + 0.5 * lax.erf(v * (0.5**0.5)) for v in pre_up]
        active = [(v * p).astype(BF) for v, p in zip(pre_up, share)]
        density = [jnp.exp(v * v * -0.5) * 0.3989422804014327 for v in pre_up]
        slope = [(p + v * q).astype(BF) for v, p, q in zip(pre_up, share, density)]
        feed_sum = [u.astype(F32) + dot(v, wdown) + w.bdown for u, v in zip(mid_low, active)]
        second = [normal(v) for v in feed_sum]
        for k, at in enumerate(chains):
            kept.n1[at, :] = first[k][0].astype(BF)
            kept.r1[at, :] = jnp.broadcast_to(first[k][1], (at.size, LANES))
            kept.mid[at, :] = mid_low[k]
            kept.act[at, :] = active[k]
            kept.slope[at, :] = slope[k]
            kept.n2[at, :] = second[k][0].astype(BF)
            kept.r2[at, :] = jnp.broadcast_to(second[k][1], (at.size, LANES))
            out[at, :] = (second[k][0] * w.g2 + w.s2).astype(BF)
        if each is not None:
            each(b, rows)

    plan.over_blocks(visit)


AT_OUT, AT_UP, AT_DOWN, AT_ALL = 768, 1024, 1536, 2048
V_IN, V_OUT, V_G1, V_S1, V_UP, V_DOWN, V_G2, V_S2, V_ALL = 0, 2, 3, 4, 5, 7, 8, 9, 16


def norm_back(upstream, n, rate, gain):
    e = upstream * gain
    inner = jnp.mean(e * n, axis=1, keepdims=True)
    return (e - jnp.mean(e, axis=1, keepdims=True) - n * inner) * rate


def doubled(v):
    return jnp.concatenate([v, v], axis=1)


def joined(values):
    return jnp.concatenate(values, axis=0) if len(values) > 1 else values[0]


def feed_back(plan, kept, w, upstream, r, before=None):
    total, small, ctx_grad, sum_grad = r.s_total, r.s_small, r.s_ctx_grad, r.s_sum_grad

    def visit(b, rows):
        if before is not None:
            before(b, rows)
        chains = parts_of(rows, 2)
        wout, wup, wdown = w.wout[...], w.wup[...], w.wdown[...]
        up = [upstream[at, :].astype(F32) for at in chains]
        n2 = [kept.n2[at, :].astype(F32) for at in chains]
        r2 = [doubled(kept.r2[at, :]) for at in chains]
        slope = [kept.slope[at, :] for at in chains]
        n1 = [kept.n1[at, :].astype(F32) for at in chains]
        r1 = [doubled(kept.r1[at, :]) for at in chains]
        act, mid, ctx = kept.act[rows, :], kept.mid[rows, :], kept.ctx[rows, :]
        feed_grad = [norm_back(u, n, v, w.g2) for u, n, v in zip(up, n2, r2)]
        feed_low = [v.astype(BF) for v in feed_grad]
        active_grad = [dot_nt(v, wdown) for v in feed_low]
        pre_grad = [(v * p.astype(F32)).astype(BF) for v, p in zip(active_grad, slope)]
        mid_grad = [dot_nt(v, wup) + u for v, u in zip(pre_grad, feed_grad)]
        mid_grad = [v.astype(BF).astype(F32) for v in mid_grad]
        attn_grad = [norm_back(u, n, v, w.g1) for u, n, v in zip(mid_grad, n1, r1)]
        attn_low = [v.astype(BF) for v in attn_grad]
        back = [dot_nt(v, wout).astype(BF) for v in attn_low]
        down_total = dot_tn(act, joined(feed_low))
        up_total = dot_tn(mid, joined(pre_grad))
        out_total = dot_tn(ctx, joined(attn_low))
        up_sums = fold(joined(pre_grad).astype(F32))
        sums = [
            (V_G2, fold(joined([u * n for u, n in zip(up, n2)]))),
            (V_S2, fold(joined(up))),
            (V_DOWN, fold(joined(feed_low).astype(F32))),
            (V_UP, up_sums[:, :256]),
            (V_UP + 1, up_sums[:, 256:]),
            (V_G1, fold(joined([u * n for u, n in zip(mid_grad, n1)]))),
            (V_S1, fold(joined(mid_grad))),
            (V_OUT, fold(joined(attn_low).astype(F32))),
        ]
        for k, at in enumerate(chains):
            sum_grad[at, :] = attn_grad[k]
            ctx_grad[at, :] = back[k]
        total[AT_DOWN:AT_ALL, :] += down_total
        total[AT_UP : AT_UP + 256, :] += up_total[:, :256]
        total[AT_UP + 256 : AT_DOWN, :] += up_total[:, 256:]
        total[AT_OUT:AT_UP, :] += out_total
        for line, v in sums:
            small[line] += v

    plan.over_blocks(visit)
    clear(ctx_grad, rows_at(plan.end, 2 * QB))


def attend_back(plan, most, kept, r):
    weights_low, ctx_grad, qkv_grad, keys_turned = r.s_probs, r.s_ctx_grad, r.s_qkv_grad, r.s_turned
    masks = head_masks()
    scaling = (256 // HEADS) ** (-0.5)
    plan.over_blocks(lambda b, rows: clear(qkv_grad, rows))

    def visit(docs):
        offset = [plan.offset(d) for d, _ in docs]
        tile = [plan.tile(d) for d, _ in docs]
        width = [n * QB for _, n in docs]
        firsts = [sum(width[:i]) for i in range(len(docs))]
        spans = [rows_at(o, v) for o, v in zip(offset, width)]
        for i, first in enumerate(firsts):
            turn(kept.qkv[spans[i], 256:512], keys_turned, first, width[i])
        chains = [(i, q, g) for i, (_, n) in enumerate(docs) for q in range(n) for g in range(2)]
        values = [[kept.qkv[at, shifted(c, 512)] for c in GROUPS] for at in spans]
        turned = [[keys_turned[c, f : f + v] for c in GROUPS] for f, v in zip(firsts, width)]
        queries = [kept.qkv[rows_at(offset[i] + q * QB, QB), GROUPS[g]] for i, q, g in chains]
        grads = [ctx_grad[rows_at(offset[i] + q * QB, QB), GROUPS[g]] for i, q, g in chains]
        probs = []
        for i, q, g in chains:
            n = docs[i][1]
            probs.append(joined([weights_low[tile[i] + q * n + k, g] for k in range(n)]))
        queries = [two_heads(v, masks) for v in queries]
        grads = [two_heads(v, masks) for v in grads]
        prob_grads = [dot_nt(values[i][g], v) for v, (i, _, g) in zip(grads, chains)]
        score_grads = []
        for low, v in zip(probs, prob_grads):
            full = low.astype(F32)
            inner = jnp.sum(full * v, axis=0, keepdims=True)
            score_grads.append((full * (v - inner)).astype(BF))
        query_grads = [dot(turned[i][g], v) for v, (i, _, g) in zip(score_grads, chains)]
        query_grads = [turned_back(v * scaling) for v in query_grads]
        sums = []
        for i in range(len(docs)):
            for g in range(2):
                mine = [k for k, c in enumerate(chains) if (c[0], c[2]) == (i, g)]
                sides = jnp.concatenate([score_grads[k] for k in mine], axis=1)
                key_sum = dot(sides, joined([queries[k] for k in mine])).astype(BF)
                sides = jnp.concatenate([probs[k] for k in mine], axis=1)
                value_sum = dot(sides, joined([grads[k] for k in mine])).astype(BF)
                sums.append((i, g, key_sum, value_sum))
        for i in range(len(docs)):
            for v, (own, q, g) in zip(query_grads, chains):
                if own == i:
                    qkv_grad[rows_at(offset[i] + q * QB, QB), GROUPS[g]] = v
            for own, g, key_sum, value_sum in sums:
                if own == i:
                    qkv_grad[spans[i], shifted(GROUPS[g], 256)] = key_sum
                    qkv_grad[spans[i], shifted(GROUPS[g], 512)] = value_sum

    plan.over_groups(most, visit)


def project_back(plan, kept, w, r, out, after=None):
    qkv_grad, sum_grad, total, small = r.s_qkv_grad, r.s_sum_grad, r.s_total, r.s_small

    def visit(b, rows):
        grad = qkv_grad[rows, :]
        sums = fold(grad.astype(F32))
        small[V_IN] += sums[:, :256]
        small[V_IN + 1] += sums[:, 512:]
        in_grad = dot_tn(kept.x[rows, :], grad)
        for k in range(3):
            total[256 * k : 256 * (k + 1), :] += in_grad[:, 256 * k : 256 * (k + 1)]
        hidden_grad = dot_nt(grad, w.win[...]) + sum_grad[rows, :]
        out[rows, :] = hidden_grad.astype(BF)
        if after is not None:
            after(b, rows)

    plan.over_blocks(visit)


def copies(r, plan, out):
    def one(near, far, sem):
        return pltpu.make_async_copy(*((near, far) if out else (far, near)), sem)

    def of_block(k, b, rows, first=0, columns=None):
        near, far = (getattr(r, side + NAMES[k]) for side in ("s_", "o_" if out else "i_"))
        at = (rows, slice(first, columns or near.shape[1]))
        return [one(near.at[at], far.at[at], r.sems.at[k + (3 if columns else 0), b])]

    def of_doc(d, n):
        at = pl.ds(plan.tile(d), max(n, 2) ** 2)
        return one(r.s_probs.at[at], (r.o_probs if out else r.i_probs).at[at], r.sems.at[4, 0])

    return of_block, of_doc


def by_block(source, target, sems):
    return lambda b, rows: [pltpu.make_async_copy(source.at[rows], target.at[rows], sems.at[b])]


def started(found):
    for c in found:
        c.start()


def waited(found):
    for c in found:
        c.wait()


def first_kernel(most, span, r):
    with_halos(r, r.s_window, span, started)
    w = layer_of(r, 0)
    plan = Plan(r)
    kept = kept_of(r)
    of_block, of_doc = copies(r, plan, True)
    leaving = by_block(r.s_rows, r.o_next, r.out_sems)
    clear_between(r.s_window, span, r.own.shape[0])
    with_halos(r, r.s_window, span, waited)
    pack(plan, most, r.s_window, kept.x)
    waited(w.coming)
    project(plan, kept, w)
    plan.over_blocks(lambda b, rows: started(of_block(0, b, rows)))
    attend(plan, most, kept, r.s_probs, r.s_turned)
    plan.over_docs(most, lambda d, n, length: of_doc(d, n).start())

    def late(b, rows):
        return leaving(b, rows) + of_block(1, b, rows) + of_block(2, b, rows)

    feed(plan, kept, w, r.s_rows, lambda b, rows: started(late(b, rows)))
    plan.over_blocks(lambda b, rows: waited(late(b, rows) + of_block(0, b, rows)))
    plan.over_docs(most, lambda d, n, length: of_doc(d, n).wait())


def second_kernel(most, span, r):
    plan = Plan(r)
    kept = kept_of(r)
    coming = by_block(r.x, kept.x, r.in_sems)
    plan.over_blocks(lambda b, rows: started(coming(b, rows)))
    w = layer_of(r, 1)
    with_halos(r, r.s_window, span, started)
    below = layer_of(r, 0)
    waited(w.coming)
    project(plan, kept, w, lambda b, rows: waited(coming(b, rows)))
    attend(plan, most, kept, r.s_probs, r.s_turned)
    leaving = by_block(r.s_ctx_grad, r.o_out, r.out_sems)
    feed(plan, kept, w, r.s_ctx_grad, lambda b, rows: started(leaving(b, rows)))
    clear_between(r.s_window, span, r.own.shape[0])
    with_halos(r, r.s_window, span, waited)
    pack(plan, most, r.s_window, r.s_rows)
    plan.over_blocks(lambda b, rows: waited(leaving(b, rows)))
    of_block, of_doc = copies(r, plan, False)

    def fed(b, rows):
        return of_block(1, b, rows) + of_block(2, b, rows)

    def projected(b, rows):
        return of_block(0, b, rows, 256)

    def given(b, rows):
        return of_block(0, b, rows, 0, 256)

    waited(below.coming)
    leaving = by_block(r.s_rows, r.o_grad, r.out_sems)

    def one(step, _):
        w = weights_of(r, 1 - step)

        def at(which, act):
            pl.when(step == which)(act)

        def come(found, act):
            plan.over_blocks(lambda b, rows: act(found(b, rows)))

        def before(b, rows):
            at(1, lambda: waited(fed(b, rows)))

        def after(b, rows):
            at(1, lambda: started(leaving(b, rows)))

        clear_totals(r)
        feed_back(plan, kept, w, r.s_rows, r, before)
        at(0, lambda: come(fed, started))

        @pl.when(step == 1)
        def _():
            plan.over_docs(most, lambda d, n, length: of_doc(d, n).wait())
            come(projected, waited)

        attend_back(plan, most, kept, r)

        @pl.when(step == 0)
        def _():
            plan.over_docs(most, lambda d, n, length: of_doc(d, n).start())
            come(projected, started)

        at(1, lambda: come(given, waited))
        project_back(plan, kept, w, r, r.s_rows, after)
        at(0, lambda: come(given, started))
        r.s_both[pl.ds(pl.multiple_of((1 - step) * V_ALL, V_ALL), V_ALL), :] = r.s_small[...].sum(1)
        at(0, lambda: send_pieces(r, r.o_keep1, r.o_send1, r.table[SELF + 1]))
        at(1, lambda: send_pieces(r, r.o_keep0, r.o_send0, r.table[SELF]))
        return 0

    lax.fori_loop(0, 2, one, 0)
    send_small(r, r.o_keep0, r.o_send0, r.table[SELF])
    plan.over_blocks(lambda b, rows: waited(leaving(b, rows)))


def third_kernel(most, span, r):
    plan = Plan(r)
    coming = [by_block(r.out, r.s_rows, r.in_sems), by_block(r.grad, r.s_sent, r.out_sems)]
    for one in coming:
        plan.over_blocks(lambda b, rows: started(one(b, rows)))
    found = []
    for k, (one, rows) in enumerate(zip(coming, (r.s_rows, r.s_sent))):
        plan.over_blocks(lambda b, at: waited(one(b, at)))
        found += unpack(plan, most, rows, r.s_window.at[k], r, span, k)
    waited(found)


VECTORS = dict(bin=512, bout=256, g1=256, s1=256, bup=512, bdown=256, g2=256, s2=256)


def weights_of(r, layer):
    near = dict(win=r.s_win, wout=r.s_wout, wup=r.s_wup, wdown=r.s_wdown)
    near = {k: v.at[layer] for k, v in near.items()}
    vectors = {k: r.s_vectors[layer, i : i + 1, 0:n] for i, (k, n) in enumerate(VECTORS.items())}
    return SimpleNamespace(**near, **vectors)


def layer_of(r, layer):
    pairs = ((r.win, r.s_win), (r.wout, r.s_wout), (r.wup, r.s_wup), (r.wdown, r.s_wdown))
    coming = []
    for k, (far, near) in enumerate(pairs):
        sem = r.weight_sems.at[4 * layer + k]
        coming.append(pltpu.make_async_copy(far.at[layer], near.at[layer], sem))
    started(coming)
    for i, (k, n) in enumerate(VECTORS.items()):
        r.s_vectors[layer, i : i + 1, 0:n] = getattr(r, k)[layer : layer + 1, :]
    w = weights_of(r, layer)
    w.coming = coming
    return w


def clear_totals(r):
    r.s_total[...] = jnp.zeros(r.s_total.shape, F32)
    r.s_small[...] = jnp.zeros(r.s_small.shape, F32)


def send_pieces(r, keep, send, own):
    half = keep.shape[0]
    rows = AT_ALL // (2 * half)
    for p in range(2 * half):
        out = keep if p < half else send
        at = pl.ds(pl.multiple_of(lax.bitwise_xor(jnp.int32(p), own) * rows, rows), rows)
        out[p % half, 0:rows, :] = r.s_total[at, :].astype(BF)


def send_small(r, keep, send, own):
    half = keep.shape[0]
    rows = AT_ALL // (2 * half)
    extra = keep.shape[1] - rows
    share = V_ALL // half
    for j in range(2 * half):
        line = r.s_both[j * share : (j + 1) * share, :]
        r.s_spread[j] = jnp.concatenate([line, jnp.zeros((extra - share, line.shape[1]), F32)], axis=0)
    for p in range(2 * half):
        out = keep if p < half else send
        out[p % half, rows : rows + extra, :] = r.s_spread[lax.bitwise_xor(jnp.int32(p), own)].astype(BF)


def last_kernel(r):
    half = r.keep0.shape[0]
    count = 2 * half
    rows = AT_ALL // count
    share = 2 * V_ALL // count
    big = (
        (0, AT_OUT, r.s_in, r.o_in),
        (AT_OUT, AT_UP, r.s_out, r.o_out),
        (AT_UP, AT_DOWN, r.s_up, r.o_up),
        (AT_DOWN, AT_ALL, r.s_down, r.o_down),
    )
    sent = []
    for layer, (keep, got) in enumerate(((r.keep0, r.got0), (r.keep1, r.got1))):
        for p in range(count):
            piece = lax.bitwise_xor(jnp.int32(p), r.table[SELF + layer])
            source = keep if p < half else got
            r.s_pieces[layer, piece, 0 : keep.shape[1], :] = source[p % half]
        for low, high, near, far in big:
            tall = near.shape[1]
            for at in range(low, high, rows):
                line, col = (at - low) % tall, (at - low) // tall * 256
                value = r.s_pieces[layer, at // rows, 0:rows, :].astype(F32)
                near[layer, line : line + rows, col : col + 256] = value
            copy = pltpu.make_async_copy(near.at[layer], far.at[layer], r.sems.at[len(sent)])
            copy.start()
            sent.append(copy)
    for j in range(count):
        tail = r.s_pieces[0, j, rows : rows + 16, :].astype(F32)
        r.s_both[j * share : (j + 1) * share, :] = tail[0:share]
    for layer in range(2):
        at = layer * V_ALL
        here = pl.ds(layer, 1)

        def line(k):
            return r.s_both[at + k : at + k + 1, :]

        r.o_bin[here, :] = jnp.concatenate([line(V_IN), line(V_IN + 1)], axis=1)
        r.o_bout[here, :] = line(V_OUT)
        r.o_g1[here, :] = line(V_G1)
        r.o_s1[here, :] = line(V_S1)
        r.o_bup[here, :] = jnp.concatenate([line(V_UP), line(V_UP + 1)], axis=1)
        r.o_bdown[here, :] = line(V_DOWN)
        r.o_g2[here, :] = line(V_G2)
        r.o_s2[here, :] = line(V_S2)
    waited(sent)


def call(kernel, consts, inputs, outputs, scratch, flops, megabytes):
    names = tuple(inputs) + tuple(outputs) + tuple(scratch)

    def run(*refs):
        kernel(*consts, SimpleNamespace(**dict(zip(names, refs))))

    got = pl.pallas_call(
        run,
        out_shape=[jax.ShapeDtypeStruct(s, d) for s, d, _ in outputs.values()],
        in_specs=[spec for _, spec in inputs.values()],
        out_specs=[spec for _, _, spec in outputs.values()],
        scratch_shapes=list(scratch.values()),
        compiler_params=pltpu.CompilerParams(vmem_limit_bytes=megabytes << 20),
        cost_estimate=pl.CostEstimate(flops=flops, bytes_accessed=8 << 20, transcendentals=0),
    )(*[a for a, _ in inputs.values()])
    return SimpleNamespace(**dict(zip(outputs, got)))


def plan_kernel(sections, whole, span, ways, r):
    base = DOCS + 1
    huge = jnp.int32(1 << 20)
    for row in range(2):
        line = r.segments[row : row + 1, :]
        starts = [jnp.int32(0)]
        for doc in range(1, DOCS):
            below = jnp.where(line < doc, 1.0, 0.0)
            starts.append(jnp.sum(below).astype(jnp.int32))
        starts.append(jnp.int32(sections * whole))
        spent = jnp.int32(0)
        for doc in range(base):
            r.start[row * base + doc] = starts[doc]
            r.spent[row * base + doc] = spent
            if doc < DOCS:
                size = starts[doc + 1] - starts[doc]
                spent = spent + size + jnp.where(size > QB, 180, 130)
                spent = spent + jnp.where(size > 2 * QB, 160, 0) + jnp.where(size > 3 * QB, 190, 0)
        for section in range(1, sections):
            low, high = jnp.int32(0), jnp.int32(0)
            for doc in range(base):
                away = starts[doc] - section * whole
                low = low + (away < -REACH).astype(jnp.int32)
                high = high + (away <= REACH).astype(jnp.int32)
            r.low[2 * section + row] = low
            r.high[2 * section + row] = high

    def over(section, visit, first):
        def outer(i, carry):
            inner = lambda j, c: visit(i, j, c)
            return lax.fori_loop(r.low[2 * section + 1], r.high[2 * section + 1], inner, carry)

        return lax.fori_loop(r.low[2 * section], r.high[2 * section], outer, first)

    def least(section, end, top, right):
        def visit(i, j, carry):
            cost, code = carry
            at = i * base + j
            step = end - r.spent[i] - r.spent[base + j]
            new = jnp.maximum(r.best[section * base * base + at], step)
            new = jnp.where((i <= top) & (j <= right), new, huge)
            better = new < cost
            return jnp.where(better, new, cost), jnp.where(better, at, code)

        return over(section, visit, (huge, jnp.int32(0)))

    for section in range(1, sections):

        def visit(i, j, carry):
            at = section * base * base + i * base + j
            end = r.spent[i] + r.spent[base + j]
            if section == 1:
                r.best[at] = end
            else:
                r.best[at], r.way[at] = least(section - 1, end, i, j)
            return carry

        over(section, visit, jnp.int32(0))
    _, code = least(sections - 1, r.spent[DOCS] + r.spent[base + DOCS], jnp.int32(DOCS), jnp.int32(DOCS))
    cuts = [jnp.int32(base * base - 1), code]
    for section in range(sections - 1, 1, -1):
        code = r.way[section * base * base + code]
        cuts.append(code)
    cuts = (cuts + [jnp.int32(0)])[::-1]
    place = r.place[0]
    low, high = jnp.int32(0), jnp.int32(0)
    for section in range(sections):
        low = jnp.where(place == section, cuts[section], low)
        high = jnp.where(place == section, cuts[section + 1], high)
    low, high = (low // base, low % base), (high // base, high % base)
    table = r.table
    carry = (jnp.int32(0), jnp.int32(0), jnp.int32(0))
    for kind in range(1, whole // QB + 1):
        for row in range(2):

            def one(doc, carry):
                k, offset, tile = carry
                begin = r.start[row * base + doc]
                length = r.start[row * base + doc + 1] - begin
                blocks = lax.shift_right_logical(length + (QB - 1), 7)
                table[k] = begin - place * whole + REACH + row * span
                table[ROOM + k] = length
                table[2 * ROOM + k] = offset
                table[3 * ROOM + k] = tile
                taken = (blocks == kind).astype(jnp.int32)
                offset = offset + taken * lax.bitwise_and(length + 15, -16)
                blocks = jnp.maximum(blocks, 2)
                return k + taken, offset, tile + taken * blocks * blocks

            carry = lax.fori_loop(low[row], high[row], one, carry)
    k, offset, _ = carry
    table[ROOM + k] = 0
    blocks = offset // TB
    rest = offset - blocks * TB
    blocks = blocks + (rest > TAIL).astype(jnp.int32)
    odd = ((rest > 0) & (rest <= TAIL)).astype(jnp.int32)
    table[4 * ROOM] = k
    table[4 * ROOM + 1] = blocks
    table[4 * ROOM + 2] = odd
    table[4 * ROOM + 3] = blocks * TB + odd * TAIL
    for i, order in enumerate(ways):
        own = jnp.int32(0)
        for axis, stride in order[:SPLIT]:
            index = r.place[0] if axis == "pipe" else r.group[0]
            own = 2 * own + lax.bitwise_and(index // stride, 1)
        table[4 * ROOM + 4 + i] = own


def halo_sent(low_part, high_part, place):
    upper = lax.rem(place, 2) == 1
    return jnp.where(upper, low_part, high_part), jnp.where(upper, high_part, low_part)


def halo(sent):
    count = lax.axis_size("pipe")
    got = []
    for odd, value in enumerate(sent):
        pairs = [(i, i + 1) for i in range(odd, count - 1, 2)]
        got.append(lax.ppermute(value, "pipe", [p for i, j in pairs for p in ((i, j), (j, i))]))
    return got


def orders():
    found = []
    for axis in ("dp", "pipe"):
        stride = 1
        while stride < lax.axis_size(axis):
            found.append((axis, stride))
            stride *= 2
    other = list(found)
    if len(found) > 2:
        other[1], other[2] = found[2], found[1]
    return found, other


SPLIT = 4


def exchange(value, axis, stride):
    count = lax.axis_size(axis)
    return lax.ppermute(value, axis, [(i, i ^ stride) for i in range(count)])


def added(a, b):
    return (a.astype(F32) + b.astype(F32)).astype(BF)


def sum_steps(keep, send, order):
    total = None
    for k, (axis, stride) in enumerate(order[:SPLIT]):
        got = exchange(send, axis, stride)
        yield None
        half = keep.shape[0] // 2
        if half:
            send, keep = added(keep[half:], got[half:]), added(keep[:half], got[:half])
        else:
            total = added(keep, got)
    for axis, stride in order[SPLIT:]:
        got = exchange(total, axis, stride)
        yield None
        total = added(total, got)
    for k, (axis, stride) in enumerate(reversed(order[:SPLIT])):
        got = exchange(total, axis, stride)
        yield (total, got)
        total = jnp.concatenate([total, got], axis=0)


def body(
    tokens,
    segments,
    cotangent,
    attention_in,
    attention_in_bias,
    attention_out,
    attention_out_bias,
    attention_gain,
    attention_shift,
    expand_weight,
    expand_bias,
    contract_weight,
    contract_bias,
    feed_gain,
    feed_shift,
):
    section_count = lax.axis_size("pipe")
    place = lax.axis_index("pipe").astype(jnp.int32)
    row_count, whole, features = tokens.shape
    span = whole + 2 * REACH + 2 * QB
    most = whole // QB
    cap = row_count * (whole + 2 * REACH) + ITEMS * 15
    cap = (cap + TB - 1) // TB * TB + 2 * QB
    tiles = row_count * 53
    vmem = pl.BlockSpec(memory_space=pltpu.VMEM)
    smem = pl.BlockSpec(memory_space=pltpu.SMEM)
    hbm = pl.BlockSpec(memory_space=pltpu.HBM)
    anywhere = pl.BlockSpec(memory_space=pl.ANY)
    weights = dict(
        win=attention_in,
        bin=attention_in_bias,
        wout=attention_out,
        bout=attention_out_bias,
        g1=attention_gain,
        s1=attention_shift,
        wup=expand_weight,
        bup=expand_bias,
        wdown=contract_weight,
        bdown=contract_bias,
        g2=feed_gain,
        s2=feed_shift,
    )
    weights = {k: (v, vmem if v.ndim == 2 else hbm) for k, v in weights.items()}
    weight_scratch = dict(
        s_win=pltpu.VMEM(attention_in.shape, BF),
        s_wout=pltpu.VMEM(attention_out.shape, BF),
        s_wup=pltpu.VMEM(expand_weight.shape, BF),
        s_wdown=pltpu.VMEM(contract_weight.shape, BF),
        s_vectors=pltpu.VMEM((attention_in.shape[0], len(VECTORS), 2 * features), F32),
        weight_sems=pltpu.SemaphoreType.DMA((4 * attention_in.shape[0],)),
    )

    ways = orders()
    pieces = 1 << SPLIT
    even, odd = halo(halo_sent(tokens[:, :REACH], tokens[:, whole - REACH :], place))
    token_rows = dict(own=(tokens, anywhere), even=(even, anywhere), odd=(odd, anywhere))
    choices = section_count * (DOCS + 1) ** 2
    planned = call(
        plan_kernel,
        (section_count, whole, span, ways),
        dict(
            segments=(segments, vmem),
            place=(place.reshape(1), smem),
            group=(lax.axis_index("dp").astype(jnp.int32).reshape(1), smem),
        ),
        dict(table=((4 * ROOM + 6,), jnp.int32, smem)),
        dict(
            start=pltpu.SMEM((2 * (DOCS + 1),), jnp.int32),
            spent=pltpu.SMEM((2 * (DOCS + 1),), jnp.int32),
            low=pltpu.SMEM((2 * section_count,), jnp.int32),
            high=pltpu.SMEM((2 * section_count,), jnp.int32),
            best=pltpu.SMEM((choices,), jnp.int32),
            way=pltpu.SMEM((choices,), jnp.int32),
        ),
        1 << 20,
        4,
    )
    plan = dict(table=(planned.table, smem), place=(place.reshape(1), smem))
    sent = halo_sent(cotangent[:, :REACH], cotangent[:, whole - REACH :], place)
    even, odd = halo(lax.optimization_barrier((*sent, planned.table))[:2])
    cotangent_rows = dict(own=(cotangent, anywhere), even=(even, anywhere), odd=(odd, anywhere))
    kept_scratch = {"s_" + k: pltpu.VMEM((cap, sum(c.values())), t) for k, (t, c) in KEPT.items()}
    kept_scratch.update(weight_scratch)
    probs_shape = (tiles, 2, QB, 2 * QB)
    kept_scratch.update(
        s_probs=pltpu.VMEM(probs_shape, BF),
        s_window=pltpu.VMEM((row_count * span, features), BF),
        s_turned=pltpu.VMEM((features, whole), BF),
    )
    sems = dict(sems=pltpu.SemaphoreType.DMA((5, MOST_BLOCKS)))
    moved = dict(
        s_rows=pltpu.VMEM((cap, features), BF),
        window_sems=pltpu.SemaphoreType.DMA((3 * row_count,)),
        in_sems=pltpu.SemaphoreType.DMA((MOST_BLOCKS,)),
        out_sems=pltpu.SemaphoreType.DMA((MOST_BLOCKS,)),
    )
    back_scratch = dict(
        s_total=pltpu.VMEM((AT_ALL, features), F32),
        s_small=pltpu.VMEM((V_ALL, 8, features), F32),
        s_ctx_grad=pltpu.VMEM((cap, features), BF),
        s_sum_grad=pltpu.VMEM((cap, features), F32),
        s_qkv_grad=pltpu.VMEM((cap, 3 * features), BF),
    )
    def pieces_out(extra):
        return ((pieces // 2, AT_ALL // pieces + extra, features), BF, vmem)

    rows_out = ((cap, features), BF, hbm)
    kept_out = {"o_" + k: ((cap, sum(c.values())), t, hbm) for k, (t, c) in KEPT.items()}
    kept_out.update(o_probs=(probs_shape, BF, hbm), o_next=rows_out)
    shape = (most, span)

    first = call(
        first_kernel,
        shape,
        plan | token_rows | weights,
        kept_out,
        kept_scratch | sems | moved,
        12 << 30,
        63,
    )
    kept_in = {"i_" + k: (getattr(first, "o_" + k), hbm) for k in NAMES + ("probs",)}
    second = call(
        second_kernel,
        shape,
        plan
        | cotangent_rows
        | kept_in
        | dict(x=(first.o_next, hbm))
        | weights,
        dict(
            o_keep0=pieces_out(16),
            o_send0=pieces_out(16),
            o_keep1=pieces_out(0),
            o_send1=pieces_out(0),
            o_out=rows_out,
            o_grad=rows_out,
        ),
        kept_scratch
        | back_scratch
        | sems
        | moved
        | dict(
            s_both=pltpu.VMEM((2 * V_ALL, features), F32),
            s_spread=pltpu.VMEM((pieces, 16, features), F32),
        ),
        60 << 30,
        63,
    )
    sums = [sum_steps(second.o_keep0, second.o_send0, ways[0])]
    sums.append(sum_steps(second.o_keep1, second.o_send1, ways[1]))
    third = call(
        third_kernel,
        shape,
        plan | dict(out=(second.o_out, hbm), grad=(second.o_grad, hbm)),
        dict(
            o_own=((2, row_count, whole, features), BF, anywhere),
            o_left=((2, row_count, REACH, features), BF, anywhere),
            o_right=((2, row_count, REACH, features), BF, anywhere),
        ),
        moved
        | dict(
            s_sent=pltpu.VMEM((cap, features), BF),
            s_window=pltpu.VMEM((2, row_count * span, features), BF),
                window_sems=pltpu.SemaphoreType.DMA((2, 3 * row_count)),
        ),
        2 << 30,
        20,
    )
    even, odd = halo(halo_sent(third.o_left, third.o_right, place))
    upper = lax.rem(place, 2) == 1
    gap = jnp.zeros((2, row_count, whole - REACH, features), BF)
    low = jnp.concatenate([jnp.where(upper, even, odd), gap], axis=2)
    high = jnp.concatenate([gap, jnp.where(upper, odd, even)], axis=2)
    layer_output, input_grad = [third.o_own[k] + low[k] + high[k] for k in range(2)]
    for ends in zip(*sums):
        pass
    layers = attention_in.shape[0]

    def out(*shape):
        return ((layers,) + shape, F32, hbm)

    def small_out(*shape):
        return ((layers,) + shape, F32, vmem)

    vector = small_out(features)
    result = call(
        last_kernel,
        (),
        dict(
            table=(planned.table, smem),
            keep0=(ends[0][0], vmem),
            got0=(ends[0][1], vmem),
            keep1=(ends[1][0], vmem),
            got1=(ends[1][1], vmem),
        ),
        dict(
            o_in=out(features, 3 * features),
            o_bin=small_out(2 * features),
            o_out=out(features, features),
            o_bout=vector,
            o_g1=vector,
            o_s1=vector,
            o_up=out(features, 2 * features),
            o_bup=small_out(2 * features),
            o_down=out(2 * features, features),
            o_bdown=vector,
            o_g2=vector,
            o_s2=vector,
        ),
        dict(
            s_pieces=pltpu.VMEM((2, pieces, AT_ALL // pieces + 16, features), BF),
            s_both=pltpu.VMEM((2 * V_ALL, features), F32),
            s_in=pltpu.VMEM((layers, features, 3 * features), F32),
            s_out=pltpu.VMEM((layers, features, features), F32),
            s_up=pltpu.VMEM((layers, features, 2 * features), F32),
            s_down=pltpu.VMEM((layers, 2 * features, features), F32),
            sems=pltpu.SemaphoreType.DMA((4 * layers,)),
        ),
        1 << 30,
        20,
    )
    return (layer_output, input_grad) + tuple(vars(result).values())


def solution(mesh):
    rows = P("dp", "pipe", None)
    return jax.shard_map(
        body,
        mesh=mesh,
        in_specs=(rows, P("dp", None), rows) + (P(),) * 12,
        out_specs=(rows, rows) + (P(),) * 12,
        check_vma=False,
    )
```
